32 devices in a mesh: dp: 8 (over z, y), head: 4 (over x, core).
Axes of the slice: x: 2, y: 2, z: 4, core: 2. Of those that a mesh axis runs over, the one named last changes fastest.
Arguments:
- latents: bfloat16 [64, 128, 768], P('dp'), may hold values from -6 to 6
- byte_array: bfloat16 [64, 616, 768], P('dp'), may hold values from -6 to 6
- cotangent: bfloat16 [64, 128, 768], P('dp'), may hold values from -6 to 6
- patch_count: int32 [64], P('dp'), may hold values from 196 to 576, as said below
- text_len: int32 [64], P('dp'), may hold values from 1 to 40, as said below
- inner_weight: float32 [3, 768, 768], P(None, 'dp', 'head'), may hold values from -0.21875 to 0.21875
- inner_moment: float32 [3, 768, 768], P(None, 'dp', 'head'), may hold values from -0.0625 to 0.0625
- inner_square: float32 [3, 768, 768], P(None, 'dp', 'head'), may hold values from 0.0001 to 0.0004
- output_weight: float32 [768, 768], P('head', 'dp')
- output_moment: float32 [768, 768], P('head', 'dp'), may hold values from -0.0625 to 0.0625
- output_square: float32 [768, 768], P('head', 'dp'), may hold values from 0.0001 to 0.0004
- expand_weight: float32 [768, 3072], P('dp', 'head'), may hold values from -0.21875 to 0.21875
- expand_moment: float32 [768, 3072], P('dp', 'head'), may hold values from -0.0625 to 0.0625
- expand_square: float32 [768, 3072], P('dp', 'head'), may hold values from 0.0001 to 0.0004
- reduce_weight: float32 [3072, 768], P('head', 'dp')
- reduce_moment: float32 [3072, 768], P('head', 'dp'), may hold values from -0.0625 to 0.0625
- reduce_square: float32 [3072, 768], P('head', 'dp'), may hold values from 0.0001 to 0.0004
- expand_bias: float32 [3072], P('head'), may hold values from -3 to 3
- bias_moment: float32 [3072], P('head'), may hold values from -0.0625 to 0.0625
- bias_square: float32 [3072], P('head'), may hold values from 0.0001 to 0.0004
- norm_vectors: float32 [7, 768], replicated
- vector_moment: float32 [7, 768], replicated, may hold values from -0.1875 to 0.1875
- vector_square: float32 [7, 768], replicated, may hold values from 0.0009 to 0.0036
Outputs:
- block_output: bfloat16 [64, 128, 768], P('dp')
- latent_gradient: bfloat16 [64, 128, 768], P('dp')
- byte_gradient: bfloat16 [64, 616, 768], P('dp', 'head')
- inner_updated: float32 [3, 768, 768], P(None, 'dp', 'head')
- inner_moment_new: float32 [3, 768, 768], P(None, 'dp', 'head')
- inner_square_new: float32 [3, 768, 768], P(None, 'dp', 'head')
- output_updated: float32 [768, 768], P('head', 'dp')
- output_moment_new: float32 [768, 768], P('head', 'dp')
- output_square_new: float32 [768, 768], P('head', 'dp')
- expand_updated: float32 [768, 3072], P('dp', 'head')
- expand_moment_new: float32 [768, 3072], P('dp', 'head')
- expand_square_new: float32 [768, 3072], P('dp', 'head')
- reduce_updated: float32 [3072, 768], P('head', 'dp')
- reduce_moment_new: float32 [3072, 768], P('head', 'dp')
- reduce_square_new: float32 [3072, 768], P('head', 'dp')
- bias_updated: float32 [3072], P('head')
- bias_moment_new: float32 [3072], P('head')
- bias_square_new: float32 [3072], P('head')
- vector_updated: float32 [7, 768], replicated
- vector_moment_new: float32 [7, 768], replicated
- vector_square_new: float32 [7, 768], replicated
- grad_norm: float32 [], replicated
The draws below stay inside these ranges and needn't reach their ends.
Inputs may be any that keep to these rules, and one draw needn't show every extreme that they name: `patch_count`: each item's count is 196 or 576; both occur in every draw. `text_len`: some item has 40.
All inputs are finite; a program needn't handle non-finite values.
Results may differ from the reference program's by a relative error of at most 0.013.
The reference program's roundings to bfloat16 on the way count: a program that leaves them out, or rounds other values in their place, can miss the bound.
Values may be sent and summed in bfloat16 or wider, within the bound.
No kernel may reach another device: no remote copies, remote signals or barrier semaphores. Data moves between devices by JAX's collectives and lax.ppermute only.
A program may use at most 192 MiB of HBM per device.

```python
import math
import jax
import jax.numpy as jnp
from jax import lax

D = 768
HEADS = 12
HEAD_DIM = 64
FF = 3072
LATENTS = 128
PATCHES = 576
SHORT = 196
TEXT = 40
FRAMES = 1
STEP = 5
KEYS = 616
ITEMS = 64


def rising(count, start_value):
    return start_value + jnp.arange(count, dtype=jnp.float32) / count


def draw_output_weight(key, part):
    key = jax.random.fold_in(key, 11)
    base = 1.0 / math.sqrt(max(D // 128, 1))
    entries = jax.random.normal(key, (D, D), jnp.float32)
    ramp = rising(D, 0.5)
    return entries * ramp[:, None] * base


def draw_reduce_weight(key, part):
    key = jax.random.fold_in(key, 12)
    base = 1.0 / math.sqrt(FF)
    entries = jax.random.normal(key, (FF, D), jnp.float32)
    ramp = rising(FF, 0.5)
    return entries * ramp[:, None] * base


def draw_norm_vectors(key, part):
    key = jax.random.fold_in(key, 13)
    first, second = jax.random.split(key)
    ramp = rising(D, 0.5)
    gains = jax.random.uniform(first, (3, D), jnp.float32, 0.8, 1.2) * ramp[None, :]
    biases = 0.3 * jax.random.normal(second, (4, D), jnp.float32)
    return jnp.stack([gains[0], biases[0], gains[1], biases[1], gains[2], biases[2], biases[3]])


def draw_patch_count(key, part):
    key = jax.random.fold_in(key, 17)
    first, second = jax.random.split(key)
    counts = SHORT + (PATCHES - SHORT) * jax.random.randint(first, (ITEMS,), 0, 2)
    place = jax.random.randint(second, (), 0, ITEMS)
    counts = counts.at[place].set(PATCHES)
    counts = counts.at[(place + 1) % ITEMS].set(SHORT)
    return counts.astype(jnp.int32)


def draw_text_len(key, part):
    key = jax.random.fold_in(key, 19)
    first, second = jax.random.split(key)
    lengths = jax.random.randint(first, (ITEMS,), 1, TEXT + 1)
    place = jax.random.randint(second, (), 0, ITEMS)
    return lengths.at[place].set(TEXT).astype(jnp.int32)


def block_scale(key, extent, cuts, smallest, high):
    def one(dim, parts):
        draws = jax.random.uniform(jax.random.fold_in(jax.random.fold_in(key, 6), dim), (parts,), jnp.float32, smallest / len(cuts), high / len(cuts))
        return jnp.repeat(jnp.exp(draws), extent[dim] // parts).reshape((-1,) + (1,) * (len(extent) - dim - 1))

    factor_of = one(*cuts[0])
    for cut in cuts[1:]:
        factor_of = factor_of * one(*cut)
    return factor_of


def bell_draw(stream_key, dims, spread, most, shards=(), kind=jnp.bfloat16):
    factor_of = block_scale(stream_key, dims, shards, -0.22, 0.18) if shards else 1.0
    drawn = jax.random.normal(stream_key, dims, jnp.float32) * spread * factor_of
    return jnp.minimum(jnp.maximum(drawn, -most), most).astype(kind)


def setup_inputs(seed: int = 0) -> dict:
    key_list = jax.random.split(jax.random.key(seed), 24)
    return {
        "latents": bell_draw(key_list[0], (ITEMS, LATENTS, D), 1.0, 6.0, ((0, 8),)),
        "byte_array": bell_draw(key_list[1], (ITEMS, KEYS, D), 1.0, 6.0, ((0, 8),)),
        "cotangent": bell_draw(key_list[2], (ITEMS, LATENTS, D), 1.0, 6.0, ((0, 8),)),
        "patch_count": draw_patch_count(jax.random.fold_in(key_list[23], 71), 0),
        "text_len": draw_text_len(jax.random.fold_in(key_list[23], 71), 0),
        "inner_weight": bell_draw(key_list[5], (3, D, D), D ** -0.5, 0.21875, ((1, 8), (2, 4)), jnp.float32),
        "inner_moment": bell_draw(key_list[6], (3, D, D), 0.01, 0.0625, ((1, 8), (2, 4)), jnp.float32),
        "inner_square": jnp.clip(jnp.exp(math.log(0.0004) - 1.3862944 * jax.random.uniform(key_list[7], (3, D, D), jnp.float32) ** block_scale(key_list[7], (3, D, D), ((1, 8), (2, 4)), -0.2, 0.2)), 0.0001, 0.0004),
        "output_weight": draw_output_weight(jax.random.fold_in(key_list[23], 71), 0),
        "output_moment": bell_draw(key_list[9], (D, D), 0.01, 0.0625, ((0, 4), (1, 8)), jnp.float32),
        "output_square": jnp.clip(jnp.exp(math.log(0.0004) - 1.3862944 * jax.random.uniform(key_list[10], (D, D), jnp.float32) ** block_scale(key_list[10], (D, D), ((0, 4), (1, 8)), -0.2, 0.2)), 0.0001, 0.0004),
        "expand_weight": bell_draw(key_list[11], (D, FF), D ** -0.5, 0.21875, ((0, 8), (1, 4)), jnp.float32),
        "expand_moment": bell_draw(key_list[12], (D, FF), 0.01, 0.0625, ((0, 8), (1, 4)), jnp.float32),
        "expand_square": jnp.clip(jnp.exp(math.log(0.0004) - 1.3862944 * jax.random.uniform(key_list[13], (D, FF), jnp.float32) ** block_scale(key_list[13], (D, FF), ((0, 8), (1, 4)), -0.2, 0.2)), 0.0001, 0.0004),
        "reduce_weight": draw_reduce_weight(jax.random.fold_in(key_list[23], 71), 0),
        "reduce_moment": bell_draw(key_list[15], (FF, D), 0.01, 0.0625, ((0, 4), (1, 8)), jnp.float32),
        "reduce_square": jnp.clip(jnp.exp(math.log(0.0004) - 1.3862944 * jax.random.uniform(key_list[16], (FF, D), jnp.float32) ** block_scale(key_list[16], (FF, D), ((0, 4), (1, 8)), -0.2, 0.2)), 0.0001, 0.0004),
        "expand_bias": bell_draw(key_list[17], (FF,), 0.5, 3.0, ((0, 4),), jnp.float32),
        "bias_moment": bell_draw(key_list[18], (FF,), 0.01, 0.0625, ((0, 4),), jnp.float32),
        "bias_square": jnp.clip(jnp.exp(math.log(0.0004) - 1.3862944 * jax.random.uniform(key_list[19], (FF,), jnp.float32) ** block_scale(key_list[19], (FF,), ((0, 4),), -0.2, 0.2)), 0.0001, 0.0004),
        "norm_vectors": draw_norm_vectors(jax.random.fold_in(key_list[23], 71), 0),
        "vector_moment": bell_draw(key_list[21], (7, D), 0.03, 0.1875, (), jnp.float32),
        "vector_square": jnp.clip(jnp.exp(jax.random.uniform(key_list[22], (7, D), jnp.float32, math.log(0.0009), math.log(0.0036))), 0.0009, 0.0036),
    }


@jax.custom_vjp
def low(v):
    return lax.optimization_barrier(v.astype(jnp.bfloat16)).astype(jnp.float32)

@jax.custom_vjp
def low_back(v):
    return v

def low_keep(v):
    return (low(v), None)

def low_pass(kept, grad):
    return (grad,)

def back_keep(v):
    return (v, None)

def back_low(kept, grad):
    return (low(grad),)
low.defvjp(low_keep, low_pass)
low_back.defvjp(back_keep, back_low)
NEG_FILL = -1000000000.0
BETA = 0.5
ADAM_EPS = 1e-08
DECAY = 0.01
CLIP_RATE = 0.01

def layer_norm(inputs, gain_row, bias_row):
    centred = inputs - lax.optimization_barrier(jnp.mean(inputs, -1, keepdims=True))
    variance = lax.optimization_barrier(jnp.mean(centred * centred, -1, keepdims=True))
    return centred * lax.rsqrt(variance + 1e-05) * gain_row + bias_row

def mix(form, left, right):
    return jnp.einsum(form, left, right, precision=lax.Precision.HIGHEST)

def key_valid(patch_count, text_len, keys_total):
    slot = jnp.arange(keys_total, dtype=jnp.int32)
    patch_slot = (slot[None, :] < FRAMES * PATCHES) & (slot[None, :] % PATCHES < patch_count[:, None])
    text_slot = (slot[None, :] >= FRAMES * PATCHES) & (slot[None, :] - FRAMES * PATCHES < text_len[:, None])
    return patch_slot | text_slot

def group_forward(weights, lat_block, byte_block, patch_block, text_block):
    query_w, key_w, value_w, outer_w, expand_w, shrink_w, bias_vec, vectors = weights
    group_size = lat_block.shape[0]
    latent_norm = low(layer_norm(lat_block, vectors[0], vectors[1]))
    byte_norm = low(layer_norm(byte_block, vectors[2], vectors[3]))
    queries = low_back(low(mix('gld,de->gle', latent_norm, query_w)))
    keys_proj = low_back(low(mix('gkd,de->gke', byte_norm, key_w)))
    values_proj = low_back(low(mix('gkd,de->gke', byte_norm, value_w)))
    query_heads = queries.reshape(group_size, LATENTS, HEADS, HEAD_DIM)
    key_heads = keys_proj.reshape(group_size, KEYS, HEADS, HEAD_DIM)
    value_heads = values_proj.reshape(group_size, KEYS, HEADS, HEAD_DIM)
    scores = low_back(mix('glhe,gkhe->ghlk', query_heads, key_heads) * (1.0 / math.sqrt(HEAD_DIM)))
    valid = key_valid(patch_block, text_block, KEYS)[:, None, None, :]
    masked = jnp.where(valid, scores, NEG_FILL)
    row_top = lax.optimization_barrier(jnp.max(masked, -1, keepdims=True))
    expo = jnp.exp(masked - row_top)
    attention = low(expo / lax.optimization_barrier(jnp.sum(expo, -1, keepdims=True)))
    mixed = low_back(low(mix('ghlk,gkhe->glhe', attention, value_heads).reshape(group_size, LATENTS, D)))
    attended = low_back(mix('gle,ed->gld', mixed, outer_w))
    residual = lat_block + attended
    mlp_norm = low(layer_norm(residual, vectors[4], vectors[5]))
    pre_act = low_back(mix('gld,df->glf', mlp_norm, expand_w) + bias_vec)
    hidden = low(jax.nn.gelu(pre_act, approximate=False))
    return residual + mix('glf,fd->gld', hidden, shrink_w) + vectors[6]

def adamw(weight, moment, square, gradient, rate, decay_rate):
    moment_new = BETA * moment + (1.0 - BETA) * gradient
    square_new = BETA * square + (1.0 - BETA) * gradient * gradient
    correction = 1.0 - BETA ** STEP
    step_dir = moment_new / correction / (jnp.sqrt(square_new / correction) + ADAM_EPS)
    return (weight - rate * (step_dir + decay_rate * weight), moment_new, square_new)

def reference(latents, byte_array, cotangent, patch_count, text_len, inner_weight, inner_moment, inner_square, output_weight, output_moment, output_square, expand_weight, expand_moment, expand_square, reduce_weight, reduce_moment, reduce_square, expand_bias, bias_moment, bias_square, norm_vectors, vector_moment, vector_square):
    group_span = 4
    groups = ITEMS // group_span

    def forward(params, lat_float, byte_float):
        inner, outer, expand, shrink, bias_vec, vectors = params
        weights = (low(inner[0]), low(inner[1]), low(inner[2]), low(outer), low(expand), low(shrink), bias_vec, vectors)

        def one_group(operands):
            lat_block, byte_block, patch_block, text_block = operands
            return group_forward(weights, lat_block, byte_block, patch_block, text_block)
        outputs = lax.map(jax.checkpoint(one_group), (lat_float.reshape(groups, group_span, LATENTS, D), byte_float.reshape(groups, group_span, KEYS, D), patch_count.reshape(groups, group_span), text_len.reshape(groups, group_span)))
        return outputs.reshape(ITEMS, LATENTS, D)
    params = (inner_weight, output_weight, expand_weight, reduce_weight, expand_bias, norm_vectors)
    block_float, pull = jax.vjp(forward, params, latents.astype(jnp.float32), byte_array.astype(jnp.float32))
    param_grads, latent_grad, byte_grad = pull(cotangent.astype(jnp.float32))
    total_squares = sum((jnp.sum(piece * piece) for piece in param_grads))
    grad_norm = jnp.sqrt(total_squares)
    factor = CLIP_RATE * math.sqrt(4 * D * D + 2 * D * FF + FF + 7 * D) / grad_norm
    inner_grad, outer_grad, expand_grad, shrink_grad, bias_grad, vector_grad = param_grads
    inner_new = adamw(inner_weight, inner_moment, inner_square, factor * inner_grad, 0.03, DECAY)
    outer_new = adamw(output_weight, output_moment, output_square, factor * outer_grad, 0.3, DECAY)
    expand_new = adamw(expand_weight, expand_moment, expand_square, factor * expand_grad, 0.03, DECAY)
    shrink_new = adamw(reduce_weight, reduce_moment, reduce_square, factor * shrink_grad, 0.015, DECAY)
    bias_new = adamw(expand_bias, bias_moment, bias_square, factor * bias_grad, 0.3, 0.0)
    vector_new = adamw(norm_vectors, vector_moment, vector_square, factor * vector_grad, 0.3, 0.0)
    return (block_float.astype(jnp.bfloat16), latent_grad.astype(jnp.bfloat16), byte_grad.astype(jnp.bfloat16), inner_new[0], inner_new[1], inner_new[2], outer_new[0], outer_new[1], outer_new[2], expand_new[0], expand_new[1], expand_new[2], shrink_new[0], shrink_new[1], shrink_new[2], bias_new[0], bias_new[1], bias_new[2], vector_new[0], vector_new[1], vector_new[2], grad_norm)
```

```python
import math

import jax
import jax.numpy as jnp
from jax import lax
from jax.experimental import pallas as pl
from jax.experimental.pallas import tpu as pltpu
from jax.sharding import PartitionSpec as P

D = 768
HEAD_DIM = 64
FF = 3072
PATCHES = 576
STEP = 5

NEG_FILL = -1000000000.0
BETA = 0.5
ADAM_EPS = 1e-08
DECAY = 0.01
CLIP_RATE = 0.01
LN_EPS = 1e-05
SCALE = 1.0 / math.sqrt(HEAD_DIM)
BF = jnp.bfloat16
F32 = jnp.float32
VMEM_LIMIT = 56 * 1024 * 1024


def dot(a, b):
    return lax.dot_general(a, b, (((1,), (0,)), ((), ())), preferred_element_type=F32)


def dot_t(a, b):
    return lax.dot_general(a, b, (((1,), (1,)), ((), ())), preferred_element_type=F32)


def norm_parts(rows):
    centred = rows - jnp.mean(rows, -1, keepdims=True)
    rstd = lax.rsqrt(jnp.mean(centred * centred, -1, keepdims=True) + LN_EPS)
    return centred * rstd, rstd


def norm_back(dy, xhat, rstd, gain):
    scaled = dy * gain
    first = jnp.mean(scaled, -1, keepdims=True)
    second = jnp.mean(scaled * xhat, -1, keepdims=True)
    dx = rstd * (scaled - first - xhat * second)
    return dx, jnp.sum(dy * xhat, 0, keepdims=True), jnp.sum(dy, 0, keepdims=True)


def swap(value, axis, mask):
    size = lax.axis_size(axis)
    return lax.ppermute(value, axis, [(i, i ^ mask) for i in range(size)])


def gather_dp(block):
    size = lax.axis_size("dp")
    index = lax.axis_index("dp")
    held = block[None]
    mask = size // 2
    while mask:
        other = swap(held, "dp", mask)
        bit = (index & mask) != 0
        held = jnp.stack([jnp.where(bit, other, held), jnp.where(bit, held, other)], 1)
        held = held.reshape((-1,) + block.shape)
        mask //= 2
    return held.reshape(-1, block.shape[1])


def scatter_dp(total):
    size = lax.axis_size("dp")
    index = lax.axis_index("dp")
    mask = 1
    while mask < size:
        k, left, rows, cols = total.shape
        pairs = total.reshape(k, left // 2, 2, rows, cols)
        bit = (index & mask) != 0
        away = jnp.where(bit, pairs[:, :, 0], pairs[:, :, 1]).astype(BF)
        kept = jnp.where(bit, pairs[:, :, 1], pairs[:, :, 0])
        total = kept + swap(away, "dp", mask).astype(F32)
        mask *= 2
    return total[:, 0]


def pair_items(mine, core, axis=0):
    other = swap(mine, "head", 1)
    low = core == 0
    return jnp.concatenate([jnp.where(low, mine, other), jnp.where(low, other, mine)], axis)


def adamw(weight, moment, square, gradient, rate, decay_rate):
    moment_new = BETA * moment + (1.0 - BETA) * gradient
    square_new = BETA * square + (1.0 - BETA) * gradient * gradient
    correction = 1.0 - BETA**STEP
    step_dir = moment_new / correction / (jnp.sqrt(square_new / correction) + ADAM_EPS)
    return (weight - rate * (step_dir + decay_rate * weight), moment_new, square_new)


def params(**kw):
    return pltpu.CompilerParams(vmem_limit_bytes=VMEM_LIMIT, **kw)


def cost(flops, nbytes, trans=0):
    return pl.CostEstimate(flops=flops, bytes_accessed=nbytes, transcendentals=trans)


def norm_kernel(info, byte_ref, lat_ref, vec_ref, norm_ref, normt_ref, raw_ref, lat_norm_ref, lat_normt_ref, scr):
    groups, true_rows, pad_rows = 4, byte_ref.shape[1] // 4, norm_ref.shape[1] // 4
    keys = byte_ref.shape[1]
    scr[pl.ds(0, keys), :] = byte_ref[0].astype(F32)
    gain, bias = vec_ref[2:3, :], vec_ref[3:4, :]
    keep = lax.broadcasted_iota(jnp.int32, (pad_rows, 1), 0) < true_rows
    for g in range(groups):
        rows = jnp.where(keep, scr[pl.ds(g * true_rows, pad_rows), :], 0.0)
        xhat, _ = norm_parts(rows)
        normed = jnp.where(keep, xhat * gain + bias, 0.0)
        here = pl.ds(g * pad_rows, pad_rows)
        raw_ref[0, here, :] = rows.astype(BF)
        norm_ref[0, here, :] = normed.astype(BF)
    normt_ref[0] = norm_ref[0].T
    xhat, _ = norm_parts(lat_ref[0].astype(F32))
    lat_norm = (xhat * vec_ref[0:1, :] + vec_ref[1:2, :]).astype(BF)
    lat_norm_ref[0] = lat_norm
    lat_normt_ref[0] = lat_norm.T


def norm_call(info, byte_array, latents, vectors, items, pad_keys):
    _, keys, width = byte_array.shape
    lat_len = latents.shape[1]
    here = lambda i, info: (info[0] * items + i, 0, 0)
    out = lambda i, info: (i, 0, 0)
    return pl.pallas_call(
        norm_kernel,
        grid_spec=pltpu.PrefetchScalarGridSpec(
            num_scalar_prefetch=1,
            grid=(items,),
            in_specs=[
                pl.BlockSpec((1, keys, width), here),
                pl.BlockSpec((1, lat_len, width), here),
                pl.BlockSpec(vectors.shape, lambda i, info: (0, 0)),
            ],
            out_specs=[
                pl.BlockSpec((1, pad_keys, width), out),
                pl.BlockSpec((1, width, pad_keys), out),
                pl.BlockSpec((1, pad_keys, width), out),
                pl.BlockSpec((1, lat_len, width), out),
                pl.BlockSpec((1, width, lat_len), out),
            ],
            scratch_shapes=[pltpu.VMEM((keys + 40, width), F32)],
        ),
        out_shape=[
            jax.ShapeDtypeStruct((items, pad_keys, width), BF),
            jax.ShapeDtypeStruct((items, width, pad_keys), BF),
            jax.ShapeDtypeStruct((items, pad_keys, width), BF),
            jax.ShapeDtypeStruct((items, lat_len, width), BF),
            jax.ShapeDtypeStruct((items, width, lat_len), BF),
        ],
        compiler_params=params(),
        cost_estimate=cost(items * keys * width * 20, items * keys * width * 8),
        name="norms",
    )(info, byte_array, latents, vectors)


def attn_fwd_kernel(info, count_ref, text_ref, norm_ref, lat_ref, wkv_ref, wqo_ref, part_ref, pt_ref, kv_ref, q_ref, mixed_ref):
    items = pl.num_programs(0)
    item = info[0] * items + pl.program_id(0)
    patches, texts = count_ref[item], text_ref[item]
    keys = norm_ref.shape[1]
    pad_rows = keys // 4
    true_rows = info[2]
    row = lax.broadcasted_iota(jnp.int32, (keys, 128), 0)
    group = sum(((row >= pad_rows * g).astype(jnp.int32) for g in range(1, 4)))
    inner = row - group * pad_rows
    slot = inner + group * true_rows
    valid = ((slot < PATCHES) & (slot < patches)) | ((slot >= PATCHES) & (slot - PATCHES < texts))
    valid = valid & (inner < true_rows)
    lane_lo = lax.broadcasted_iota(jnp.int32, (128, 128), 1) < HEAD_DIM
    row_lo = lax.broadcasted_iota(jnp.int32, (128, 128), 0) < HEAD_DIM
    kv_all = dot(norm_ref[0], wkv_ref[...]).astype(BF)
    kv_ref[0] = kv_all
    lat_norm = lat_ref[0]
    total = None
    for p in range(2):
        kv = kv_all[:, p * 384 : (p + 1) * 384]
        base = p * 384
        q = dot(lat_norm, wqo_ref[:, base : base + 256]) * SCALE
        q01, q2 = q[:, :128], jnp.where(lane_lo, q[:, 128:], 0.0).astype(BF)
        q_ref[0, p, :, 0:128] = q01.astype(BF)
        q_ref[0, p, :, 128:256] = q2
        stacked = jnp.concatenate([jnp.where(lane_lo, q01, 0.0), jnp.where(lane_lo, 0.0, q01)], 0).astype(BF)
        first = dot_t(kv[:, 0:128], stacked)
        second = dot_t(kv[:, 256:384], q2)
        pieces = []
        for piece in (first[:, 0:128], first[:, 128:256], second):
            piece = jnp.where(valid, piece, NEG_FILL)
            top = jnp.max(piece, 0, keepdims=True)
            expo = jnp.exp(piece - top)
            pieces.append(expo * (1.0 / jnp.sum(expo, 0, keepdims=True)))
        for h in range(3):
            pt_ref[0, p, :, h * 128 : (h + 1) * 128] = pieces[h]
        low01 = jnp.concatenate([pieces[0].astype(BF), pieces[1].astype(BF)], 1)
        o01 = dot(kv[:, 128:256].T, low01)
        o2 = dot(kv[:, 256:384].T, pieces[2].astype(BF))
        mixed2 = jnp.where(row_lo, 0.0, o2).astype(BF)
        mixed01 = jnp.where(row_lo, o01[:, 0:128], o01[:, 128:256]).astype(BF)
        mixed_ref[0, p, 0:128, :] = mixed2
        mixed_ref[0, p, 128:256, :] = mixed01
        mixed = jnp.concatenate([mixed2.T, mixed01.T], 1)
        add = dot_t(mixed, wqo_ref[:, base + 128 : base + 384])
        total = add if total is None else total + add
    part_ref[0] = total.astype(BF)


def attn_fwd_call(info, counts, texts, norm, lat_norm, wkv, wqo):
    items, keys, width = norm.shape
    lat_len = lat_norm.shape[1]
    out3 = lambda i, *_: (i, 0, 0)
    out4 = lambda i, *_: (i, 0, 0, 0)
    whole = lambda i, *_: (0, 0)
    flops = items * 2 * (keys * width * 768 + lat_len * width * 768 + 4 * keys * lat_len * 384)
    return pl.pallas_call(
        attn_fwd_kernel,
        grid_spec=pltpu.PrefetchScalarGridSpec(
            num_scalar_prefetch=3,
            grid=(items,),
            in_specs=[
                pl.BlockSpec((1, keys, width), out3),
                pl.BlockSpec((1, lat_len, width), out3),
                pl.BlockSpec(wkv.shape, whole),
                pl.BlockSpec(wqo.shape, whole),
            ],
            out_specs=[
                pl.BlockSpec((1, lat_len, width), out3),
                pl.BlockSpec((1, 2, keys, 384), out4),
                pl.BlockSpec((1, keys, 768), out3),
                pl.BlockSpec((1, 2, lat_len, 256), out4),
                pl.BlockSpec((1, 2, 256, lat_len), out4),
            ],
        ),
        out_shape=[
            jax.ShapeDtypeStruct((items, lat_len, width), BF),
            jax.ShapeDtypeStruct((items, 2, keys, 384), F32),
            jax.ShapeDtypeStruct((items, keys, 768), BF),
            jax.ShapeDtypeStruct((items, 2, lat_len, 256), BF),
            jax.ShapeDtypeStruct((items, 2, 256, lat_len), BF),
        ],
        compiler_params=params(),
        cost_estimate=cost(flops, 16 * 1024 * 1024, items * keys * 768),
        name="attn_fwd",
    )(info, counts, texts, norm, lat_norm, wkv, wqo)


def ff_core_kernel(info, lat_ref, cot_ref, own_ref, got_ref, vec_ref, bias_ref, w_own_ref, w_oth_ref,
                   res_ref, normt_ref, cott_ref, hidden_ref, pre_ref, part_ref):
    width = vec_ref.shape[1]
    flat = lambda ref: ref[...].reshape(-1, width).astype(F32)
    residual = flat(lat_ref) + (flat(own_ref) + flat(got_ref))
    res_ref[...] = residual
    xhat, _ = norm_parts(residual)
    normed = (xhat * vec_ref[4:5, :] + vec_ref[5:6, :]).astype(BF)
    cot = cot_ref[...].reshape(-1, width)
    total = None
    step = 256
    for p, w_ref in enumerate((w_own_ref, w_oth_ref)):
        for j in range(768 // step):
            cols = slice(j * step, (j + 1) * step)
            w1 = w_ref[:, j * step : (j + 1) * step]
            pre = dot(normed, w1) + bias_ref[p : p + 1, cols]
            back = dot(cot, w_ref[:, 768 + j * step : 768 + (j + 1) * step])
            cdf = 0.5 + 0.5 * lax.erf(pre * math.sqrt(0.5))
            pdf = jnp.exp(pre * pre * -0.5) * (1.0 / math.sqrt(2.0 * math.pi))
            hidden_ref[p, :, cols] = (pre * cdf).astype(BF)
            grad = (back * (cdf + pre * pdf)).astype(BF)
            pre_ref[p, :, cols] = grad
            add = dot_t(grad, w1)
            total = add if total is None else total + add
    part_ref[...] = total.astype(BF)
    normt_ref[...] = normed.T
    cott_ref[...] = cot.T


def ff_core_call(info, latents, cotangent, own, got, vectors, bias, w_own, w_oth):
    items, lat_len, width = own.shape
    rows = items * lat_len
    half = lambda i, info: (info[0], 0, 0)
    z3 = lambda i, info: (0, 0, 0)
    z2 = lambda i, info: (0, 0)
    return pl.pallas_call(
        ff_core_kernel,
        grid_spec=pltpu.PrefetchScalarGridSpec(
            num_scalar_prefetch=1,
            grid=(1,),
            in_specs=[
                pl.BlockSpec((items, lat_len, width), half),
                pl.BlockSpec((items, lat_len, width), half),
                pl.BlockSpec(own.shape, z3),
                pl.BlockSpec(got.shape, z3),
                pl.BlockSpec(vectors.shape, z2),
                pl.BlockSpec(bias.shape, z2),
                pl.BlockSpec(w_own.shape, z2),
                pl.BlockSpec(w_oth.shape, z2),
            ],
            out_specs=[
                pl.BlockSpec((rows, width), z2),
                pl.BlockSpec((width, rows), z2),
                pl.BlockSpec((width, rows), z2),
                pl.BlockSpec((2, rows, 768), z3),
                pl.BlockSpec((2, rows, 768), z3),
                pl.BlockSpec((rows, width), z2),
            ],
        ),
        out_shape=[
            jax.ShapeDtypeStruct((rows, width), F32),
            jax.ShapeDtypeStruct((width, rows), BF),
            jax.ShapeDtypeStruct((width, rows), BF),
            jax.ShapeDtypeStruct((2, rows, 768), BF),
            jax.ShapeDtypeStruct((2, rows, 768), BF),
            jax.ShapeDtypeStruct((rows, width), BF),
        ],
        compiler_params=params(),
        cost_estimate=cost(6 * rows * width * 1536, 16 * 1024 * 1024, 2 * rows * 1536),
        name="ff_core",
    )(info, latents, cotangent, own, got, vectors, bias, w_own, w_oth)


def ff_grad_kernel(normt_ref, cott_ref, hidden_ref, pre_ref, w2_own_ref, w2_oth_ref,
                   g_own_ref, g_oth_ref, part_ref, bias_ref, cot_sum_ref, acc):
    j = pl.program_id(0)
    normt, cott = normt_ref[...], cott_ref[...]
    total = None
    for p, w_ref in enumerate((w2_own_ref, w2_oth_ref)):
        hidden, pre = hidden_ref[p], pre_ref[p]
        add = dot_t(hidden, w_ref[...])
        total = add if total is None else total + add
        out = (g_own_ref, g_oth_ref)[p]
        out[0] = dot(normt, pre).astype(out.dtype)
        out[1] = dot(cott, hidden).astype(out.dtype)
        bias_ref[p : p + 1, :] = jnp.sum(pre.astype(F32), 0, keepdims=True)

    @pl.when(j == 0)
    def _():
        acc[...] = total
        cot_sum_ref[...] = jnp.sum(cott.astype(F32), 1, keepdims=True)

    @pl.when(j > 0)
    def _():
        acc[...] += total

    part_ref[...] = acc[...].astype(BF)


def ff_grad_call(normt, cott, hidden, pre, w_own, w_oth):
    width, rows = normt.shape
    step = 256
    n = 768 // step
    z2 = lambda j: (0, 0)
    return pl.pallas_call(
        ff_grad_kernel,
        grid=(n,),
        in_specs=[
            pl.BlockSpec((width, rows), z2),
            pl.BlockSpec((width, rows), z2),
            pl.BlockSpec((2, rows, step), lambda j: (0, 0, j)),
            pl.BlockSpec((2, rows, step), lambda j: (0, 0, j)),
            pl.BlockSpec((width, step), lambda j: (0, n + j)),
            pl.BlockSpec((width, step), lambda j: (0, n + j)),
        ],
        out_specs=[
            pl.BlockSpec((2, width, step), lambda j: (0, 0, j)),
            pl.BlockSpec((2, width, step), lambda j: (0, 0, j)),
            pl.BlockSpec((rows, width), z2),
            pl.BlockSpec((2, step), lambda j: (0, j)),
            pl.BlockSpec((width, 1), z2),
        ],
        out_shape=[
            jax.ShapeDtypeStruct((2, width, 768), F32),
            jax.ShapeDtypeStruct((2, width, 768), BF),
            jax.ShapeDtypeStruct((rows, width), BF),
            jax.ShapeDtypeStruct((2, 768), F32),
            jax.ShapeDtypeStruct((width, 1), F32),
        ],
        scratch_shapes=[pltpu.VMEM((rows, width), F32)],
        compiler_params=params(),
        cost_estimate=cost(6 * rows * width * 1536, 16 * 1024 * 1024),
        name="ff_grad",
    )(normt, cott, hidden, pre, w_own, w_oth)


def residual_kernel(info, cot_ref, res_ref, own_ref, got_ref, vec_ref, grad_ref, low_ref, lowt_ref, sums_ref):
    width = vec_ref.shape[1]
    xhat, rstd = norm_parts(res_ref[...])
    dy = own_ref[...].astype(F32) + got_ref[...].astype(F32)
    dx, dgain, dbias = norm_back(dy, xhat, rstd, vec_ref[4:5, :])
    grad = cot_ref[...].reshape(-1, width).astype(F32) + dx
    grad_ref[...] = grad
    low = grad.astype(BF)
    low_ref[...] = low
    lowt_ref[...] = low.T
    sums_ref[0:1, :] = dgain
    sums_ref[1:2, :] = dbias


def residual_call(info, cotangent, residual, own, got, vectors):
    rows, width = residual.shape
    lat_len = cotangent.shape[1]
    items = rows // lat_len
    z2 = lambda i, info: (0, 0)
    return pl.pallas_call(
        residual_kernel,
        grid_spec=pltpu.PrefetchScalarGridSpec(
            num_scalar_prefetch=1,
            grid=(1,),
            in_specs=[
                pl.BlockSpec((items, lat_len, width), lambda i, info: (info[0], 0, 0)),
                pl.BlockSpec((rows, width), z2),
                pl.BlockSpec((rows, width), z2),
                pl.BlockSpec((rows, width), z2),
                pl.BlockSpec(vectors.shape, z2),
            ],
            out_specs=[
                pl.BlockSpec((rows, width), z2),
                pl.BlockSpec((rows, width), z2),
                pl.BlockSpec((width, rows), z2),
                pl.BlockSpec((2, width), z2),
            ],
        ),
        out_shape=[
            jax.ShapeDtypeStruct((rows, width), F32),
            jax.ShapeDtypeStruct((rows, width), BF),
            jax.ShapeDtypeStruct((width, rows), BF),
            jax.ShapeDtypeStruct((2, width), F32),
        ],
        compiler_params=params(),
        cost_estimate=cost(rows * width * 20, 10 * 1024 * 1024),
        name="residual_back",
    )(info, cotangent, residual, own, got, vectors)


def attn_bwd_kernel(low_ref, lowt_ref, pt_ref, kv_ref, q_ref, mixed_ref, normt_ref, lat_normt_ref, wqo_ref,
                    lat_part_ref, dkv_ref, g_own_ref, g_oth_ref, gkv, gqo):
    i = pl.program_id(0)

    @pl.when(i == 0)
    def _():
        gkv[...] = jnp.zeros_like(gkv)
        gqo[...] = jnp.zeros_like(gqo)

    lane_lo = lax.broadcasted_iota(jnp.int32, (128, 128), 1) < HEAD_DIM
    row_lo = lax.broadcasted_iota(jnp.int32, (128, 128), 0) < HEAD_DIM
    low = low_ref[...]
    both = jnp.concatenate([lat_normt_ref[0], lowt_ref[...]], 1)
    none = jnp.zeros((128, 128), BF)
    total = None
    for p in range(2):
        base = p * 384
        kv = kv_ref[0, :, base : base + 384]
        mixed_grad = dot(low, wqo_ref[:, base + 128 : base + 384])
        mg2 = jnp.where(lane_lo, 0.0, mixed_grad[:, 0:128]).astype(BF)
        mg01 = mixed_grad[:, 128:256]
        mg01 = jnp.concatenate([jnp.where(lane_lo, mg01, 0.0), jnp.where(lane_lo, 0.0, mg01)], 0).astype(BF)
        first = dot_t(kv[:, 128:256], mg01)
        second = dot_t(kv[:, 256:384], mg2)
        probs, scores = [], []
        for h, piece in enumerate((first[:, 0:128], first[:, 128:256], second)):
            prob = pt_ref[0, p, :, h * 128 : (h + 1) * 128]
            inner = jnp.sum(piece * prob, 0, keepdims=True)
            scores.append((prob * (piece - inner)).astype(BF))
            probs.append(prob.astype(BF))
        q01 = q_ref[0, p, :, 0:128].astype(F32)
        q01 = jnp.concatenate([jnp.where(lane_lo, q01, 0.0), jnp.where(lane_lo, 0.0, q01)], 0).astype(BF)
        q2 = q_ref[0, p, :, 128:256]
        ds01 = jnp.concatenate(scores[:2], 1)
        dkv_ref[0, :, base : base + 128] = dot(ds01, q01).astype(BF)
        dkv_ref[0, :, base + 128 : base + 256] = dot(jnp.concatenate(probs[:2], 1), mg01).astype(BF)
        dkv_ref[0, :, base + 256 : base + 384] = dot(
            jnp.concatenate([scores[2], probs[2]], 1), jnp.concatenate([q2, mg2], 0)
        ).astype(BF)
        dq01 = dot(kv[:, 0:128].T, ds01)
        dq2 = dot(kv[:, 256:384].T, scores[2])
        dq01 = (jnp.where(row_lo, dq01[:, 0:128], dq01[:, 128:256]) * SCALE).astype(BF)
        dq2 = (jnp.where(row_lo, dq2, 0.0) * SCALE).astype(BF)
        add = dot_t(jnp.concatenate([dq01.T, dq2.T], 1), wqo_ref[:, base : base + 256])
        total = add if total is None else total + add
        right = jnp.concatenate(
            [
                jnp.concatenate([dq01, none], 1),
                jnp.concatenate([dq2, mixed_ref[0, p, 0:128, :]], 1),
                jnp.concatenate([none, mixed_ref[0, p, 128:256, :]], 1),
            ],
            0,
        )
        gqo[:, base : base + 384] += dot_t(both, right)
    lat_part_ref[...] = total.astype(BF)
    gkv[...] += dot(normt_ref[0], dkv_ref[0])

    @pl.when(i == pl.num_programs(0) - 1)
    def _():
        g_own_ref[:, 0:384] = gkv[:, 0:384]
        g_own_ref[:, 384:768] = gqo[:, 0:384]
        g_oth_ref[:, 0:384] = gkv[:, 384:768].astype(BF)
        g_oth_ref[:, 384:768] = gqo[:, 384:768].astype(BF)


def attn_bwd_call(low, lowt, pt, kv, q, mixed, normt, lat_normt, wqo):
    items, keys, _ = kv.shape
    width = lowt.shape[0]
    lat_len = q.shape[2]
    three = lambda i: (i, 0, 0)
    four = lambda i: (i, 0, 0, 0)
    z2 = lambda i: (0, 0)
    flops = items * 2 * (keys * width * 768 + 3 * lat_len * width * 768 + 10 * keys * lat_len * 384)
    return pl.pallas_call(
        attn_bwd_kernel,
        grid=(items,),
        in_specs=[
            pl.BlockSpec((lat_len, width), lambda i: (i, 0)),
            pl.BlockSpec((width, lat_len), lambda i: (0, i)),
            pl.BlockSpec((1, 2, keys, 384), four),
            pl.BlockSpec((1, keys, 768), three),
            pl.BlockSpec((1, 2, lat_len, 256), four),
            pl.BlockSpec((1, 2, 256, lat_len), four),
            pl.BlockSpec((1, width, keys), three),
            pl.BlockSpec((1, width, lat_len), three),
            pl.BlockSpec(wqo.shape, z2),
        ],
        out_specs=[
            pl.BlockSpec((lat_len, width), lambda i: (i, 0)),
            pl.BlockSpec((1, keys, 768), three),
            pl.BlockSpec((width, 768), z2),
            pl.BlockSpec((width, 768), z2),
        ],
        out_shape=[
            jax.ShapeDtypeStruct((items * lat_len, width), BF),
            jax.ShapeDtypeStruct((items, keys, 768), BF),
            jax.ShapeDtypeStruct((width, 768), F32),
            jax.ShapeDtypeStruct((width, 768), BF),
        ],
        scratch_shapes=[pltpu.VMEM((width, 768), F32), pltpu.VMEM((width, 768), F32)],
        compiler_params=params(),
        cost_estimate=cost(flops, 24 * 1024 * 1024),
        name="attn_bwd",
    )(low, lowt, pt, kv, q, mixed, normt, lat_normt, wqo)


def latent_kernel(info, lat_ref, grad_ref, own_ref, got_ref, vec_ref, out_ref, sums_ref):
    width = vec_ref.shape[1]
    xhat, rstd = norm_parts(lat_ref[...].reshape(-1, width).astype(F32))
    dy = own_ref[...].astype(F32) + got_ref[...].astype(F32)
    dx, dgain, dbias = norm_back(dy, xhat, rstd, vec_ref[0:1, :])
    out_ref[...] = (grad_ref[...] + dx).astype(BF).reshape(out_ref.shape)
    sums_ref[0:1, :] = dgain
    sums_ref[1:2, :] = dbias


def latent_call(info, latents, grad, own, got, vectors):
    rows, width = grad.shape
    lat_len = latents.shape[1]
    items = rows // lat_len
    z2 = lambda i, info: (0, 0)
    return pl.pallas_call(
        latent_kernel,
        grid_spec=pltpu.PrefetchScalarGridSpec(
            num_scalar_prefetch=1,
            grid=(1,),
            in_specs=[
                pl.BlockSpec((items, lat_len, width), lambda i, info: (info[0], 0, 0)),
                pl.BlockSpec((rows, width), z2),
                pl.BlockSpec((rows, width), z2),
                pl.BlockSpec((rows, width), z2),
                pl.BlockSpec(vectors.shape, z2),
            ],
            out_specs=[
                pl.BlockSpec((items, lat_len, width), lambda i, info: (0, 0, 0)),
                pl.BlockSpec((2, width), z2),
            ],
        ),
        out_shape=[
            jax.ShapeDtypeStruct((items, lat_len, width), BF),
            jax.ShapeDtypeStruct((2, width), F32),
        ],
        compiler_params=params(),
        cost_estimate=cost(rows * width * 20, 6 * 1024 * 1024),
        name="latent_back",
    )(info, latents, grad, own, got, vectors)


def byte_send_kernel(info, dkv_ref, wkv_ref, out_ref):
    out_ref[0] = dot_t(dkv_ref[0], wkv_ref[...]).astype(BF)


def byte_send_call(info, dkv, wkv):
    items, keys, _ = dkv.shape
    width = wkv.shape[0]
    half = keys // 2
    return pl.pallas_call(
        byte_send_kernel,
        grid_spec=pltpu.PrefetchScalarGridSpec(
            num_scalar_prefetch=1,
            grid=(items,),
            in_specs=[
                pl.BlockSpec((1, half, 768), lambda i, info: (i, 1 - info[1], 0)),
                pl.BlockSpec(wkv.shape, lambda i, info: (0, 0)),
            ],
            out_specs=pl.BlockSpec((1, half, width), lambda i, info: (i, 0, 0)),
        ),
        out_shape=jax.ShapeDtypeStruct((items, half, width), BF),
        compiler_params=params(),
        cost_estimate=cost(items * half * width * 768 * 2, 6 * 1024 * 1024),
        name="byte_send",
    )(info, dkv, wkv)


def byte_back_kernel(info, dkv_ref, got_ref, raw_ref, wkv_ref, vec_ref, own_ref, oth_ref, sums_ref):
    i = pl.program_id(0)
    dy = dot_t(dkv_ref[0], wkv_ref[...]) + got_ref[0].astype(F32)
    xhat, rstd = norm_parts(raw_ref[0].astype(F32))
    dx, dgain, dbias = norm_back(dy, xhat, rstd, vec_ref[2:3, :])
    quarter = dx.shape[0] // 2

    @pl.when(info[0] == 0)
    def _():
        own_ref[0] = dx[:quarter].astype(BF)
        oth_ref[0] = dx[quarter:].astype(BF)

    @pl.when(info[0] != 0)
    def _():
        own_ref[0] = dx[quarter:].astype(BF)
        oth_ref[0] = dx[:quarter].astype(BF)

    @pl.when(i == 0)
    def _():
        sums_ref[...] = jnp.zeros_like(sums_ref)

    sums_ref[0:1, :] += dgain
    sums_ref[1:2, :] += dbias


def byte_back_call(info, dkv, got, raw, wkv, vectors):
    items, keys, _ = dkv.shape
    width = wkv.shape[0]
    half = keys // 2
    mine = lambda i, info: (i, info[1], 0)
    out = lambda i, info: (i, 0, 0)
    z2 = lambda i, info: (0, 0)
    return pl.pallas_call(
        byte_back_kernel,
        grid_spec=pltpu.PrefetchScalarGridSpec(
            num_scalar_prefetch=1,
            grid=(items,),
            in_specs=[
                pl.BlockSpec((1, half, 768), mine),
                pl.BlockSpec((1, half, width), out),
                pl.BlockSpec((1, half, width), mine),
                pl.BlockSpec(wkv.shape, z2),
                pl.BlockSpec(vectors.shape, z2),
            ],
            out_specs=[
                pl.BlockSpec((1, half // 2, width), out),
                pl.BlockSpec((1, half // 2, width), out),
                pl.BlockSpec((2, width), z2),
            ],
        ),
        out_shape=[
            jax.ShapeDtypeStruct((items, half // 2, width), BF),
            jax.ShapeDtypeStruct((items, half // 2, width), BF),
            jax.ShapeDtypeStruct((2, width), F32),
        ],
        compiler_params=params(),
        cost_estimate=cost(items * half * width * 768 * 2, 8 * 1024 * 1024),
        name="byte_back",
    )(info, dkv, got, raw, wkv, vectors)


def body(
    latents, byte_array, cotangent, patch_count, text_len,
    inner_weight, inner_moment, inner_square,
    output_weight, output_moment, output_square,
    expand_weight, expand_moment, expand_square,
    reduce_weight, reduce_moment, reduce_square,
    expand_bias, bias_moment, bias_square,
    norm_vectors, vector_moment, vector_square,
):
    item_count, lat_len, width = latents.shape
    keys = byte_array.shape[1]
    items = item_count // 2
    n = lax.axis_size("dp")
    head = lax.axis_index("head")
    core, xside = head & 1, head >> 1
    true_rows = keys // lax.axis_size("head")
    pad_rows = -(-true_rows // 32) * 32
    pad_keys = 4 * pad_rows
    info = jnp.stack([core, xside, jnp.int32(true_rows)]).astype(jnp.int32)

    low_inner = inner_weight.astype(BF)
    wq, wk, wv = low_inner[0], low_inner[1], low_inner[2]
    wo = output_weight.astype(BF).T
    pack = jnp.concatenate(
        [wk[:, :128], wv[:, :128], wk[:, 128:], wv[:, 128:], wq[:, :128], wq[:, 128:], wo[:, 128:], wo[:, :128]], 1
    )
    own_w = gather_dp(pack)
    oth_w = swap(own_w, "head", 1)
    wkv = jnp.concatenate([own_w[:, :384], oth_w[:, :384]], 1)
    wqo = jnp.concatenate([own_w[:, 384:], oth_w[:, 384:]], 1)
    ff_pack = jnp.concatenate([expand_weight.astype(BF), reduce_weight.astype(BF).T], 1)
    ff_own = lax.all_gather(ff_pack, "dp", axis=0, tiled=True)
    ff_oth = swap(ff_own, "head", 1)
    bias_both = jnp.stack([expand_bias, swap(expand_bias, "head", 1)])

    norm, normt, raw, lat_norm, lat_normt = norm_call(info, byte_array, latents, norm_vectors, items, pad_keys)
    attn_part, pt, kv, q, mixed = attn_fwd_call(info, patch_count, text_len, norm, lat_norm, wkv, wqo)
    attn_got = swap(attn_part, "head", 2)

    residual, mlp_normt, cott, hidden, pre_grad, norm_part = ff_core_call(
        info, latents, cotangent, attn_part, attn_got, norm_vectors, bias_both, ff_own, ff_oth
    )
    norm_got = swap(norm_part, "head", 2)
    g_ff, g_ff_oth, mlp_part, bias_part, cot_sum = ff_grad_call(mlp_normt, cott, hidden, pre_grad, ff_own, ff_oth)
    mlp_got = swap(mlp_part, "head", 2)
    block_mine = residual + (mlp_part.astype(F32) + mlp_got.astype(F32)) + norm_vectors[6]
    block_output = pair_items(block_mine.astype(BF).reshape(items, lat_len, width), core)

    residual_grad, low, lowt, mlp_sums = residual_call(info, cotangent, residual, norm_part, norm_got, norm_vectors)
    lat_part, dkv, g_attn, g_attn_oth = attn_bwd_call(low, lowt, pt, kv, q, mixed, normt, lat_normt, wqo)

    byte_got = swap(byte_send_call(info, dkv, wkv), "head", 2)
    byte_own, byte_oth, byte_sums = byte_back_call(info, dkv, byte_got, raw, wkv, norm_vectors)
    byte_recv = swap(byte_oth, "head", 1)
    is_low = core == 0
    byte_gradient = jnp.concatenate(
        [jnp.where(is_low, byte_own, byte_recv), jnp.where(is_low, byte_recv, byte_own)], 0
    )[:, :true_rows]

    lat_got = swap(lat_part, "head", 2)
    lat_mine, lat_sums = latent_call(info, latents, residual_grad, lat_part, lat_got, norm_vectors)
    latent_gradient = pair_items(lat_mine, core)

    g_ff = scatter_dp((g_ff + swap(g_ff_oth, "head", 1).astype(F32)).reshape(2, n, width // n, 768))
    g_attn = scatter_dp((g_attn + swap(g_attn_oth, "head", 1).astype(F32)).reshape(1, n, width // n, 768))[0]
    bias_own = bias_part[0] + swap(bias_part[1], "head", 1)
    expand_g, reduce_gt = g_ff[0], g_ff[1]
    once = (xside == 0).astype(F32)
    squares = jnp.sum(g_ff * g_ff) + jnp.sum(g_attn * g_attn)
    vec = jnp.concatenate(
        [lat_sums * once, byte_sums, mlp_sums * once, (cot_sum * once).reshape(1, width)], 0
    )
    load = jnp.concatenate([vec, bias_own[None], jnp.full((1, width), squares, F32)], 0)
    mask = n // 2
    while mask:
        load = load + swap(load, "dp", mask)
        mask //= 2
    bias_sum = load[7]
    squares = load[8:9] + jnp.sum(bias_sum * bias_sum)
    load = jnp.concatenate([load[:7], squares], 0)
    load = load + swap(load, "head", 1)
    load = load + swap(load, "head", 2)
    vector_sum = load[:7]
    grad_norm = jnp.sqrt(load[7, 0] + jnp.sum(vector_sum * vector_sum))
    factor = CLIP_RATE * math.sqrt(4 * D * D + 2 * D * FF + FF + 7 * D) / grad_norm

    g_k = jnp.concatenate([g_attn[:, 0:128], g_attn[:, 256:320]], 1)
    g_v = jnp.concatenate([g_attn[:, 128:256], g_attn[:, 320:384]], 1)
    g_q = jnp.concatenate([g_attn[:, 384:512], g_attn[:, 512:576]], 1)
    g_o = jnp.concatenate([g_attn[:, 640:768], g_attn[:, 576:640]], 1).T
    inner_new = adamw(inner_weight, inner_moment, inner_square, factor * jnp.stack([g_q, g_k, g_v]), 0.03, DECAY)
    outer_new = adamw(output_weight, output_moment, output_square, factor * g_o, 0.3, DECAY)
    expand_new = adamw(expand_weight, expand_moment, expand_square, factor * expand_g, 0.03, DECAY)
    shrink_new = adamw(reduce_weight, reduce_moment, reduce_square, factor * reduce_gt.T, 0.015, DECAY)
    bias_new = adamw(expand_bias, bias_moment, bias_square, factor * bias_sum, 0.3, 0.0)
    vector_new = adamw(norm_vectors, vector_moment, vector_square, factor * vector_sum, 0.3, 0.0)
    return (
        block_output, latent_gradient, byte_gradient,
        *inner_new, *outer_new, *expand_new, *shrink_new, *bias_new, *vector_new, grad_norm,
    )


def solution(mesh):
    rows, cols = P("dp", "head"), P("head", "dp")
    inner, items = P(None, "dp", "head"), P("dp", None, None)
    weights = (inner,) * 3 + (cols,) * 3 + (rows,) * 3 + (cols,) * 3 + (P("head"),) * 3 + (P(),) * 3
    return jax.shard_map(
        body,
        mesh=mesh,
        in_specs=(items, items, items, P("dp"), P("dp")) + weights,
        out_specs=(items, items, P("dp", "head", None)) + weights + (P(),),
        check_vma=False,
    )
```

```python
import functools
import math

import jax
import jax.numpy as jnp
from jax import lax
from jax.experimental import pallas as pl
from jax.experimental.pallas import tpu as pltpu
from jax.sharding import PartitionSpec as P

D = 768
HEAD_DIM = 64
FF = 3072
PATCHES = 576
STEP = 5

NEG_FILL = -1000000000.0
BETA = 0.5
ADAM_EPS = 1e-08
DECAY = 0.01
CLIP_RATE = 0.01
LN_EPS = 1e-05
SCALE = 1.0 / math.sqrt(HEAD_DIM)
BF = jnp.bfloat16
F32 = jnp.float32
VMEM_LIMIT = 56 * 1024 * 1024


def dot(a, b):
    return lax.dot_general(a, b, (((1,), (0,)), ((), ())), preferred_element_type=F32)


def dot_t(a, b):
    return lax.dot_general(a, b, (((1,), (1,)), ((), ())), preferred_element_type=F32)


def norm_parts(rows):
    centred = rows - jnp.mean(rows, -1, keepdims=True)
    rstd = lax.rsqrt(jnp.mean(centred * centred, -1, keepdims=True) + LN_EPS)
    return centred * rstd, rstd


def norm_back(dy, xhat, rstd, gain):
    scaled = dy * gain
    first = jnp.mean(scaled, -1, keepdims=True)
    second = jnp.mean(scaled * xhat, -1, keepdims=True)
    dx = rstd * (scaled - first - xhat * second)
    return dx, jnp.sum(dy * xhat, 0, keepdims=True), jnp.sum(dy, 0, keepdims=True)


def swap(value, axis, mask):
    size = lax.axis_size(axis)
    return lax.ppermute(value, axis, [(i, i ^ mask) for i in range(size)])


def tie(*values):
    return lax.optimization_barrier(tuple(values))


def plus(a, b):
    return (a.astype(F32) + b.astype(F32)).astype(BF)


def plus3(a, b, c):
    return (a.astype(F32) + b.astype(F32) + c.astype(F32)).astype(BF)


def adamw(weight, moment, square, gradient, rate, decay_rate):
    moment_new = BETA * moment + (1.0 - BETA) * gradient
    square_new = BETA * square + (1.0 - BETA) * gradient * gradient
    correction = 1.0 - BETA**STEP
    step_dir = moment_new * (1.0 / correction) / (jnp.sqrt(square_new * (1.0 / correction)) + ADAM_EPS)
    return (weight - rate * (step_dir + decay_rate * weight), moment_new, square_new)


def params(**kw):
    return pltpu.CompilerParams(vmem_limit_bytes=VMEM_LIMIT, **kw)


def cost(flops, nbytes, trans=0):
    return pl.CostEstimate(flops=flops, bytes_accessed=nbytes, transcendentals=trans)


GROUPS = ((0, 4, 2, 1), (6, 5, 3), (7,))


def assemble(info, parts, outs, splits):
    rows = parts[0].shape[0]
    blocks = [(k, 0, parts[k], 0) for k in range(8)]
    for part, group in zip(parts[8:], GROUPS):
        blocks += [(k, 1, part, i * rows) for i, k in enumerate(group)]
    for k, c, part, first in blocks:
        for out, start, stop, offset in splits[c]:
            outs[out][info[4] ^ k, :, offset : offset + stop - start] = part[first : first + rows, start:stop]


def fold_kernel(own_ref, got_ref, *outs):
    for k in range(8):
        outs[k][...] = (own_ref[k].astype(F32) + got_ref[k].astype(F32)).astype(BF)


def fold_call(own, got):
    _, rows, cols = own.shape
    return pl.pallas_call(
        fold_kernel,
        out_shape=[jax.ShapeDtypeStruct((rows, cols), BF)] * 8,
        compiler_params=params(),
        cost_estimate=cost(1, 48 * rows * cols),
        name="fold",
    )(own, got)


def pair_kernel(chunks, info, *refs):
    out = refs[-1]
    rows = out.shape[1]
    per = refs[0].shape[0]
    for side in range(2):
        first = (info[0] ^ side) * (chunks * per)
        for c in range(chunks):
            ref = refs[side * chunks + c]
            for k in range(per):
                out[first + c * per + k] = ref[k, :rows, :]


def pair_call(info, own, other, rows):
    per, _, width = own[0].shape
    chunks = len(own)
    return pl.pallas_call(
        functools.partial(pair_kernel, chunks),
        grid_spec=pltpu.PrefetchScalarGridSpec(
            num_scalar_prefetch=1,
            grid=(1,),
            in_specs=[pl.BlockSpec(own[0].shape, lambda i, info: (0, 0, 0))] * (2 * chunks),
            out_specs=pl.BlockSpec((2 * chunks * per, rows, width), lambda i, info: (0, 0, 0)),
        ),
        out_shape=jax.ShapeDtypeStruct((2 * chunks * per, rows, width), BF),
        compiler_params=params(),
        cost_estimate=cost(1, 4 * chunks * per * rows * width * 2),
        name="pair",
    )(info, *own, *other)


def adam_kernel(load_ref, attn_ref, ff_ref, *refs):
    inner, output, expand, reduce, vector = (refs[3 * k : 3 * k + 3] for k in range(5))
    outs = refs[15:]
    load = load_ref[...]
    vectors = load[0:7]
    total = load[7:8, 0:1] + jnp.sum(jnp.sum(vectors * vectors, 0, keepdims=True), 1, keepdims=True)
    norm = jnp.sqrt(total)
    outs[15][...] = norm
    factor = CLIP_RATE * math.sqrt(4 * D * D + 2 * D * FF + FF + 7 * D) / norm

    def update(which, at, grad, rate, decay_rate):
        state = refs[3 * which : 3 * which + 3]
        for ref, new in zip(
            outs[3 * which : 3 * which + 3],
            adamw(*(ref[at] for ref in state), factor * grad, rate, decay_rate),
        ):
            ref[at] = new

    low, high = slice(0, 128), slice(128, 192)
    every = slice(None)
    for matrix, first, second in ((0, 384, 512), (1, 0, 256), (2, 128, 320)):
        update(0, (matrix, every, low), attn_ref[:, first : first + 128], 0.03, DECAY)
        update(0, (matrix, every, high), attn_ref[:, second : second + 64], 0.03, DECAY)
    update(1, (low, every), attn_ref[:, 640:768].T, 0.3, DECAY)
    update(1, (high, every), attn_ref[:, 512:640].T[64:128], 0.3, DECAY)
    rows = expand[0].shape[0]
    update(2, Ellipsis, ff_ref[0:rows, :], 0.03, DECAY)
    update(3, Ellipsis, ff_ref[rows : 2 * rows, :], 0.015, DECAY)
    update(4, Ellipsis, vectors, 0.3, 0.0)


def adam_call(load, attn, ff, state):
    shapes = [jax.ShapeDtypeStruct(x.shape, F32) for x in state] + [jax.ShapeDtypeStruct((1, 1), F32)]
    return pl.pallas_call(
        adam_kernel,
        out_shape=shapes,
        compiler_params=params(),
        cost_estimate=cost(1, sum(x.size for x in state) * 4 * 2),
        name="adam",
    )(load, attn, ff, *state)


def norm_kernel(info, byte_ref, lat_ref, vec_ref, norm_ref, normt_ref, raw_ref, lat_norm_ref, lat_normt_ref, scr):
    groups, true_rows, pad_rows = 4, byte_ref.shape[1] // 4, norm_ref.shape[1] // 4
    keys = byte_ref.shape[1]
    scr[pl.ds(0, keys), :] = byte_ref[0].astype(F32)
    gain, bias = vec_ref[2:3, :], vec_ref[3:4, :]
    keep = lax.broadcasted_iota(jnp.int32, (pad_rows, 1), 0) < true_rows
    for g in range(groups):
        rows = jnp.where(keep, scr[pl.ds(g * true_rows, pad_rows), :], 0.0)
        xhat, _ = norm_parts(rows)
        normed = jnp.where(keep, xhat * gain + bias, 0.0)
        here = pl.ds(g * pad_rows, pad_rows)
        raw_ref[0, here, :] = rows.astype(BF)
        norm_ref[0, here, :] = normed.astype(BF)
    normt_ref[0] = norm_ref[0].T
    xhat, _ = norm_parts(lat_ref[0].astype(F32))
    lat_norm = (xhat * vec_ref[0:1, :] + vec_ref[1:2, :]).astype(BF)
    lat_norm_ref[0] = lat_norm
    lat_normt_ref[0] = lat_norm.T


def norm_call(first_item, all_items, info, byte_array, latents, vectors, items, pad_keys):
    _, keys, width = byte_array.shape
    lat_len = latents.shape[1]
    here = lambda i, info: (info[0] * all_items + first_item + i, 0, 0)
    out = lambda i, info: (i, 0, 0)
    return pl.pallas_call(
        norm_kernel,
        grid_spec=pltpu.PrefetchScalarGridSpec(
            num_scalar_prefetch=1,
            grid=(items,),
            in_specs=[
                pl.BlockSpec((1, keys, width), here),
                pl.BlockSpec((1, lat_len, width), here),
                pl.BlockSpec(vectors.shape, lambda i, info: (0, 0)),
            ],
            out_specs=[
                pl.BlockSpec((1, pad_keys, width), out),
                pl.BlockSpec((1, width, pad_keys), out),
                pl.BlockSpec((1, pad_keys, width), out),
                pl.BlockSpec((1, lat_len, width), out),
                pl.BlockSpec((1, width, lat_len), out),
            ],
            scratch_shapes=[pltpu.VMEM((keys + 40, width), F32)],
        ),
        out_shape=[
            jax.ShapeDtypeStruct((items, pad_keys, width), BF),
            jax.ShapeDtypeStruct((items, width, pad_keys), BF),
            jax.ShapeDtypeStruct((items, pad_keys, width), BF),
            jax.ShapeDtypeStruct((items, lat_len, width), BF),
            jax.ShapeDtypeStruct((items, width, lat_len), BF),
        ],
        compiler_params=params(),
        cost_estimate=cost(items * keys * width * 20, items * keys * width * 8),
        name="norms",
    )(info, byte_array, latents, vectors)


SPLITS = (((0, 0, 384, 0), (1, 384, 768, 0)), ((0, 0, 384, 384), (1, 384, 768, 384)))


def attn_fwd_kernel(first_item, info, count_ref, text_ref, norm_ref, lat_ref, *refs):
    if first_item == 0:
        pieces, (part_ref, pt_ref, kv_ref, q_ref, mixed_ref, wkv_ref, wqo_ref) = refs[:11], refs[11:]

        @pl.when(pl.program_id(0) == 0)
        def _():
            assemble(info, pieces, (wkv_ref, wqo_ref), SPLITS)

    else:
        wkv_ref, wqo_ref, part_ref, pt_ref, kv_ref, q_ref, mixed_ref = refs
    wkv = wkv_ref[...].reshape(-1, 768)
    columns = lambda start, stop: wqo_ref[:, :, start:stop].reshape(-1, stop - start)
    item = info[0] * info[3] + first_item + pl.program_id(0)
    patches, texts = count_ref[item], text_ref[item]
    keys = norm_ref.shape[1]
    pad_rows = keys // 4
    true_rows = info[2]
    row = lax.broadcasted_iota(jnp.int32, (keys, 128), 0)
    group = sum(((row >= pad_rows * g).astype(jnp.int32) for g in range(1, 4)))
    inner = row - group * pad_rows
    slot = inner + group * true_rows
    valid = ((slot < PATCHES) & (slot < patches)) | ((slot >= PATCHES) & (slot - PATCHES < texts))
    valid = valid & (inner < true_rows)
    lane_lo = lax.broadcasted_iota(jnp.int32, (128, 128), 1) < HEAD_DIM
    row_lo = lax.broadcasted_iota(jnp.int32, (128, 128), 0) < HEAD_DIM
    kv_all = dot(norm_ref[0], wkv).astype(BF)
    kv_ref[0] = kv_all
    lat_norm = lat_ref[0]
    total = None
    for p in range(2):
        kv = kv_all[:, p * 384 : (p + 1) * 384]
        base = p * 384
        q = dot(lat_norm, columns(base, base + 256)) * SCALE
        q01, q2 = q[:, :128], jnp.where(lane_lo, q[:, 128:], 0.0).astype(BF)
        q_ref[0, p, :, 0:128] = q01.astype(BF)
        q_ref[0, p, :, 128:256] = q2
        stacked = jnp.concatenate([jnp.where(lane_lo, q01, 0.0), jnp.where(lane_lo, 0.0, q01)], 0).astype(BF)
        first = dot_t(kv[:, 0:128], stacked)
        second = dot_t(kv[:, 256:384], q2)
        pieces = []
        for piece in (first[:, 0:128], first[:, 128:256], second):
            piece = jnp.where(valid, piece, NEG_FILL)
            top = jnp.max(piece, 0, keepdims=True)
            expo = jnp.exp(piece - top)
            pieces.append(expo * (1.0 / jnp.sum(expo, 0, keepdims=True)))
        for h in range(3):
            pt_ref[0, p, :, h * 128 : (h + 1) * 128] = pieces[h]
        low01 = jnp.concatenate([pieces[0].astype(BF), pieces[1].astype(BF)], 1)
        o01 = dot(kv[:, 128:256].T, low01)
        o2 = dot(kv[:, 256:384].T, pieces[2].astype(BF))
        mixed2 = jnp.where(row_lo, 0.0, o2).astype(BF)
        mixed01 = jnp.where(row_lo, o01[:, 0:128], o01[:, 128:256]).astype(BF)
        mixed_ref[0, p, 0:128, :] = mixed2
        mixed_ref[0, p, 128:256, :] = mixed01
        mixed = jnp.concatenate([mixed2.T, mixed01.T], 1)
        add = dot_t(mixed, columns(base + 128, base + 384))
        total = add if total is None else total + add
    part_ref[0] = total.astype(BF)


def attn_fwd_call(first_item, info, counts, texts, norm, lat_norm, weights):
    items, keys, width = norm.shape
    lat_len = lat_norm.shape[1]
    out3 = lambda i, *_: (i, 0, 0)
    out4 = lambda i, *_: (i, 0, 0, 0)
    given = [pl.BlockSpec(w.shape, lambda i, *_, d=w.ndim: (0,) * d) for w in weights]
    made = [pl.BlockSpec((8, width // 8, 768), lambda i, *_: (0, 0, 0))] * (2 * (first_item == 0))
    flops = items * 2 * (keys * width * 768 + lat_len * width * 768 + 4 * keys * lat_len * 384)
    return pl.pallas_call(
        functools.partial(attn_fwd_kernel, first_item),
        grid_spec=pltpu.PrefetchScalarGridSpec(
            num_scalar_prefetch=3,
            grid=(items,),
            in_specs=[
                pl.BlockSpec((1, keys, width), out3),
                pl.BlockSpec((1, lat_len, width), out3),
                *given,
            ],
            out_specs=[
                pl.BlockSpec((1, lat_len, width), out3),
                pl.BlockSpec((1, 2, keys, 384), out4),
                pl.BlockSpec((1, keys, 768), out3),
                pl.BlockSpec((1, 2, lat_len, 256), out4),
                pl.BlockSpec((1, 2, 256, lat_len), out4),
                *made,
            ],
        ),
        out_shape=[
            jax.ShapeDtypeStruct((items, lat_len, width), BF),
            jax.ShapeDtypeStruct((items, 2, keys, 384), F32),
            jax.ShapeDtypeStruct((items, keys, 768), BF),
            jax.ShapeDtypeStruct((items, 2, lat_len, 256), BF),
            jax.ShapeDtypeStruct((items, 2, 256, lat_len), BF),
        ]
        + [jax.ShapeDtypeStruct((8, width // 8, 768), BF)] * len(made),
        compiler_params=params(),
        cost_estimate=cost(flops, 8 * 1024 * 1024, items * keys * 768),
        name="attn_fwd",
    )(info, counts, texts, norm, lat_norm, *weights)


def ff_core_kernel(chunk, info, lat_ref, cot_ref, own_ref, got_ref, vec_ref, bias_ref, *refs):
    if chunk == 0:
        pieces, (res_ref, normt_ref, cott_ref, hidden_ref, pre_ref, part_ref, *weights) = refs[:11], refs[11:]
        assemble(info, pieces, weights, (((0, 0, 1536, 0),), ((1, 0, 1536, 0),)))
    else:
        weights, (res_ref, normt_ref, cott_ref, hidden_ref, pre_ref, part_ref) = refs[:2], refs[2:]
    width = vec_ref.shape[1]
    flat = lambda ref: ref[...].reshape(-1, width).astype(F32)
    residual = flat(lat_ref) + (flat(own_ref) + flat(got_ref))
    res_ref[...] = residual
    xhat, _ = norm_parts(residual)
    normed = (xhat * vec_ref[4:5, :] + vec_ref[5:6, :]).astype(BF)
    cot = cot_ref[...].reshape(-1, width)
    total = None
    step = 256
    for p, w_ref in enumerate(weights):
        columns = lambda start: w_ref[:, :, start : start + step].reshape(-1, step)
        for j in range(768 // step):
            cols = slice(j * step, (j + 1) * step)
            w1 = columns(j * step)
            pre = dot(normed, w1) + bias_ref[p : p + 1, cols]
            back = dot(cot, columns(768 + j * step))
            cdf = 0.5 + 0.5 * lax.erf(pre * math.sqrt(0.5))
            pdf = jnp.exp(pre * pre * -0.5) * (1.0 / math.sqrt(2.0 * math.pi))
            hidden_ref[p, :, cols] = (pre * cdf).astype(BF)
            grad = (back * (cdf + pre * pdf)).astype(BF)
            pre_ref[p, :, cols] = grad
            add = dot_t(grad, w1)
            total = add if total is None else total + add
    part_ref[...] = total.astype(BF)
    normt_ref[...] = normed.T
    cott_ref[...] = cot.T


def ff_core_call(chunk, info, latents, cotangent, own, got, vectors, bias, weights):
    items, lat_len, width = own.shape
    rows = items * lat_len
    half = lambda i, info: (2 * info[0] + chunk, 0, 0)
    z3 = lambda i, info: (0, 0, 0)
    z2 = lambda i, info: (0, 0)
    given = [pl.BlockSpec(w.shape, lambda i, info, d=w.ndim: (0,) * d) for w in weights]
    made = [pl.BlockSpec((8, width // 8, 1536), z3)] * (2 * (chunk == 0))
    return pl.pallas_call(
        functools.partial(ff_core_kernel, chunk),
        grid_spec=pltpu.PrefetchScalarGridSpec(
            num_scalar_prefetch=1,
            grid=(1,),
            in_specs=[
                pl.BlockSpec((items, lat_len, width), half),
                pl.BlockSpec((items, lat_len, width), half),
                pl.BlockSpec(own.shape, z3),
                pl.BlockSpec(got.shape, z3),
                pl.BlockSpec(vectors.shape, z2),
                pl.BlockSpec(bias.shape, z2),
                *given,
            ],
            out_specs=[
                pl.BlockSpec((rows, width), z2),
                pl.BlockSpec((width, rows), z2),
                pl.BlockSpec((width, rows), z2),
                pl.BlockSpec((2, rows, 768), z3),
                pl.BlockSpec((2, rows, 768), z3),
                pl.BlockSpec((rows, width), z2),
                *made,
            ],
        ),
        out_shape=[
            jax.ShapeDtypeStruct((rows, width), F32),
            jax.ShapeDtypeStruct((width, rows), BF),
            jax.ShapeDtypeStruct((width, rows), BF),
            jax.ShapeDtypeStruct((2, rows, 768), BF),
            jax.ShapeDtypeStruct((2, rows, 768), BF),
            jax.ShapeDtypeStruct((rows, width), BF),
        ]
        + [jax.ShapeDtypeStruct((8, width // 8, 1536), BF)] * len(made),
        compiler_params=params(),
        cost_estimate=cost(6 * rows * width * 1536, 8 * 1024 * 1024, 2 * rows * 1536),
        name="ff_core",
    )(info, latents, cotangent, own, got, vectors, bias, *weights)


def relative_rows(info, ref):
    block = ref.shape[0] // 8
    return jnp.concatenate([ref[pl.ds(pl.multiple_of((info[4] ^ k) * block, 16), block), :] for k in range(8)], 0)


def ff_grad_kernel(p, info, *refs):
    chunks, refs = (refs[:4], refs[4:8]), refs[8:]
    grad_ref, bias_ref = refs[-5:-3] if p == 0 else refs
    expand, reduce, bias = 0.0, 0.0, 0.0
    for normt_ref, cott_ref, hidden_ref, pre_ref in chunks:
        hidden, pre = hidden_ref[p], pre_ref[p]
        expand += dot(relative_rows(info, normt_ref), pre)
        reduce += dot(relative_rows(info, cott_ref), hidden)
        bias += jnp.sum(pre.astype(F32), 0, keepdims=True)
    grad_ref[:, 0] = expand.astype(BF).reshape(8, -1, expand.shape[1])
    grad_ref[:, 1] = reduce.astype(BF).reshape(8, -1, reduce.shape[1])
    bias_ref[...] = bias
    if p == 0:
        w_refs, (part_ref, cot_sum_ref, acc) = refs[:2], refs[-3:]
        j = pl.program_id(0)
        rows = chunks[0][0].shape[1]
        for c, chunk in enumerate(chunks):
            here = pl.ds(c * rows, rows)
            add = sum(dot_t(chunk[2][q], w_ref[...].reshape(-1, w_ref.shape[2])) for q, w_ref in enumerate(w_refs))
            acc[here, :] = jnp.where(j == 0, 0.0, acc[here, :]) + add

        @pl.when(j == pl.num_programs(0) - 1)
        def _():
            part_ref[...] = acc[...].astype(BF)
            cot_sum_ref[...] = sum(jnp.sum(chunk[1][...].astype(F32), 1, keepdims=True) for chunk in chunks)


def ff_grad_call(p, info, chunks, weights=()):
    width, rows = chunks[0][0].shape
    step = 256
    n = 768 // step
    z2 = lambda j, info: (0, 0)
    per_chunk = [
        pl.BlockSpec((width, rows), z2),
        pl.BlockSpec((width, rows), z2),
        pl.BlockSpec((2, rows, step), lambda j, info: (0, 0, j)),
        pl.BlockSpec((2, rows, step), lambda j, info: (0, 0, j)),
    ]
    specs = [
        pl.BlockSpec((8, 2, width // 8, step), lambda j, info: (0, 0, 0, j)),
        pl.BlockSpec((1, step), lambda j, info: (0, j)),
        pl.BlockSpec((2 * rows, width), z2),
        pl.BlockSpec((width, 1), z2),
    ]
    shapes = [
        jax.ShapeDtypeStruct((8, 2, width // 8, 768), BF),
        jax.ShapeDtypeStruct((1, 768), F32),
        jax.ShapeDtypeStruct((2 * rows, width), BF),
        jax.ShapeDtypeStruct((width, 1), F32),
    ]
    count = 4 if p == 0 else 2
    return pl.pallas_call(
        functools.partial(ff_grad_kernel, p),
        grid_spec=pltpu.PrefetchScalarGridSpec(
            num_scalar_prefetch=1,
            grid=(n,),
            in_specs=per_chunk * 2
            + [pl.BlockSpec((8, width // 8, step), lambda j, info: (0, 0, n + j))] * len(weights),
            out_specs=specs[:count],
            scratch_shapes=[pltpu.VMEM((2 * rows, width), F32)] * (p == 0),
        ),
        out_shape=shapes[:count],
        compiler_params=params(),
        cost_estimate=cost((2 + 2 * (p == 0)) * 2 * rows * width * 1536, (8 + 6 * (p == 0)) * 1024 * 1024),
        name="ff_grad",
    )(info, *chunks[0], *chunks[1], *weights)


def attn_bwd_kernel(last, info, cot_ref, lat_ref, res_ref, own_ref, got_ref, vec_ref,
                    pt_ref, kv_ref, q_ref, mixed_ref, normt_ref, lat_normt_ref, wqo_ref, *refs):
    if last:
        gkv_in, gqo_in, res_grad_ref, lat_part_ref, dkv_ref, sums_ref, g_own_ref, g_oth_ref, gkv, gqo = refs
    else:
        res_grad_ref, lat_part_ref, dkv_ref, sums_ref, gkv, gqo = refs
    i = pl.program_id(0)

    @pl.when(i == 0)
    def _():
        gkv[...] = gkv_in[...] if last else jnp.zeros_like(gkv)
        gqo[...] = gqo_in[...] if last else jnp.zeros_like(gqo)
        sums_ref[...] = jnp.zeros_like(sums_ref)

    xhat, rstd = norm_parts(res_ref[...])
    dy = own_ref[...].astype(F32) + got_ref[...].astype(F32)
    dx, dgain, dbias = norm_back(dy, xhat, rstd, vec_ref[4:5, :])
    grad = cot_ref[0].astype(F32) + dx
    res_grad_ref[...] = grad
    sums_ref[0:1, :] += dgain
    sums_ref[1:2, :] += dbias
    low = grad.astype(BF)
    columns = lambda start, stop: wqo_ref[:, :, start:stop].reshape(-1, stop - start)
    lane_lo = lax.broadcasted_iota(jnp.int32, (128, 128), 1) < HEAD_DIM
    row_lo = lax.broadcasted_iota(jnp.int32, (128, 128), 0) < HEAD_DIM
    both = jnp.concatenate([lat_normt_ref[0], low.T], 1)
    none = jnp.zeros((128, 128), BF)
    total = None
    for p in range(2):
        base = p * 384
        kv = kv_ref[0, :, base : base + 384]
        mixed_grad = dot(low, columns(base + 128, base + 384))
        mg2 = jnp.where(lane_lo, 0.0, mixed_grad[:, 0:128]).astype(BF)
        mg01 = mixed_grad[:, 128:256]
        mg01 = jnp.concatenate([jnp.where(lane_lo, mg01, 0.0), jnp.where(lane_lo, 0.0, mg01)], 0).astype(BF)
        first = dot_t(kv[:, 128:256], mg01)
        second = dot_t(kv[:, 256:384], mg2)
        probs, scores = [], []
        for h, piece in enumerate((first[:, 0:128], first[:, 128:256], second)):
            prob = pt_ref[0, p, :, h * 128 : (h + 1) * 128]
            inner = jnp.sum(piece * prob, 0, keepdims=True)
            scores.append((prob * (piece - inner)).astype(BF))
            probs.append(prob.astype(BF))
        q01 = q_ref[0, p, :, 0:128].astype(F32)
        q01 = jnp.concatenate([jnp.where(lane_lo, q01, 0.0), jnp.where(lane_lo, 0.0, q01)], 0).astype(BF)
        q2 = q_ref[0, p, :, 128:256]
        ds01 = jnp.concatenate(scores[:2], 1)
        dkv_ref[0, :, base : base + 128] = dot(ds01, q01).astype(BF)
        dkv_ref[0, :, base + 128 : base + 256] = dot(jnp.concatenate(probs[:2], 1), mg01).astype(BF)
        dkv_ref[0, :, base + 256 : base + 384] = dot(
            jnp.concatenate([scores[2], probs[2]], 1), jnp.concatenate([q2, mg2], 0)
        ).astype(BF)
        dq01 = dot(kv[:, 0:128].T, ds01)
        dq2 = dot(kv[:, 256:384].T, scores[2])
        dq01 = (jnp.where(row_lo, dq01[:, 0:128], dq01[:, 128:256]) * SCALE).astype(BF)
        dq2 = (jnp.where(row_lo, dq2, 0.0) * SCALE).astype(BF)
        add = dot_t(jnp.concatenate([dq01.T, dq2.T], 1), columns(base, base + 256))
        total = add if total is None else total + add
        right = jnp.concatenate(
            [
                jnp.concatenate([dq01, none], 1),
                jnp.concatenate([dq2, mixed_ref[0, p, 0:128, :]], 1),
                jnp.concatenate([none, mixed_ref[0, p, 128:256, :]], 1),
            ],
            0,
        )
        gqo[:, base : base + 384] += dot_t(both, right)
    lat_part_ref[...] = total.astype(BF)
    lat_hat, _ = norm_parts(lat_ref[0].astype(F32))
    sums_ref[2:3, :] += jnp.sum(total * lat_hat, 0, keepdims=True)
    sums_ref[3:4, :] += jnp.sum(total, 0, keepdims=True)
    gkv[...] += dot(normt_ref[0], dkv_ref[0])

    if last:

        @pl.when(i == pl.num_programs(0) - 1)
        def _():
            block = gkv.shape[0] // 8
            for k in range(8):
                source = pl.ds(pl.multiple_of((info[4] ^ k) * block, 8), block)
                rows = slice(k * block, (k + 1) * block)
                g_own_ref[rows, 0:384] = gkv[source, 0:384].astype(BF)
                g_own_ref[rows, 384:768] = gqo[source, 0:384].astype(BF)
                g_oth_ref[rows, 0:384] = gkv[source, 384:768].astype(BF)
                g_oth_ref[rows, 384:768] = gqo[source, 384:768].astype(BF)


def attn_bwd_call(first_item, all_items, info, cotangent, latents, residual, own, got, vectors,
                  pt, kv, q, mixed, normt, lat_normt, wqo, grads=None):
    items, keys, _ = kv.shape
    width = normt.shape[1]
    lat_len = q.shape[2]
    last = grads is not None
    one = lambda i, *_: (i, 0)
    three = lambda i, *_: (i, 0, 0)
    mine = lambda i, info: (info[0] * all_items + first_item + i, 0, 0)
    four = lambda i, *_: (i, 0, 0, 0)
    z2 = lambda i, *_: (0, 0)
    flops = items * 2 * (keys * width * 768 + 3 * lat_len * width * 768 + 10 * keys * lat_len * 384)
    out_specs = [
        pl.BlockSpec((lat_len, width), one),
        pl.BlockSpec((lat_len, width), one),
        pl.BlockSpec((1, keys, 768), three),
        pl.BlockSpec((4, width), z2),
        pl.BlockSpec((width, 768), z2),
        pl.BlockSpec((width, 768), z2),
    ]
    out_shape = [
        jax.ShapeDtypeStruct((items * lat_len, width), F32),
        jax.ShapeDtypeStruct((items * lat_len, width), BF),
        jax.ShapeDtypeStruct((items, keys, 768), BF),
        jax.ShapeDtypeStruct((4, width), F32),
        jax.ShapeDtypeStruct((width, 768), BF if last else F32),
        jax.ShapeDtypeStruct((width, 768), BF if last else F32),
    ]
    return pl.pallas_call(
        functools.partial(attn_bwd_kernel, last),
        grid_spec=pltpu.PrefetchScalarGridSpec(
            num_scalar_prefetch=1,
            grid=(items,),
            in_specs=[
                pl.BlockSpec((1, lat_len, width), mine),
                pl.BlockSpec((1, lat_len, width), mine),
                pl.BlockSpec((lat_len, width), one),
                pl.BlockSpec((lat_len, width), one),
                pl.BlockSpec((lat_len, width), one),
                pl.BlockSpec(vectors.shape, z2),
                pl.BlockSpec((1, 2, keys, 384), four),
                pl.BlockSpec((1, keys, 768), three),
                pl.BlockSpec((1, 2, lat_len, 256), four),
                pl.BlockSpec((1, 2, 256, lat_len), four),
                pl.BlockSpec((1, width, keys), three),
                pl.BlockSpec((1, width, lat_len), three),
                pl.BlockSpec(wqo.shape, lambda i, *_: (0, 0, 0)),
            ]
            + [pl.BlockSpec((width, 768), z2)] * (2 * last),
            out_specs=out_specs,
            scratch_shapes=[pltpu.VMEM((width, 768), F32), pltpu.VMEM((width, 768), F32)] * last,
        ),
        out_shape=out_shape,
        compiler_params=params(),
        cost_estimate=cost(flops, 12 * 1024 * 1024),
        name="attn_bwd",
    )(info, cotangent, latents, residual, own, got, vectors, pt, kv, q, mixed, normt, lat_normt, wqo, *(grads or ()))


def latent_kernel(info, lat_ref, *refs):
    vec_ref, out_ref = refs[6:]
    width = vec_ref.shape[1]
    half, step = refs[0].shape[0], out_ref.shape[1]
    per = half // step
    for c in range(2):
        grad_ref, own_ref, got_ref = refs[c], refs[2 + c], refs[4 + c]
        xhat, rstd = norm_parts(lat_ref[c * per : (c + 1) * per].reshape(-1, width).astype(F32))
        dy = own_ref[...].astype(F32) + got_ref[...].astype(F32)
        dx, _, _ = norm_back(dy, xhat, rstd, vec_ref[0:1, :])
        out_ref[c * per : (c + 1) * per] = (grad_ref[...] + dx).astype(BF).reshape(per, step, width)


def latent_call(info, latents, grads, own, got, vectors):
    half, width = own[0].shape
    lat_len = latents.shape[1]
    items = 2 * half // lat_len
    z2 = lambda i, info: (0, 0)
    return pl.pallas_call(
        latent_kernel,
        grid_spec=pltpu.PrefetchScalarGridSpec(
            num_scalar_prefetch=1,
            grid=(1,),
            in_specs=[pl.BlockSpec((items, lat_len, width), lambda i, info: (info[0], 0, 0))]
            + [pl.BlockSpec((half, width), z2)] * 6
            + [pl.BlockSpec(vectors.shape, z2)],
            out_specs=pl.BlockSpec((items, lat_len, width), lambda i, info: (0, 0, 0)),
        ),
        out_shape=jax.ShapeDtypeStruct((items, lat_len, width), BF),
        compiler_params=params(),
        cost_estimate=cost(items * lat_len * width * 20, 6 * 1024 * 1024),
        name="latent_back",
    )(info, latents, *grads, *own, *got, vectors)


def byte_part_kernel(info, dkv_ref, raw_ref, wkv_ref, own_ref, send_ref, sums_ref):
    part = dot_t(dkv_ref[0], wkv_ref[...].reshape(-1, 768))
    xhat, _ = norm_parts(raw_ref[0].astype(F32))
    half = part.shape[0] // 2

    @pl.when(pl.program_id(0) == 0)
    def _():
        sums_ref[...] = jnp.zeros_like(sums_ref)

    sums_ref[0:1, :] += jnp.sum(part * xhat, 0, keepdims=True)
    sums_ref[1:2, :] += jnp.sum(part, 0, keepdims=True)
    low = part.astype(BF)

    @pl.when(info[1] == 0)
    def _():
        own_ref[0] = low[:half]
        send_ref[0] = low[half:]

    @pl.when(info[1] != 0)
    def _():
        own_ref[0] = low[half:]
        send_ref[0] = low[:half]


def byte_part_call(info, dkv, raw, wkv):
    items, keys, _ = dkv.shape
    width = raw.shape[2]
    half = keys // 2
    out = lambda i, info: (i, 0, 0)
    z2 = lambda i, info: (0, 0)
    return pl.pallas_call(
        byte_part_kernel,
        grid_spec=pltpu.PrefetchScalarGridSpec(
            num_scalar_prefetch=1,
            grid=(items,),
            in_specs=[
                pl.BlockSpec((1, keys, 768), out),
                pl.BlockSpec((1, keys, width), out),
                pl.BlockSpec(wkv.shape, lambda i, info: (0, 0, 0)),
            ],
            out_specs=[
                pl.BlockSpec((1, half, width), out),
                pl.BlockSpec((1, half, width), out),
                pl.BlockSpec((2, width), z2),
            ],
        ),
        out_shape=[
            jax.ShapeDtypeStruct((items, half, width), BF),
            jax.ShapeDtypeStruct((items, half, width), BF),
            jax.ShapeDtypeStruct((2, width), F32),
        ],
        compiler_params=params(),
        cost_estimate=cost(items * keys * width * 768 * 2, 6 * 1024 * 1024),
        name="byte_part",
    )(info, dkv, raw, wkv)


def byte_back_kernel(info, part_ref, raw_ref, vec_ref, *refs):
    got_refs, (own_ref, oth_ref) = refs[:-2], refs[-2:]
    half = part_ref.shape[1]
    quarter = half // 2
    got = [ref[k] for ref in got_refs for k in range(ref.shape[0])]
    for k, piece in enumerate(got):
        dy = part_ref[k].astype(F32) + piece.astype(F32)
        xhat, rstd = norm_parts(raw_ref[k].astype(F32))
        dx, _, _ = norm_back(dy, xhat, rstd, vec_ref[2:3, :])
        dx = dx.astype(BF)

        @pl.when(info[0] == 0)
        def _():
            own_ref[k] = dx[:quarter]
            oth_ref[k] = dx[quarter:]

        @pl.when(info[0] != 0)
        def _():
            own_ref[k] = dx[quarter:]
            oth_ref[k] = dx[:quarter]


def byte_back_call(info, part, got, raw, vectors):
    items, half, width = part.shape
    z3 = lambda i, info: (0, 0, 0)
    return pl.pallas_call(
        byte_back_kernel,
        grid_spec=pltpu.PrefetchScalarGridSpec(
            num_scalar_prefetch=1,
            grid=(1,),
            in_specs=[
                pl.BlockSpec((items, half, width), z3),
                pl.BlockSpec((items, half, width), lambda i, info: (0, info[1], 0)),
                pl.BlockSpec(vectors.shape, lambda i, info: (0, 0)),
                *(pl.BlockSpec(piece.shape, z3) for piece in got),
            ],
            out_specs=[pl.BlockSpec((items, half // 2, width), z3)] * 2,
        ),
        out_shape=[jax.ShapeDtypeStruct((items, half // 2, width), BF)] * 2,
        compiler_params=params(),
        cost_estimate=cost(items * half * width * 20, 4 * 1024 * 1024),
        name="byte_back",
    )(info, part, raw, vectors, *got)


def body(
    latents, byte_array, cotangent, patch_count, text_len,
    inner_weight, inner_moment, inner_square,
    output_weight, output_moment, output_square,
    expand_weight, expand_moment, expand_square,
    reduce_weight, reduce_moment, reduce_square,
    expand_bias, bias_moment, bias_square,
    norm_vectors, vector_moment, vector_square,
):
    item_count, lat_len, width = latents.shape
    keys = byte_array.shape[1]
    items = item_count // 2
    n = lax.axis_size("dp")
    head = lax.axis_index("head")
    core, xside = head & 1, head >> 1
    true_rows = keys // lax.axis_size("head")
    pad_rows = -(-true_rows // 32) * 32
    pad_keys = 4 * pad_rows
    quick = n == 8
    place = lax.axis_index("dp") if quick else jnp.int32(0)
    info = jnp.stack([core, xside, jnp.int32(true_rows), jnp.int32(items), place]).astype(jnp.int32)
    half_items = items // 2

    low_inner = inner_weight.astype(BF)
    wq, wk, wv = low_inner[0], low_inner[1], low_inner[2]
    wo = output_weight.T.astype(BF)
    pack = jnp.concatenate(
        [wk[:, :128], wv[:, :128], wk[:, 128:], wv[:, 128:], wq[:, :128], wq[:, 128:], wo[:, 128:], wo[:, :128]], 1
    )
    ff_pack = jnp.concatenate([expand_weight.astype(BF), reduce_weight.T.astype(BF)], 1)
    normalise = lambda c, byte_array: norm_call(
        c * half_items, items, info, byte_array, latents, norm_vectors, half_items, pad_keys
    )
    flip = lambda value: swap(value, "head", 1)
    over = lambda value, mask: swap(value, "dp", mask)
    grouped = lambda p: [flip(jnp.concatenate([p[k] for k in group], 0)) for group in GROUPS]
    if quick:
        g = {0: pack, 4: over(pack, 4), 2: over(pack, 2), 1: over(pack, 1)}
        norm0 = normalise(0, byte_array)
        g[4], g[2], g[1], *norm0 = tie(g[4], g[2], g[1], *norm0)
        g[6], g[5], g[3] = over(g[4], 2), over(g[4], 1), over(g[2], 1)
        g[6], g[5], g[3], byte_later, ff_pack = tie(g[6], g[5], g[3], byte_array, ff_pack)
        f = {0: ff_pack}
        f[4], f[2], f[1] = over(f[0], 4), over(f[0], 2), over(f[0], 1)
        g[7] = over(g[6], 1)
        norm1 = normalise(1, byte_later)
        g[7], f[4], f[2], f[1], *norm1 = tie(g[7], f[4], f[2], f[1], *norm1)
        pieces = [g[k] for k in range(8)] + grouped(g)
        pieces[0], f[4], f[2], f[1] = tie(pieces[0], f[4], f[2], f[1])
        f[6], f[5], f[3] = over(f[4], 2), over(f[4], 1), over(f[2], 1)
    else:
        norm0, norm1 = normalise(0, byte_array), normalise(1, byte_array)
        blocks = lax.all_gather(pack, "dp", axis=0, tiled=True).reshape(8, width // 8, 768)
        g = [blocks[k] for k in range(8)]
        pieces = g + grouped(g)
        blocks = lax.all_gather(ff_pack, "dp", axis=0, tiled=True).reshape(8, width // 8, 1536)
        f = [blocks[k] for k in range(8)]
    norm, normt, raw, lat_norm, lat_normt = zip(norm0, norm1)
    bias_other = flip(expand_bias)

    attend = lambda c, weights: attn_fwd_call(
        c * half_items, info, patch_count, text_len, norm[c], lat_norm[c], weights
    )
    part0, *kept0, wkv, wqo = attend(0, pieces)
    got0 = swap(part0, "head", 2)
    if quick:
        first_flip = flip(jnp.concatenate([f[k] for k in GROUPS[0]], 0))
        wkv, f[6], f[5], f[3], first_flip, bias_other = tie(wkv, f[6], f[5], f[3], first_flip, bias_other)
        f[7] = over(f[6], 1)
        second_flip = flip(jnp.concatenate([f[k] for k in GROUPS[1]], 0))
    part1, *kept1 = attend(1, [wkv, wqo])
    part1, got0 = tie(part1, got0)
    got1 = swap(part1, "head", 2)
    if quick:
        part1, second_flip, f[7] = tie(part1, second_flip, f[7])
        ff_pieces = [f[k] for k in range(8)] + [first_flip, second_flip, flip(f[7])]
    else:
        ff_pieces = f + grouped(f)

    bias_both = jnp.stack([expand_bias, bias_other])
    feed = lambda c, part, got, weights: ff_core_call(
        c, info, latents, cotangent, part, got, norm_vectors, bias_both, weights
    )
    res0, *ff0, npart0, ff_own, ff_oth = feed(0, part0, got0, ff_pieces)
    ngot0 = swap(npart0, "head", 2)
    res1, *ff1, npart1 = feed(1, part1, got1, [ff_own, ff_oth])
    npart1, ngot0, pre1 = tie(npart1, ngot0, ff1[3])
    ff1[3] = pre1
    ngot1 = swap(npart1, "head", 2)
    flat = (8, 2 * (width // 8), 768)
    g_oth, bias_oth = ff_grad_call(1, info, [ff0, ff1])
    g_oth, pre1 = tie(g_oth, pre1)
    ff1[3] = pre1
    g_got = flip(g_oth.reshape(flat))
    g_own, bias_own, mlp_part, cot_sum = ff_grad_call(0, info, [ff0, ff1], [ff_own, ff_oth])
    g_own, ngot1, g_got = tie(g_own, ngot1, g_got)
    bias_own = bias_own[0] + flip(bias_oth[0])
    g_own = g_own.reshape(flat)
    t = {k: plus(g_own[k], g_got[k]) for k in (7, 5, 3, 1)}

    attend_back = lambda c, res, npart, ngot, kept, grads: attn_bwd_call(
        c * half_items, items, info, cotangent, latents, res, npart, ngot,
        norm_vectors, *kept, normt[c], lat_normt[c], wqo, grads
    )
    res0, ngot1, t[7], t[5], t[3], t[1] = tie(res0, ngot1, t[7], t[5], t[3], t[1])
    mlp_part = tie(mlp_part, ngot1)[0]
    mlp_got = swap(mlp_part, "head", 2)
    if quick:
        y = {k: over(t[k], 1) for k in (7, 5, 3, 1)}
    rgrad0, lpart0, dkv0, sums0, *grads = attend_back(0, res0, npart0, ngot0, kept0, None)
    if quick:
        dkv0, y[7], y[5] = tie(dkv0, y[7], y[5])
        t[6], t[4] = (plus3(g_own[k], g_got[k], y[k + 1]) for k in (6, 4))
        z6 = over(t[6], 2)
    bown0, bsend0, bsums0 = byte_part_call(info, dkv0, raw[0], wkv)
    if quick:
        res1, mlp_got, bsend0, z6, y[3] = tie(res1, mlp_got, bsend0, z6, y[3])
        t[4], t[2] = plus(t[4], z6), plus3(g_own[2], g_got[2], y[3])
        z4, z2 = over(t[4], 4), over(t[2], 2)
    else:
        res1, mlp_got, bsend0 = tie(res1, mlp_got, bsend0)
    bgot0 = swap(bsend0, "head", 2)
    lgot0 = swap(lpart0, "head", 2)
    rgrad1, lpart1, dkv1, sums1, g_attn, g_attn_oth = attend_back(1, res1, npart1, ngot1, kept1, grads)
    if quick:
        g_attn_oth, z4, z2, y[1], bgot0 = tie(g_attn_oth, z4, z2, y[1], bgot0)
        g_ff = sum(value.astype(F32) for value in (g_own[0], g_got[0], y[1], z2, z4))
    else:
        g_ff = (g_own.astype(F32) + g_got.astype(F32)).reshape(8, 2, width // 8, 768).swapaxes(0, 1)
        g_ff = lax.psum_scatter(g_ff.reshape(2, width, 768), "dp", scatter_dimension=1, tiled=True)
        g_ff = g_ff.reshape(-1, 768)
    g_attn_got = flip(g_attn_oth)
    lgot1 = swap(lpart1, "head", 2)
    u = list(fold_call(g_attn.reshape(8, width // 8, 768), g_attn_got.reshape(8, width // 8, 768)))
    dkv1, lgot0, mlp_got, u[7] = tie(dkv1, lgot0, mlp_got, u[7])

    residual = jnp.concatenate([res0, res1], 0)
    block_mine = residual + (mlp_part.astype(F32) + mlp_got.astype(F32)) + norm_vectors[6]
    block_mine = block_mine.astype(BF).reshape(items, lat_len, width)
    block_flip = flip(block_mine)

    if quick:
        y = {k: over(u[k], 1) for k in (7, 5, 3, 1)}
    bown1, bsend1, bsums1 = byte_part_call(info, dkv1, raw[1], wkv)
    if quick:
        bsend1, y[7], y[5], ff_squares, lgot1 = tie(bsend1, y[7], y[5], jnp.sum(g_ff * g_ff), lgot1)
    bgot1 = swap(bsend1, "head", 2)
    if quick:
        u[6], u[4] = plus(u[6], y[7]), plus(u[4], y[5])
        z6 = over(u[6], 2)
    byte_side = lambda c, own, got: byte_back_call(info, own, got, raw[c], norm_vectors)
    side0 = list(byte_side(0, bown0, [bgot0]))
    if quick:
        side0[0], block_flip, z6, y[3], y[1] = tie(side0[0], block_flip, z6, y[3], y[1])
        z4, z2 = over(plus(u[4], z6), 4), over(plus(u[2], y[3]), 2)
    lat_mine = latent_call(info, latents, [rgrad0, rgrad1], [lpart0, lpart1], [lgot0, lgot1], norm_vectors)
    block_output = pair_call(info, [block_mine], [block_flip], lat_len)
    if quick:
        lat_mine, block_output, z4, z2, bgot1 = tie(lat_mine, block_output, z4, z2, bgot1)
        g_attn = sum(value.astype(F32) for value in (u[0], y[1], z2, z4))
    else:
        g_attn = lax.psum_scatter(jnp.concatenate(u, 0).astype(F32), "dp", scatter_dimension=0, tiled=True)
    lat_flip = flip(lat_mine)
    side1 = byte_side(1, bown1, [bgot1])

    once = (xside == 0).astype(F32)
    squares = (ff_squares if quick else jnp.sum(g_ff * g_ff)) + jnp.sum(g_attn * g_attn)
    sums = sums0 + sums1
    vec = jnp.concatenate([sums[2:4], bsums0 + bsums1, sums[0:2] * once, (cot_sum * once).reshape(1, width)], 0)
    load = jnp.concatenate([vec, bias_own[None], jnp.full((1, width), squares, F32)], 0)
    beside = [
        lambda: pair_call(info, [lat_mine], [lat_flip], lat_len),
        lambda: side1,
        lambda: pair_call(
            info, [side0[0], outs[1][0]], [flip(side0[1]), flip(outs[1][1])], true_rows
        ),
    ]
    outs = []
    mask = n // 2
    while mask:
        hop = over(load, mask)
        if beside:
            hop, out = tie(hop, beside.pop(0)())
            outs.append(out)
        load = load + hop
        mask //= 2
    latent_gradient, _, byte_gradient = outs
    bias_sum = load[7:8]
    squares = load[8:9] + jnp.sum(bias_sum * bias_sum)
    load = jnp.concatenate([load[:7], squares], 0)
    load = load + swap(load, "head", 1)
    load = load + swap(load, "head", 2)

    *news, grad_norm = adam_call(
        load,
        g_attn,
        g_ff,
        [
            inner_weight, inner_moment, inner_square, output_weight, output_moment, output_square,
            expand_weight, expand_moment, expand_square, reduce_weight.T, reduce_moment.T, reduce_square.T,
            norm_vectors, vector_moment, vector_square,
        ],
    )
    factor = CLIP_RATE * math.sqrt(4 * D * D + 2 * D * FF + FF + 7 * D) / grad_norm[0, 0]
    bias_new = adamw(expand_bias, bias_moment, bias_square, factor * bias_sum[0], 0.3, 0.0)
    news[9:12] = [new.T for new in news[9:12]]
    return (
        block_output, latent_gradient, byte_gradient, *news[:12], *bias_new, *news[12:], grad_norm[0, 0]
    )


def solution(mesh):
    rows, cols = P("dp", "head"), P("head", "dp")
    inner, items = P(None, "dp", "head"), P("dp", None, None)
    weights = (inner,) * 3 + (cols,) * 3 + (rows,) * 3 + (cols,) * 3 + (P("head"),) * 3 + (P(),) * 3
    return jax.shard_map(
        body,
        mesh=mesh,
        in_specs=(items, items, items, P("dp"), P("dp")) + weights,
        out_specs=(items, items, P("dp", "head", None)) + weights + (P(),),
        check_vma=False,
    )
```

```python
import functools
import math

import jax
import jax.numpy as jnp
from jax import lax
from jax.experimental import pallas as pl
from jax.experimental.pallas import tpu as pltpu
from jax.sharding import PartitionSpec as P

D = 768
HEAD_DIM = 64
FF = 3072
PATCHES = 576
STEP = 5

NEG_FILL = -1000000000.0
BETA = 0.5
ADAM_EPS = 1e-08
DECAY = 0.01
CLIP_RATE = 0.01
LN_EPS = 1e-05
SCALE = 1.0 / math.sqrt(HEAD_DIM)
BF = jnp.bfloat16
F32 = jnp.float32
VMEM_LIMIT = 20 * 1024 * 1024


def dot(a, b):
    return lax.dot_general(a, b, (((1,), (0,)), ((), ())), preferred_element_type=F32)


def dot_t(a, b):
    return lax.dot_general(a, b, (((1,), (1,)), ((), ())), preferred_element_type=F32)


def norm_parts(rows):
    centred = rows - jnp.mean(rows, -1, keepdims=True)
    rstd = lax.rsqrt(jnp.mean(centred * centred, -1, keepdims=True) + LN_EPS)
    return centred * rstd, rstd


def norm_back(dy, xhat, rstd, gain):
    scaled = dy * gain
    first = jnp.mean(scaled, -1, keepdims=True)
    second = jnp.mean(scaled * xhat, -1, keepdims=True)
    dx = rstd * (scaled - first - xhat * second)
    return dx, jnp.sum(dy * xhat, 0, keepdims=True), jnp.sum(dy, 0, keepdims=True)


def swap(value, axis, mask):
    size = lax.axis_size(axis)
    return lax.ppermute(value, axis, [(i, i ^ mask) for i in range(size)])


def tie(*values):
    return lax.optimization_barrier(tuple(values))


def plus(a, b):
    return (a.astype(F32) + b.astype(F32)).astype(BF)


def plus3(a, b, c):
    return (a.astype(F32) + b.astype(F32) + c.astype(F32)).astype(BF)


def adamw(weight, moment, square, gradient, rate, decay_rate):
    moment_new = BETA * moment + (1.0 - BETA) * gradient
    square_new = BETA * square + (1.0 - BETA) * gradient * gradient
    correction = 1.0 - BETA**STEP
    step_dir = moment_new * (1.0 / correction) / (jnp.sqrt(square_new * (1.0 / correction)) + ADAM_EPS)
    return (weight - rate * (step_dir + decay_rate * weight), moment_new, square_new)


def params(**kw):
    return pltpu.CompilerParams(vmem_limit_bytes=VMEM_LIMIT, **kw)


def cost(flops, nbytes, trans=0):
    return pl.CostEstimate(flops=flops, bytes_accessed=nbytes, transcendentals=trans)


GROUPS = ((0, 4, 2, 1), (6, 5, 3), (7,))


def assemble(info, parts, outs, splits):
    rows = parts[0].shape[0]
    blocks = [(k, 0, parts[k], 0) for k in range(8)]
    for part, group in zip(parts[8:], GROUPS):
        blocks += [(k, 1, part, i * rows) for i, k in enumerate(group)]
    for k, c, part, first in blocks:
        for out, start, stop, offset in splits[c]:
            outs[out][info[4] ^ k, :, offset : offset + stop - start] = part[first : first + rows, start:stop]


ORDER = (7, 5, 3, 1, 6, 4, 2, 0)


def pair_kernel(chunks, info, *refs):
    out = refs[-1]
    rows = out.shape[1]
    per = refs[0].shape[0]
    for side in range(2):
        first = (info[0] ^ side) * (chunks * per)
        for c in range(chunks):
            ref = refs[side * chunks + c]
            for k in range(per):
                out[first + c * per + k] = ref[k, :rows, :]


def pair_call(info, own, other, rows):
    per, _, width = own[0].shape
    chunks = len(own)
    return pl.pallas_call(
        functools.partial(pair_kernel, chunks),
        grid_spec=pltpu.PrefetchScalarGridSpec(
            num_scalar_prefetch=1,
            grid=(1,),
            in_specs=[pl.BlockSpec(own[0].shape, lambda i, info: (0, 0, 0))] * (2 * chunks),
            out_specs=pl.BlockSpec((2 * chunks * per, rows, width), lambda i, info: (0, 0, 0)),
        ),
        out_shape=jax.ShapeDtypeStruct((2 * chunks * per, rows, width), BF),
        compiler_params=params(),
        cost_estimate=cost(1, 4 * chunks * per * rows * width * 2),
        name="pair",
    )(info, *own, *other)


def adam_kernel(load_ref, attn_ref, ff_ref, *refs):
    inner, output, expand, reduce, vector = (refs[3 * k : 3 * k + 3] for k in range(5))
    outs = refs[15:]
    load = load_ref[...]
    vectors = load[0:7]
    total = load[7:8, 0:1] + jnp.sum(jnp.sum(vectors * vectors, 0, keepdims=True), 1, keepdims=True)
    norm = jnp.sqrt(total)
    outs[15][...] = norm
    factor = CLIP_RATE * math.sqrt(4 * D * D + 2 * D * FF + FF + 7 * D) / norm

    def update(which, at, grad, rate, decay_rate):
        state = refs[3 * which : 3 * which + 3]
        for ref, new in zip(
            outs[3 * which : 3 * which + 3],
            adamw(*(ref[at] for ref in state), factor * grad, rate, decay_rate),
        ):
            ref[at] = new

    low, high = slice(0, 128), slice(128, 192)
    every = slice(None)
    for matrix, first, second in ((0, 384, 512), (1, 0, 256), (2, 128, 320)):
        update(0, (matrix, every, low), attn_ref[:, first : first + 128], 0.03, DECAY)
        update(0, (matrix, every, high), attn_ref[:, second : second + 64], 0.03, DECAY)
    update(1, (low, every), attn_ref[:, 640:768].T, 0.3, DECAY)
    update(1, (high, every), attn_ref[:, 512:640].T[64:128], 0.3, DECAY)
    rows = expand[0].shape[0]
    update(2, Ellipsis, ff_ref[0:rows, :], 0.03, DECAY)
    update(3, Ellipsis, ff_ref[rows : 2 * rows, :], 0.015, DECAY)
    update(4, Ellipsis, vectors, 0.3, 0.0)


def adam_call(load, attn, ff, state):
    shapes = [jax.ShapeDtypeStruct(x.shape, F32) for x in state] + [jax.ShapeDtypeStruct((1, 1), F32)]
    return pl.pallas_call(
        adam_kernel,
        out_shape=shapes,
        compiler_params=params(),
        cost_estimate=cost(1, sum(x.size for x in state) * 4 * 2),
        name="adam",
    )(load, attn, ff, *state)


def norm_kernel(info, byte_ref, lat_ref, vec_ref, norm_ref, normt_ref, raw_ref, lat_norm_ref, lat_normt_ref, scr):
    groups, true_rows, pad_rows = 4, byte_ref.shape[1] // 4, norm_ref.shape[1] // 4
    keys = byte_ref.shape[1]
    scr[pl.ds(0, keys), :] = byte_ref[0].astype(F32)
    gain, bias = vec_ref[2:3, :], vec_ref[3:4, :]
    keep = lax.broadcasted_iota(jnp.int32, (pad_rows, 1), 0) < true_rows
    for g in range(groups):
        rows = jnp.where(keep, scr[pl.ds(g * true_rows, pad_rows), :], 0.0)
        xhat, _ = norm_parts(rows)
        normed = jnp.where(keep, xhat * gain + bias, 0.0)
        here = pl.ds(g * pad_rows, pad_rows)
        raw_ref[0, here, :] = rows.astype(BF)
        norm_ref[0, here, :] = normed.astype(BF)
    normt_ref[0] = norm_ref[0].T
    xhat, _ = norm_parts(lat_ref[0].astype(F32))
    lat_norm = (xhat * vec_ref[0:1, :] + vec_ref[1:2, :]).astype(BF)
    lat_norm_ref[0] = lat_norm
    lat_normt_ref[0] = lat_norm.T


def norm_call(first_item, all_items, info, byte_array, latents, vectors, items, pad_keys):
    _, keys, width = byte_array.shape
    lat_len = latents.shape[1]
    here = lambda i, info: (info[0] * all_items + first_item + i, 0, 0)
    out = lambda i, info: (i, 0, 0)
    return pl.pallas_call(
        norm_kernel,
        grid_spec=pltpu.PrefetchScalarGridSpec(
            num_scalar_prefetch=1,
            grid=(items,),
            in_specs=[
                pl.BlockSpec((1, keys, width), here),
                pl.BlockSpec((1, lat_len, width), here),
                pl.BlockSpec(vectors.shape, lambda i, info: (0, 0)),
            ],
            out_specs=[
                pl.BlockSpec((1, pad_keys, width), out),
                pl.BlockSpec((1, width, pad_keys), out),
                pl.BlockSpec((1, pad_keys, width), out),
                pl.BlockSpec((1, lat_len, width), out),
                pl.BlockSpec((1, width, lat_len), out),
            ],
            scratch_shapes=[pltpu.VMEM((keys + 40, width), F32)],
        ),
        out_shape=[
            jax.ShapeDtypeStruct((items, pad_keys, width), BF),
            jax.ShapeDtypeStruct((items, width, pad_keys), BF),
            jax.ShapeDtypeStruct((items, pad_keys, width), BF),
            jax.ShapeDtypeStruct((items, lat_len, width), BF),
            jax.ShapeDtypeStruct((items, width, lat_len), BF),
        ],
        compiler_params=params(),
        cost_estimate=cost(items * keys * width * 20, items * keys * width * 8),
        name="norms",
    )(info, byte_array, latents, vectors)


SPLITS = (((0, 0, 384, 0), (1, 384, 768, 0)), ((0, 0, 384, 384), (1, 384, 768, 384)))


def attn_fwd_kernel(first_item, info, count_ref, text_ref, norm_ref, lat_ref, *refs):
    if first_item == 0:
        pieces, (mixed_ref, pt_ref, kv_ref, q_ref, wkv_ref, wqo_ref) = refs[:11], refs[11:]

        @pl.when(pl.program_id(0) == 0)
        def _():
            assemble(info, pieces, (wkv_ref, wqo_ref), SPLITS)

    else:
        wkv_ref, wqo_ref, mixed_ref, pt_ref, kv_ref, q_ref = refs
    wkv = wkv_ref[...].reshape(-1, 768)
    columns = lambda start, stop: wqo_ref[:, :, start:stop].reshape(-1, stop - start)
    item = info[0] * info[3] + first_item + pl.program_id(0)
    patches, texts = count_ref[item], text_ref[item]
    keys = norm_ref.shape[1]
    pad_rows = keys // 4
    true_rows = info[2]
    row = lax.broadcasted_iota(jnp.int32, (keys, 128), 0)
    group = sum(((row >= pad_rows * g).astype(jnp.int32) for g in range(1, 4)))
    inner = row - group * pad_rows
    slot = inner + group * true_rows
    valid = ((slot < PATCHES) & (slot < patches)) | ((slot >= PATCHES) & (slot - PATCHES < texts))
    valid = valid & (inner < true_rows)
    lane_lo = lax.broadcasted_iota(jnp.int32, (128, 128), 1) < HEAD_DIM
    row_lo = lax.broadcasted_iota(jnp.int32, (128, 128), 0) < HEAD_DIM
    kv_all = dot(norm_ref[0], wkv).astype(BF)
    kv_ref[0] = kv_all
    lat_norm = lat_ref[0]
    for p in range(2):
        kv = kv_all[:, p * 384 : (p + 1) * 384]
        base = p * 384
        q = dot(lat_norm, columns(base, base + 256)) * SCALE
        q01, q2 = q[:, :128], jnp.where(lane_lo, q[:, 128:], 0.0).astype(BF)
        q_ref[0, p, :, 0:128] = q01.astype(BF)
        q_ref[0, p, :, 128:256] = q2
        stacked = jnp.concatenate([jnp.where(lane_lo, q01, 0.0), jnp.where(lane_lo, 0.0, q01)], 0).astype(BF)
        first = dot_t(kv[:, 0:128], stacked)
        second = dot_t(kv[:, 256:384], q2)
        pieces = []
        for piece in (first[:, 0:128], first[:, 128:256], second):
            piece = jnp.where(valid, piece, NEG_FILL)
            top = jnp.max(piece, 0, keepdims=True)
            expo = jnp.exp(piece - top)
            pieces.append(expo * (1.0 / jnp.sum(expo, 0, keepdims=True)))
        for h in range(3):
            pt_ref[0, p, :, h * 128 : (h + 1) * 128] = pieces[h]
        low01 = jnp.concatenate([pieces[0].astype(BF), pieces[1].astype(BF)], 1)
        o01 = dot(kv[:, 128:256].T, low01)
        o2 = dot(kv[:, 256:384].T, pieces[2].astype(BF))
        mixed_ref[0, p, 0:64, :] = o2[64:128].astype(BF)
        mixed_ref[0, p, 64:192, :] = jnp.where(row_lo, o01[:, 0:128], o01[:, 128:256]).astype(BF)


def attn_fwd_call(first_item, info, counts, texts, norm, lat_norm, weights):
    items, keys, width = norm.shape
    lat_len = lat_norm.shape[1]
    out3 = lambda i, *_: (i, 0, 0)
    out4 = lambda i, *_: (i, 0, 0, 0)
    given = [pl.BlockSpec(w.shape, lambda i, *_, d=w.ndim: (0,) * d) for w in weights]
    made = [pl.BlockSpec((8, width // 8, 768), lambda i, *_: (0, 0, 0))] * (2 * (first_item == 0))
    flops = items * 2 * (keys * width * 768 + lat_len * width * 768 + 4 * keys * lat_len * 384)
    return pl.pallas_call(
        functools.partial(attn_fwd_kernel, first_item),
        grid_spec=pltpu.PrefetchScalarGridSpec(
            num_scalar_prefetch=3,
            grid=(items,),
            in_specs=[
                pl.BlockSpec((1, keys, width), out3),
                pl.BlockSpec((1, lat_len, width), out3),
                *given,
            ],
            out_specs=[
                pl.BlockSpec((1, 2, 192, lat_len), out4),
                pl.BlockSpec((1, 2, keys, 384), out4),
                pl.BlockSpec((1, keys, 768), out3),
                pl.BlockSpec((1, 2, lat_len, 256), out4),
                *made,
            ],
        ),
        out_shape=[
            jax.ShapeDtypeStruct((items, 2, 192, lat_len), BF),
            jax.ShapeDtypeStruct((items, 2, keys, 384), F32),
            jax.ShapeDtypeStruct((items, keys, 768), BF),
            jax.ShapeDtypeStruct((items, 2, lat_len, 256), BF),
        ]
        + [jax.ShapeDtypeStruct((8, width // 8, 768), BF)] * len(made),
        compiler_params=params(),
        cost_estimate=cost(flops, 8 * 1024 * 1024, items * keys * 768),
        name="attn_fwd",
    )(info, counts, texts, norm, lat_norm, *weights)


def spread(mixed_ref, w_ref, queries):
    zeros = jnp.zeros((64, mixed_ref.shape[3]), BF)
    total = []
    for item in range(mixed_ref.shape[0]):
        rows = None
        for p in range(2):
            mixed = mixed_ref[item, p]
            parts = (mixed[0:128], mixed[128:192], zeros) if queries else (zeros, mixed[0:64], mixed[64:192])
            first = p * 384 + 128 * (not queries)
            columns = w_ref[:, :, first : first + 256].reshape(-1, 256)
            add = dot_t(jnp.concatenate(parts, 0).T, columns)
            rows = add if rows is None else rows + add
        total.append(rows)
    return jnp.concatenate(total, 0)


def ff_core_kernel(chunk, info, lat_ref, cot_ref, own_ref, got_ref, vec_ref, bias_ref, wqo_ref, *refs):
    if chunk == 0:
        pieces, crossed = refs[:11], refs[11:13]
        res_ref, normt_ref, cott_ref, hidden_ref, pre_ref, part_ref, cot_sum_ref, *weights, wqx_ref = refs[13:]
        assemble(info, pieces, weights, (((0, 0, 1536, 0),), ((1, 0, 1536, 0),)))
        rows = wqx_ref.shape[1]
        for k in range(8):
            for c in range(2):
                wqx_ref[info[4] ^ k, :, 384 * c : 384 * (c + 1)] = crossed[c][k * rows : (k + 1) * rows, :]
    else:
        weights, wqx_ref = refs[:2], refs[2]
        res_ref, normt_ref, cott_ref, hidden_ref, pre_ref, part_ref, cot_sum_ref = refs[3:]
    width = vec_ref.shape[1]
    flat = lambda ref: ref[...].reshape(-1, width).astype(F32)
    residual = flat(lat_ref) + (spread(own_ref, wqo_ref, False) + spread(got_ref, wqx_ref, False))
    res_ref[...] = residual
    xhat, _ = norm_parts(residual)
    normed = (xhat * vec_ref[4:5, :] + vec_ref[5:6, :]).astype(BF)
    cot = cot_ref[...].reshape(-1, width)
    total = None
    step = 256
    for p, w_ref in enumerate(weights):
        columns = lambda start: w_ref[:, :, start : start + step].reshape(-1, step)
        for j in range(768 // step):
            cols = slice(j * step, (j + 1) * step)
            w1 = columns(j * step)
            pre = dot(normed, w1) + bias_ref[p : p + 1, cols]
            back = dot(cot, columns(768 + j * step))
            cdf = 0.5 + 0.5 * lax.erf(pre * math.sqrt(0.5))
            pdf = jnp.exp(pre * pre * -0.5) * (1.0 / math.sqrt(2.0 * math.pi))
            hidden_ref[p, :, cols] = (pre * cdf).astype(BF)
            grad = (back * (cdf + pre * pdf)).astype(BF)
            pre_ref[p, :, cols] = grad
            add = dot_t(grad, w1)
            total = add if total is None else total + add
    part_ref[...] = total.astype(BF)
    normt_ref[...] = normed.T
    cott_ref[...] = cot.T
    cot_sum_ref[...] = jnp.sum(cot.astype(F32), 0, keepdims=True)


def ff_core_call(chunk, info, latents, cotangent, own, got, vectors, bias, wqo, weights):
    items = own.shape[0]
    _, lat_len, width = latents.shape
    rows = items * lat_len
    half = lambda i, info: (2 * info[0] + chunk, 0, 0)
    z3 = lambda i, info: (0, 0, 0)
    z4 = lambda i, info: (0, 0, 0, 0)
    z2 = lambda i, info: (0, 0)
    given = [pl.BlockSpec(w.shape, lambda i, info, d=w.ndim: (0,) * d) for w in weights]
    lanes = (1536, 1536, 768) if chunk == 0 else ()
    made = [pl.BlockSpec((8, width // 8, cols), z3) for cols in lanes]
    return pl.pallas_call(
        functools.partial(ff_core_kernel, chunk),
        grid_spec=pltpu.PrefetchScalarGridSpec(
            num_scalar_prefetch=1,
            grid=(1,),
            in_specs=[
                pl.BlockSpec((items, lat_len, width), half),
                pl.BlockSpec((items, lat_len, width), half),
                pl.BlockSpec(own.shape, z4),
                pl.BlockSpec(got.shape, z4),
                pl.BlockSpec(vectors.shape, z2),
                pl.BlockSpec(bias.shape, z2),
                pl.BlockSpec(wqo.shape, z3),
                *given,
            ],
            out_specs=[
                pl.BlockSpec((rows, width), z2),
                pl.BlockSpec((width, rows), z2),
                pl.BlockSpec((width, rows), z2),
                pl.BlockSpec((2, rows, 768), z3),
                pl.BlockSpec((2, rows, 768), z3),
                pl.BlockSpec((rows, width), z2),
                pl.BlockSpec((1, width), z2),
                *made,
            ],
        ),
        out_shape=[
            jax.ShapeDtypeStruct((rows, width), F32),
            jax.ShapeDtypeStruct((width, rows), BF),
            jax.ShapeDtypeStruct((width, rows), BF),
            jax.ShapeDtypeStruct((2, rows, 768), BF),
            jax.ShapeDtypeStruct((2, rows, 768), BF),
            jax.ShapeDtypeStruct((rows, width), BF),
            jax.ShapeDtypeStruct((1, width), F32),
        ]
        + [jax.ShapeDtypeStruct((8, width // 8, cols), BF) for cols in lanes],
        compiler_params=params(),
        cost_estimate=cost(6 * rows * width * 1536, 8 * 1024 * 1024, 2 * rows * 1536),
        name="ff_core",
    )(info, latents, cotangent, own, got, vectors, bias, wqo, *weights)


def relative_rows(info, ref):
    block = ref.shape[0] // 8
    return jnp.concatenate([ref[pl.ds(pl.multiple_of((info[4] ^ k) * block, 16), block), :] for k in ORDER], 0)


def ff_grad_kernel(p, info, *refs):
    chunks, refs = (refs[:4], refs[4:8]), refs[8:]
    grad_ref, bias_ref = refs[-4:-2] if p == 0 else refs
    expand, reduce, bias = 0.0, 0.0, 0.0
    for normt_ref, cott_ref, hidden_ref, pre_ref in chunks:
        hidden, pre = hidden_ref[p], pre_ref[p]
        expand += dot(relative_rows(info, normt_ref), pre)
        reduce += dot(relative_rows(info, cott_ref), hidden)
        bias += jnp.sum(pre.astype(F32), 0, keepdims=True)
    grad_ref[:, 0] = expand.astype(BF).reshape(8, -1, expand.shape[1])
    grad_ref[:, 1] = reduce.astype(BF).reshape(8, -1, reduce.shape[1])
    bias_ref[...] = bias
    if p == 0:
        w_refs, (part_ref, acc) = refs[:2], refs[-2:]
        j = pl.program_id(0)
        rows = chunks[0][0].shape[1]
        for c, chunk in enumerate(chunks):
            here = pl.ds(c * rows, rows)
            add = sum(dot_t(chunk[2][q], w_ref[...].reshape(-1, w_ref.shape[2])) for q, w_ref in enumerate(w_refs))
            acc[here, :] = jnp.where(j == 0, 0.0, acc[here, :]) + add

        @pl.when(j == pl.num_programs(0) - 1)
        def _():
            part_ref[...] = acc[...].astype(BF)


def ff_grad_call(p, info, chunks, weights=()):
    width, rows = chunks[0][0].shape
    step = 256
    n = 768 // step
    z2 = lambda j, info: (0, 0)
    per_chunk = [
        pl.BlockSpec((width, rows), z2),
        pl.BlockSpec((width, rows), z2),
        pl.BlockSpec((2, rows, step), lambda j, info: (0, 0, j)),
        pl.BlockSpec((2, rows, step), lambda j, info: (0, 0, j)),
    ]
    specs = [
        pl.BlockSpec((8, 2, width // 8, step), lambda j, info: (0, 0, 0, j)),
        pl.BlockSpec((1, step), lambda j, info: (0, j)),
        pl.BlockSpec((2 * rows, width), z2),
    ]
    shapes = [
        jax.ShapeDtypeStruct((8, 2, width // 8, 768), BF),
        jax.ShapeDtypeStruct((1, 768), F32),
        jax.ShapeDtypeStruct((2 * rows, width), BF),
    ]
    count = 3 if p == 0 else 2
    return pl.pallas_call(
        functools.partial(ff_grad_kernel, p),
        grid_spec=pltpu.PrefetchScalarGridSpec(
            num_scalar_prefetch=1,
            grid=(n,),
            in_specs=per_chunk * 2
            + [pl.BlockSpec((8, width // 8, step), lambda j, info: (0, 0, n + j))] * len(weights),
            out_specs=specs[:count],
            scratch_shapes=[pltpu.VMEM((2 * rows, width), F32)] * (p == 0),
        ),
        out_shape=shapes[:count],
        compiler_params=params(),
        cost_estimate=cost((2 + 2 * (p == 0)) * 2 * rows * width * 1536, (8 + 6 * (p == 0)) * 1024 * 1024),
        name="ff_grad",
    )(info, *chunks[0], *chunks[1], *weights)


def attn_bwd_kernel(last, info, cot_ref, lat_ref, res_ref, own_ref, got_ref, vec_ref,
                    mixed_ref, pt_ref, kv_ref, q_ref, normt_ref, lat_normt_ref, wqo_ref, *refs):
    if last:
        gkv_in, gqo_in, res_grad_ref, dq_ref, dkv_ref, sums_ref, g_own_ref, g_oth_ref, gkv, gqo = refs
    else:
        res_grad_ref, dq_ref, dkv_ref, sums_ref, gkv, gqo = refs
    i = pl.program_id(0)

    @pl.when(i == 0)
    def _():
        gkv[...] = gkv_in[...] if last else jnp.zeros_like(gkv)
        gqo[...] = gqo_in[...] if last else jnp.zeros_like(gqo)
        sums_ref[...] = jnp.zeros_like(sums_ref)

    xhat, rstd = norm_parts(res_ref[...])
    dy = own_ref[...].astype(F32) + got_ref[...].astype(F32)
    dx, dgain, dbias = norm_back(dy, xhat, rstd, vec_ref[4:5, :])
    grad = cot_ref[0].astype(F32) + dx
    res_grad_ref[...] = grad
    sums_ref[0:1, :] += dgain
    sums_ref[1:2, :] += dbias
    low = grad.astype(BF)
    columns = lambda start, stop: wqo_ref[:, :, start:stop].reshape(-1, stop - start)
    lane_lo = lax.broadcasted_iota(jnp.int32, (128, 128), 1) < HEAD_DIM
    row_lo = lax.broadcasted_iota(jnp.int32, (128, 128), 0) < HEAD_DIM
    both = jnp.concatenate([lat_normt_ref[0], low.T], 1)
    none = jnp.zeros((128, 128), BF)
    zeros = jnp.zeros((64, 128), BF)
    total = None
    for p in range(2):
        base = p * 384
        kv = kv_ref[0, :, base : base + 384]
        mixed_grad = dot(low, columns(base + 128, base + 384))
        mg2 = jnp.where(lane_lo, 0.0, mixed_grad[:, 0:128]).astype(BF)
        mg01 = mixed_grad[:, 128:256]
        mg01 = jnp.concatenate([jnp.where(lane_lo, mg01, 0.0), jnp.where(lane_lo, 0.0, mg01)], 0).astype(BF)
        first = dot_t(kv[:, 128:256], mg01)
        second = dot_t(kv[:, 256:384], mg2)
        probs, scores = [], []
        for h, piece in enumerate((first[:, 0:128], first[:, 128:256], second)):
            prob = pt_ref[0, p, :, h * 128 : (h + 1) * 128]
            inner = jnp.sum(piece * prob, 0, keepdims=True)
            scores.append((prob * (piece - inner)).astype(BF))
            probs.append(prob.astype(BF))
        q01 = q_ref[0, p, :, 0:128].astype(F32)
        q01 = jnp.concatenate([jnp.where(lane_lo, q01, 0.0), jnp.where(lane_lo, 0.0, q01)], 0).astype(BF)
        q2 = q_ref[0, p, :, 128:256]
        ds01 = jnp.concatenate(scores[:2], 1)
        dkv_ref[0, :, base : base + 128] = dot(ds01, q01).astype(BF)
        dkv_ref[0, :, base + 128 : base + 256] = dot(jnp.concatenate(probs[:2], 1), mg01).astype(BF)
        dkv_ref[0, :, base + 256 : base + 384] = dot(
            jnp.concatenate([scores[2], probs[2]], 1), jnp.concatenate([q2, mg2], 0)
        ).astype(BF)
        dq01 = dot(kv[:, 0:128].T, ds01)
        dq2 = dot(kv[:, 256:384].T, scores[2])
        dq01 = (jnp.where(row_lo, dq01[:, 0:128], dq01[:, 128:256]) * SCALE).astype(BF)
        dq2 = (jnp.where(row_lo, dq2, 0.0) * SCALE).astype(BF)
        dq_ref[0, p, 0:128, :] = dq01
        dq_ref[0, p, 128:192, :] = dq2[0:64]
        add = dot_t(jnp.concatenate([dq01.T, dq2.T], 1), columns(base, base + 256))
        total = add if total is None else total + add
        right = jnp.concatenate(
            [
                jnp.concatenate([dq01, none], 1),
                jnp.concatenate([dq2, jnp.concatenate([zeros, mixed_ref[0, p, 0:64, :]], 0)], 1),
                jnp.concatenate([none, mixed_ref[0, p, 64:192, :]], 1),
            ],
            0,
        )
        gqo[:, base : base + 384] += dot_t(both, right)
    lat_hat, _ = norm_parts(lat_ref[0].astype(F32))
    sums_ref[2:3, :] += jnp.sum(total * lat_hat, 0, keepdims=True)
    sums_ref[3:4, :] += jnp.sum(total, 0, keepdims=True)
    gkv[...] += dot(normt_ref[0], dkv_ref[0])

    if last:

        @pl.when(i == pl.num_programs(0) - 1)
        def _():
            block = gkv.shape[0] // 8
            for j, k in enumerate(ORDER):
                source = pl.ds(pl.multiple_of((info[4] ^ k) * block, 8), block)
                rows = slice(j * block, (j + 1) * block)
                g_own_ref[rows, 0:384] = gkv[source, 0:384].astype(BF)
                g_own_ref[rows, 384:768] = gqo[source, 0:384].astype(BF)
                g_oth_ref[rows, 0:384] = gkv[source, 384:768].astype(BF)
                g_oth_ref[rows, 384:768] = gqo[source, 384:768].astype(BF)


def attn_bwd_call(first_item, all_items, info, cotangent, latents, residual, own, got, vectors,
                  mixed, pt, kv, q, normt, lat_normt, wqo, grads=None):
    items, keys, _ = kv.shape
    width = normt.shape[1]
    lat_len = q.shape[2]
    last = grads is not None
    one = lambda i, *_: (i, 0)
    three = lambda i, *_: (i, 0, 0)
    mine = lambda i, info: (info[0] * all_items + first_item + i, 0, 0)
    four = lambda i, *_: (i, 0, 0, 0)
    z2 = lambda i, *_: (0, 0)
    flops = items * 2 * (keys * width * 768 + 3 * lat_len * width * 768 + 10 * keys * lat_len * 384)
    out_specs = [
        pl.BlockSpec((lat_len, width), one),
        pl.BlockSpec((1, 2, 192, lat_len), four),
        pl.BlockSpec((1, keys, 768), three),
        pl.BlockSpec((4, width), z2),
        pl.BlockSpec((width, 768), z2),
        pl.BlockSpec((width, 768), z2),
    ]
    out_shape = [
        jax.ShapeDtypeStruct((items * lat_len, width), F32),
        jax.ShapeDtypeStruct((items, 2, 192, lat_len), BF),
        jax.ShapeDtypeStruct((items, keys, 768), BF),
        jax.ShapeDtypeStruct((4, width), F32),
        jax.ShapeDtypeStruct((width, 768), BF if last else F32),
        jax.ShapeDtypeStruct((width, 768), BF if last else F32),
    ]
    return pl.pallas_call(
        functools.partial(attn_bwd_kernel, last),
        grid_spec=pltpu.PrefetchScalarGridSpec(
            num_scalar_prefetch=1,
            grid=(items,),
            in_specs=[
                pl.BlockSpec((1, lat_len, width), mine),
                pl.BlockSpec((1, lat_len, width), mine),
                pl.BlockSpec((lat_len, width), one),
                pl.BlockSpec((lat_len, width), one),
                pl.BlockSpec((lat_len, width), one),
                pl.BlockSpec(vectors.shape, z2),
                pl.BlockSpec((1, 2, 192, lat_len), four),
                pl.BlockSpec((1, 2, keys, 384), four),
                pl.BlockSpec((1, keys, 768), three),
                pl.BlockSpec((1, 2, lat_len, 256), four),
                pl.BlockSpec((1, width, keys), three),
                pl.BlockSpec((1, width, lat_len), three),
                pl.BlockSpec(wqo.shape, lambda i, *_: (0, 0, 0)),
            ]
            + [pl.BlockSpec((width, 768), z2)] * (2 * last),
            out_specs=out_specs,
            scratch_shapes=[pltpu.VMEM((width, 768), F32), pltpu.VMEM((width, 768), F32)] * last,
        ),
        out_shape=out_shape,
        compiler_params=params(),
        cost_estimate=cost(flops, 12 * 1024 * 1024),
        name="attn_bwd",
    )(info, cotangent, latents, residual, own, got, vectors, mixed, pt, kv, q, normt, lat_normt, wqo, *(grads or ()))


def latent_kernel(info, lat_ref, *refs):
    vec_ref, wqo_ref, wqx_ref, out_ref = refs[6:]
    width = vec_ref.shape[1]
    step = out_ref.shape[1]
    per = refs[0].shape[0] // step
    for c in range(2):
        grad_ref, own_ref, got_ref = refs[c], refs[2 + c], refs[4 + c]
        xhat, rstd = norm_parts(lat_ref[c * per : (c + 1) * per].reshape(-1, width).astype(F32))
        dy = spread(own_ref, wqo_ref, True) + spread(got_ref, wqx_ref, True)
        dx, _, _ = norm_back(dy, xhat, rstd, vec_ref[0:1, :])
        out_ref[c * per : (c + 1) * per] = (grad_ref[...] + dx).astype(BF).reshape(per, step, width)


def latent_call(info, latents, grads, own, got, vectors, wqo, wqx):
    half, width = grads[0].shape
    lat_len = latents.shape[1]
    items = 2 * half // lat_len
    z2 = lambda i, info: (0, 0)
    z3 = lambda i, info: (0, 0, 0)
    return pl.pallas_call(
        latent_kernel,
        grid_spec=pltpu.PrefetchScalarGridSpec(
            num_scalar_prefetch=1,
            grid=(1,),
            in_specs=[pl.BlockSpec((items, lat_len, width), lambda i, info: (info[0], 0, 0))]
            + [pl.BlockSpec((half, width), z2)] * 2
            + [pl.BlockSpec(own[0].shape, lambda i, info: (0, 0, 0, 0))] * 4
            + [pl.BlockSpec(vectors.shape, z2), pl.BlockSpec(wqo.shape, z3), pl.BlockSpec(wqx.shape, z3)],
            out_specs=pl.BlockSpec((items, lat_len, width), z3),
        ),
        out_shape=jax.ShapeDtypeStruct((items, lat_len, width), BF),
        compiler_params=params(),
        cost_estimate=cost(4 * items * lat_len * width * 768, 6 * 1024 * 1024),
        name="latent_back",
    )(info, latents, *grads, *own, *got, vectors, wqo, wqx)


def byte_part_kernel(info, dkv_ref, raw_ref, wkv_ref, own_ref, send_ref, sums_ref):
    part = dot_t(dkv_ref[0], wkv_ref[...].reshape(-1, 768))
    xhat, _ = norm_parts(raw_ref[0].astype(F32))
    half = part.shape[0] // 2

    @pl.when(pl.program_id(0) == 0)
    def _():
        sums_ref[...] = jnp.zeros_like(sums_ref)

    sums_ref[0:1, :] += jnp.sum(part * xhat, 0, keepdims=True)
    sums_ref[1:2, :] += jnp.sum(part, 0, keepdims=True)
    low = part.astype(BF)

    @pl.when(info[1] == 0)
    def _():
        own_ref[0] = low[:half]
        send_ref[0] = low[half:]

    @pl.when(info[1] != 0)
    def _():
        own_ref[0] = low[half:]
        send_ref[0] = low[:half]


def byte_part_call(info, dkv, raw, wkv):
    items, keys, _ = dkv.shape
    width = raw.shape[2]
    half = keys // 2
    out = lambda i, info: (i, 0, 0)
    z2 = lambda i, info: (0, 0)
    return pl.pallas_call(
        byte_part_kernel,
        grid_spec=pltpu.PrefetchScalarGridSpec(
            num_scalar_prefetch=1,
            grid=(items,),
            in_specs=[
                pl.BlockSpec((1, keys, 768), out),
                pl.BlockSpec((1, keys, width), out),
                pl.BlockSpec(wkv.shape, lambda i, info: (0, 0, 0)),
            ],
            out_specs=[
                pl.BlockSpec((1, half, width), out),
                pl.BlockSpec((1, half, width), out),
                pl.BlockSpec((2, width), z2),
            ],
        ),
        out_shape=[
            jax.ShapeDtypeStruct((items, half, width), BF),
            jax.ShapeDtypeStruct((items, half, width), BF),
            jax.ShapeDtypeStruct((2, width), F32),
        ],
        compiler_params=params(),
        cost_estimate=cost(items * keys * width * 768 * 2, 6 * 1024 * 1024),
        name="byte_part",
    )(info, dkv, raw, wkv)


def byte_back_kernel(info, part_ref, raw_ref, vec_ref, *refs):
    got_refs, (own_ref, oth_ref) = refs[:-2], refs[-2:]
    half = part_ref.shape[1]
    quarter = half // 2
    got = [ref[k] for ref in got_refs for k in range(ref.shape[0])]
    for k, piece in enumerate(got):
        dy = part_ref[k].astype(F32) + piece.astype(F32)
        xhat, rstd = norm_parts(raw_ref[k].astype(F32))
        dx, _, _ = norm_back(dy, xhat, rstd, vec_ref[2:3, :])
        dx = dx.astype(BF)

        @pl.when(info[0] == 0)
        def _():
            own_ref[k] = dx[:quarter]
            oth_ref[k] = dx[quarter:]

        @pl.when(info[0] != 0)
        def _():
            own_ref[k] = dx[quarter:]
            oth_ref[k] = dx[:quarter]


def byte_back_call(info, part, got, raw, vectors):
    items, half, width = part.shape
    z3 = lambda i, info: (0, 0, 0)
    return pl.pallas_call(
        byte_back_kernel,
        grid_spec=pltpu.PrefetchScalarGridSpec(
            num_scalar_prefetch=1,
            grid=(1,),
            in_specs=[
                pl.BlockSpec((items, half, width), z3),
                pl.BlockSpec((items, half, width), lambda i, info: (0, info[1], 0)),
                pl.BlockSpec(vectors.shape, lambda i, info: (0, 0)),
                *(pl.BlockSpec(piece.shape, z3) for piece in got),
            ],
            out_specs=[pl.BlockSpec((items, half // 2, width), z3)] * 2,
        ),
        out_shape=[jax.ShapeDtypeStruct((items, half // 2, width), BF)] * 2,
        compiler_params=params(),
        cost_estimate=cost(items * half * width * 20, 4 * 1024 * 1024),
        name="byte_back",
    )(info, part, raw, vectors, *got)


def body(
    latents, byte_array, cotangent, patch_count, text_len,
    inner_weight, inner_moment, inner_square,
    output_weight, output_moment, output_square,
    expand_weight, expand_moment, expand_square,
    reduce_weight, reduce_moment, reduce_square,
    expand_bias, bias_moment, bias_square,
    norm_vectors, vector_moment, vector_square,
):
    item_count, lat_len, width = latents.shape
    keys = byte_array.shape[1]
    items = item_count // 2
    n = lax.axis_size("dp")
    head = lax.axis_index("head")
    core, xside = head & 1, head >> 1
    true_rows = keys // lax.axis_size("head")
    pad_rows = -(-true_rows // 32) * 32
    pad_keys = 4 * pad_rows
    quick = n == 8
    place = lax.axis_index("dp") if quick else jnp.int32(0)
    info = jnp.stack([core, xside, jnp.int32(true_rows), jnp.int32(items), place]).astype(jnp.int32)
    half_items = items // 2

    low_inner = inner_weight.astype(BF)
    wq, wk, wv = low_inner[0], low_inner[1], low_inner[2]
    wo = output_weight.T.astype(BF)
    pack = jnp.concatenate(
        [wk[:, :128], wv[:, :128], wk[:, 128:], wv[:, 128:], wq[:, :128], wq[:, 128:], wo[:, 128:], wo[:, :128]], 1
    )
    ff_pack = jnp.concatenate([expand_weight.astype(BF), reduce_weight.T.astype(BF)], 1)
    normalise = lambda c, byte_array: norm_call(
        c * half_items, items, info, byte_array, latents, norm_vectors, half_items, pad_keys
    )
    flip = lambda value: swap(value, "head", 1)
    over = lambda value, mask: swap(value, "dp", mask)
    grouped = lambda p: [flip(jnp.concatenate([p[k] for k in group], 0)) for group in GROUPS]
    if quick:
        g = {0: pack, 4: over(pack, 4), 2: over(pack, 2), 1: over(pack, 1)}
        norm0 = normalise(0, byte_array)
        g[4], g[2], g[1], *norm0 = tie(g[4], g[2], g[1], *norm0)
        g[6], g[5], g[3] = over(g[4], 2), over(g[4], 1), over(g[2], 1)
        g[6], g[5], g[3], byte_later, ff_pack = tie(g[6], g[5], g[3], byte_array, ff_pack)
        f = {0: ff_pack, 4: over(ff_pack, 4), 2: over(ff_pack, 2), 1: over(ff_pack, 1)}
        g[7] = over(g[6], 1)
        norm1 = normalise(1, byte_later)
        g[7], f[4], f[2], f[1], *norm1 = tie(g[7], f[4], f[2], f[1], *norm1)
        f[6], f[5], f[3] = over(f[4], 2), over(f[4], 1), over(f[2], 1)
        pieces = [g[k] for k in range(8)] + grouped(g)
    else:
        norm0, norm1 = normalise(0, byte_array), normalise(1, byte_array)
        blocks = lax.all_gather(pack, "dp", axis=0, tiled=True).reshape(8, width // 8, 768)
        g = [blocks[k] for k in range(8)]
        pieces = g + grouped(g)
        blocks = lax.all_gather(ff_pack, "dp", axis=0, tiled=True).reshape(8, width // 8, 1536)
        f = [blocks[k] for k in range(8)]
    norm, normt, raw, lat_norm, lat_normt = zip(norm0, norm1)
    bias_other = flip(expand_bias)

    crossed = swap(jnp.concatenate([g[k][:, 384:] for k in range(8)], 0), "head", 2)

    attend = lambda c, weights: attn_fwd_call(
        c * half_items, info, patch_count, text_len, norm[c], lat_norm[c], weights
    )
    mixed0, *kept0, wkv, wqo = attend(0, pieces)
    got0 = swap(mixed0, "head", 2)
    if quick:
        first_flip = flip(jnp.concatenate([f[k] for k in GROUPS[0]], 0))
        wkv, f[6], f[5], f[3], first_flip, bias_other, crossed = tie(
            wkv, f[6], f[5], f[3], first_flip, bias_other, crossed
        )
        f[7] = over(f[6], 1)
        second_flip = flip(jnp.concatenate([f[k] for k in GROUPS[1]], 0))
    crossed = [crossed, flip(crossed)]
    mixed1, *kept1 = attend(1, [wkv, wqo])
    mixed1, got0, crossed[1] = tie(mixed1, got0, crossed[1])
    got1 = swap(mixed1, "head", 2)
    if quick:
        mixed1, second_flip, f[7] = tie(mixed1, second_flip, f[7])
        ff_pieces = [f[k] for k in range(8)] + [first_flip, second_flip, flip(f[7])]
    else:
        ff_pieces = f + grouped(f)

    bias_both = jnp.stack([expand_bias, bias_other])
    feed = lambda c, mixed, got, weights: ff_core_call(
        c, info, latents, cotangent, mixed, got, norm_vectors, bias_both, wqo, weights
    )
    res0, *ff0, npart0, cot_sum0, ff_own, ff_oth, wqx = feed(0, mixed0, got0, [*ff_pieces, *crossed])
    npart0, got1 = tie(npart0, got1)
    ngot0 = swap(npart0, "head", 2)
    res1, *ff1, npart1, cot_sum1 = feed(1, mixed1, got1, [ff_own, ff_oth, wqx])
    npart1, ngot0, pre1 = tie(npart1, ngot0, ff1[3])
    ff1[3] = pre1
    ngot1 = swap(npart1, "head", 2)
    flat = (8, 2 * (width // 8), 768)
    g_oth, bias_oth = ff_grad_call(1, info, [ff0, ff1])
    g_oth, pre1 = tie(g_oth, pre1)
    ff1[3] = pre1
    g_got = flip(g_oth.reshape(flat))
    g_own, bias_own, mlp_part = ff_grad_call(0, info, [ff0, ff1], [ff_own, ff_oth])
    g_own, ngot0, ngot1, g_got = tie(g_own, ngot0, ngot1, g_got)
    bias_own = bias_own + flip(bias_oth)
    g_own = g_own.reshape(flat)
    t75 = plus(g_own[0:2], g_got[0:2])

    attend_back = lambda c, res, npart, ngot, mixed, kept, grads: attn_bwd_call(
        c * half_items, items, info, cotangent, latents, res, npart, ngot,
        norm_vectors, mixed, *kept, normt[c], lat_normt[c], wqo, grads
    )
    res0, ngot0, t75, bias_own, mlp_part = tie(res0, ngot0, t75, bias_own, mlp_part)
    mlp_got = swap(mlp_part, "head", 2)
    if quick:
        y75 = over(t75, 1)
    rgrad0, dq0, dkv0, sums0, *grads = attend_back(0, res0, npart0, ngot0, mixed0, kept0, None)
    bown0, bsend0, bsums0 = byte_part_call(info, dkv0, raw[0], wkv)
    res1, bsend0, mlp_got = tie(res1, bsend0, mlp_got)
    bgot00 = swap(bsend0[:1], "head", 2)
    if quick:
        res1, y75 = tie(res1, y75)
        t64 = plus3(g_own[4:6], g_got[4:6], y75)
        z6 = over(t64[0], 2)
        y31 = over(plus(g_own[2:4], g_got[2:4]), 1)
    rgrad1, dq1, dkv1, sums1, g_attn, g_attn_oth = attend_back(1, res1, npart1, ngot1, mixed1, kept1, grads)
    g_attn_oth, bgot00 = tie(g_attn_oth, bgot00)
    if quick:
        g_attn_oth, z6, y31 = tie(g_attn_oth, z6, y31)
        y_last = y31
    else:
        g_ff = jnp.stack([g_own[ORDER.index(k)] for k in range(8)]).astype(F32)
        g_ff = g_ff + jnp.stack([g_got[ORDER.index(k)] for k in range(8)]).astype(F32)
        g_ff = g_ff.reshape(8, 2, width // 8, 768).swapaxes(0, 1).reshape(2, width, 768)
        g_ff = lax.psum_scatter(g_ff, "dp", scatter_dimension=1, tiled=True).reshape(-1, 768)
    u = g_attn.reshape(8, width // 8, 768)
    v = flip(g_attn_oth).reshape(8, width // 8, 768)
    bgot01 = swap(bsend0[1:], "head", 2)
    lgot0 = swap(dq0, "head", 2)
    lgot1 = swap(dq1, "head", 2)
    u75 = plus(u[0:2], v[0:2])

    if quick:
        y75 = over(u75, 1)
        y31 = over(plus(u[2:4], v[2:4]), 1)
        u75, z6, y_last = tie(u75, z6, y_last)
        z4 = over(plus(t64[1], z6), 4)
        z2 = over(plus3(g_own[6], g_got[6], y_last[0]), 2)
    dkv1, mlp_got, u75 = tie(dkv1, mlp_got, u75)
    bown1, bsend1, bsums1 = byte_part_call(info, dkv1, raw[1], wkv)
    if quick:
        bsend1, y75, bgot01 = tie(bsend1, y75, bgot01)
        u64 = plus3(u[4:6], v[4:6], y75)
        z6 = over(u64[0], 2)
    bgot10, bgot11 = swap(bsend1[:1], "head", 2), swap(bsend1[1:], "head", 2)

    residual = jnp.concatenate([res0, res1], 0)
    block_mine = residual + (mlp_part.astype(F32) + mlp_got.astype(F32)) + norm_vectors[6]
    block_mine = block_mine.astype(BF).reshape(items, lat_len, width)
    block_flip = flip(block_mine)

    byte_side = lambda c, own, got: byte_back_call(info, own, got, raw[c], norm_vectors)
    side0 = list(byte_side(0, bown0, [bgot00, bgot01]))
    if quick:
        block_flip, z6, y31, z4, z2, lgot0, lgot1 = tie(block_flip, z6, y31, z4, z2, lgot0, lgot1)
        g_ff = sum(value.astype(F32) for value in (g_own[7], g_got[7], y_last[1], z2, z4))
        z4 = over(plus(u64[1], z6), 4)
        z2 = over(plus3(u[6], v[6], y31[0]), 2)
    block_output = pair_call(info, [block_mine], [block_flip], lat_len)
    lat_mine = latent_call(
        info, latents, [rgrad0, rgrad1], [dq0, dq1], [lgot0, lgot1], norm_vectors, wqo, wqx
    )
    if quick:
        block_output, z4, z2, side0[0], ff_squares, bgot10, lat_mine = tie(
            block_output, z4, z2, side0[0], jnp.sum(g_ff * g_ff), bgot10, lat_mine
        )
        g_attn = sum(value.astype(F32) for value in (u[7], v[7], y31[1], z2, z4))
    else:
        g_attn = u.astype(F32) + v.astype(F32)
        g_attn = jnp.concatenate([g_attn[ORDER.index(k)] for k in range(8)], 0)
        g_attn = lax.psum_scatter(g_attn, "dp", scatter_dimension=0, tiled=True)
    side1 = byte_side(1, bown1, [bgot10, bgot11])
    once = (xside == 0).astype(F32)
    squares = (ff_squares if quick else jnp.sum(g_ff * g_ff)) + jnp.sum(g_attn * g_attn)
    sums = sums0 + sums1
    vec = jnp.concatenate([sums[2:4], bsums0 + bsums1, sums[0:2] * once, (cot_sum0 + cot_sum1) * once], 0)
    load = jnp.concatenate([vec, bias_own, jnp.full((1, width), squares, F32)], 0)
    lat_flip = flip(lat_mine)
    beside = [
        lambda: pair_call(info, [lat_mine], [lat_flip], lat_len),
        lambda: side1,
        lambda: pair_call(info, [side0[0], outs[1][0]], [flip(side0[1]), flip(outs[1][1])], true_rows),
    ]
    outs = []
    mask = n // 2
    while mask:
        hop = over(load, mask)
        if beside:
            hop, out = lax.optimization_barrier((hop, beside.pop(0)()))
            outs.append(out)
        load = load + hop
        mask //= 2
    latent_gradient, _, byte_gradient = outs
    bias_sum = load[7:8]
    squares = load[8:9] + jnp.sum(bias_sum * bias_sum)
    load = jnp.concatenate([load[:7], squares], 0)
    load = load + swap(load, "head", 1)
    load = load + swap(load, "head", 2)

    *news, grad_norm = adam_call(
        load,
        g_attn,
        g_ff,
        [
            inner_weight, inner_moment, inner_square, output_weight, output_moment, output_square,
            expand_weight, expand_moment, expand_square, reduce_weight.T, reduce_moment.T, reduce_square.T,
            norm_vectors, vector_moment, vector_square,
        ],
    )
    factor = CLIP_RATE * math.sqrt(4 * D * D + 2 * D * FF + FF + 7 * D) / grad_norm[0, 0]
    bias_new = adamw(expand_bias, bias_moment, bias_square, factor * bias_sum[0], 0.3, 0.0)
    news[9:12] = [new.T for new in news[9:12]]
    return (
        block_output, latent_gradient, byte_gradient, *news[:12], *bias_new, *news[12:], grad_norm[0, 0]
    )


def solution(mesh):
    rows, cols = P("dp", "head"), P("head", "dp")
    inner, items = P(None, "dp", "head"), P("dp", None, None)
    weights = (inner,) * 3 + (cols,) * 3 + (rows,) * 3 + (cols,) * 3 + (P("head"),) * 3 + (P(),) * 3
    return jax.shard_map(
        body,
        mesh=mesh,
        in_specs=(items, items, items, P("dp"), P("dp")) + weights,
        out_specs=(items, items, P("dp", "head", None)) + weights + (P(),),
        check_vma=False,
    )
```

```python
import functools
import math

import jax
import jax.numpy as jnp
from jax import lax
from jax.experimental import pallas as pl
from jax.experimental.pallas import tpu as pltpu
from jax.sharding import PartitionSpec as P

D = 768
HEAD_DIM = 64
FF = 3072
PATCHES = 576
STEP = 5

NEG_FILL = -1000000000.0
BETA = 0.5
ADAM_EPS = 1e-08
DECAY = 0.01
CLIP_RATE = 0.01
LN_EPS = 1e-05
SCALE = 1.0 / math.sqrt(HEAD_DIM)
BF = jnp.bfloat16
F32 = jnp.float32
VMEM_LIMIT = 20 * 1024 * 1024


def dot(a, b):
    return lax.dot_general(a, b, (((1,), (0,)), ((), ())), preferred_element_type=F32)


def dot_t(a, b):
    return lax.dot_general(a, b, (((1,), (1,)), ((), ())), preferred_element_type=F32)


def norm_parts(rows):
    centred = rows - jnp.mean(rows, -1, keepdims=True)
    rstd = lax.rsqrt(jnp.mean(centred * centred, -1, keepdims=True) + LN_EPS)
    return centred * rstd, rstd


def norm_back(dy, xhat, rstd, gain):
    scaled = dy * gain
    first = jnp.mean(scaled, -1, keepdims=True)
    second = jnp.mean(scaled * xhat, -1, keepdims=True)
    dx = rstd * (scaled - first - xhat * second)
    return dx, jnp.sum(dy * xhat, 0, keepdims=True), jnp.sum(dy, 0, keepdims=True)


def swap(value, axis, mask):
    size = lax.axis_size(axis)
    return lax.ppermute(value, axis, [(i, i ^ mask) for i in range(size)])


def tie(*values):
    return lax.optimization_barrier(tuple(values))


def plus(*values):
    return sum(value.astype(F32) for value in values).astype(BF)


def adamw(weight, moment, square, gradient, rate, decay_rate):
    moment_new = BETA * moment + (1.0 - BETA) * gradient
    square_new = BETA * square + (1.0 - BETA) * gradient * gradient
    correction = 1.0 - BETA**STEP
    step_dir = moment_new * (1.0 / correction) / (jnp.sqrt(square_new * (1.0 / correction)) + ADAM_EPS)
    return (weight - rate * (step_dir + decay_rate * weight), moment_new, square_new)


def params(**kw):
    return pltpu.CompilerParams(vmem_limit_bytes=VMEM_LIMIT, **kw)


def cost(flops, nbytes, trans=0):
    return pl.CostEstimate(flops=flops, bytes_accessed=nbytes, transcendentals=trans)


GROUPS = ((0, 4, 2, 1), (6, 5, 3), (7,))


def assemble(info, parts, outs, splits):
    rows = parts[0].shape[0]
    blocks = [(k, 0, parts[k], 0) for k in range(8)]
    for part, group in zip(parts[8:], GROUPS):
        blocks += [(k, 1, part, i * rows) for i, k in enumerate(group)]
    for k, c, part, first in blocks:
        for out, start, stop, offset in splits[c]:
            outs[out][info[4] ^ k, :, offset : offset + stop - start] = part[first : first + rows, start:stop]


ORDER = (7, 5, 3, 1, 6, 4, 2, 0)
FF_ORDERS = ((7, 3, 5, 1, 6, 2, 4, 0), (7, 3, 6, 2, 5, 1, 4, 0))


def pair_kernel(chunks, info, *refs):
    out = refs[-1]
    rows = out.shape[1]
    per = refs[0].shape[0]
    for side in range(2):
        first = (info[0] ^ side) * (chunks * per)
        for c in range(chunks):
            ref = refs[side * chunks + c]
            for k in range(per):
                out[first + c * per + k] = ref[k, :rows, :]


def pair_call(info, own, other, rows):
    per, _, width = own[0].shape
    chunks = len(own)
    return pl.pallas_call(
        functools.partial(pair_kernel, chunks),
        grid_spec=pltpu.PrefetchScalarGridSpec(
            num_scalar_prefetch=1,
            grid=(1,),
            in_specs=[pl.BlockSpec(own[0].shape, lambda i, info: (0, 0, 0))] * (2 * chunks),
            out_specs=pl.BlockSpec((2 * chunks * per, rows, width), lambda i, info: (0, 0, 0)),
        ),
        out_shape=jax.ShapeDtypeStruct((2 * chunks * per, rows, width), BF),
        compiler_params=params(),
        cost_estimate=cost(1, 4 * chunks * per * rows * width * 2),
        name="pair",
    )(info, *own, *other)


def collect_kernel(count, info, *refs):
    terms, (sums0, sums1, bytes0, bytes1, cot0, cot1, bias, squares, grad_ref, load_ref) = refs[:count], refs[count:]
    grad = sum(ref[...].astype(F32) for ref in terms)
    grad_ref[...] = grad
    once = jnp.where(info[1] == 0, 1.0, 0.0)
    sums = sums0[...] + sums1[...]
    load_ref[0:2, :] = sums[2:4]
    load_ref[2:4, :] = bytes0[...] + bytes1[...]
    load_ref[4:6, :] = sums[0:2] * once
    load_ref[6:7, :] = (cot0[...] + cot1[...]) * once
    load_ref[7:8, :] = bias[...]
    total = jnp.sum(jnp.sum(grad * grad, 0, keepdims=True), 1, keepdims=True) + squares[...]
    load_ref[8:9, :] = jnp.broadcast_to(total, (1, load_ref.shape[1]))


def collect_call(info, terms, small):
    rows, width = terms[0].shape
    whole = lambda i, info: (0, 0)
    return pl.pallas_call(
        functools.partial(collect_kernel, len(terms)),
        grid_spec=pltpu.PrefetchScalarGridSpec(
            num_scalar_prefetch=1,
            grid=(1,),
            in_specs=[pl.BlockSpec(x.shape, whole) for x in (*terms, *small)],
            out_specs=[pl.BlockSpec((rows, width), whole), pl.BlockSpec((9, width), whole)],
        ),
        out_shape=[jax.ShapeDtypeStruct((rows, width), F32), jax.ShapeDtypeStruct((9, width), F32)],
        compiler_params=params(),
        cost_estimate=cost(1, 16 * rows * width),
        name="collect",
    )(info, *terms, *small)


def adam_kernel(load_ref, attn_ref, ff_ref, *refs):
    inner, output, expand, reduce, vector = (refs[3 * k : 3 * k + 3] for k in range(5))
    outs = refs[15:]
    load = load_ref[...]
    vectors = load[0:7]
    total = load[7:8, 0:1] + jnp.sum(jnp.sum(vectors * vectors, 0, keepdims=True), 1, keepdims=True)
    norm = jnp.sqrt(total)
    outs[15][...] = norm
    factor = CLIP_RATE * math.sqrt(4 * D * D + 2 * D * FF + FF + 7 * D) / norm

    def update(which, at, grad, rate, decay_rate):
        state = refs[3 * which : 3 * which + 3]
        for ref, new in zip(
            outs[3 * which : 3 * which + 3],
            adamw(*(ref[at] for ref in state), factor * grad, rate, decay_rate),
        ):
            ref[at] = new

    low, high = slice(0, 128), slice(128, 192)
    every = slice(None)
    for matrix, first, second in ((0, 384, 512), (1, 0, 256), (2, 128, 320)):
        update(0, (matrix, every, low), attn_ref[:, first : first + 128], 0.03, DECAY)
        update(0, (matrix, every, high), attn_ref[:, second : second + 64], 0.03, DECAY)
    update(1, (low, every), attn_ref[:, 640:768].T, 0.3, DECAY)
    update(1, (high, every), attn_ref[:, 512:640].T[64:128], 0.3, DECAY)
    rows = expand[0].shape[0]
    update(2, Ellipsis, ff_ref[0:rows, :], 0.03, DECAY)
    update(3, Ellipsis, ff_ref[rows : 2 * rows, :], 0.015, DECAY)
    update(4, Ellipsis, vectors, 0.3, 0.0)


def adam_call(load, attn, ff, state):
    shapes = [jax.ShapeDtypeStruct(x.shape, F32) for x in state] + [jax.ShapeDtypeStruct((1, 1), F32)]
    return pl.pallas_call(
        adam_kernel,
        out_shape=shapes,
        compiler_params=params(),
        cost_estimate=cost(1, sum(x.size for x in state) * 4 * 2),
        name="adam",
    )(load, attn, ff, *state)


def norm_kernel(info, byte_ref, lat_ref, vec_ref, norm_ref, normt_ref, raw_ref, lat_norm_ref, lat_normt_ref, scr):
    groups, true_rows, pad_rows = 4, byte_ref.shape[1] // 4, norm_ref.shape[1] // 4
    keys = byte_ref.shape[1]
    scr[pl.ds(0, keys), :] = byte_ref[0].astype(F32)
    gain, bias = vec_ref[2:3, :], vec_ref[3:4, :]
    keep = lax.broadcasted_iota(jnp.int32, (pad_rows, 1), 0) < true_rows
    for g in range(groups):
        rows = jnp.where(keep, scr[pl.ds(g * true_rows, pad_rows), :], 0.0)
        xhat, _ = norm_parts(rows)
        normed = jnp.where(keep, xhat * gain + bias, 0.0)
        here = pl.ds(g * pad_rows, pad_rows)
        raw_ref[0, here, :] = rows.astype(BF)
        norm_ref[0, here, :] = normed.astype(BF)
    normt_ref[0] = norm_ref[0].T
    xhat, _ = norm_parts(lat_ref[0].astype(F32))
    lat_norm = (xhat * vec_ref[0:1, :] + vec_ref[1:2, :]).astype(BF)
    lat_norm_ref[0] = lat_norm
    lat_normt_ref[0] = lat_norm.T


def norm_call(first_item, all_items, info, byte_array, latents, vectors, items, pad_keys):
    _, keys, width = byte_array.shape
    lat_len = latents.shape[1]
    here = lambda i, info: (info[0] * all_items + first_item + i, 0, 0)
    out = lambda i, info: (i, 0, 0)
    return pl.pallas_call(
        norm_kernel,
        grid_spec=pltpu.PrefetchScalarGridSpec(
            num_scalar_prefetch=1,
            grid=(items,),
            in_specs=[
                pl.BlockSpec((1, keys, width), here),
                pl.BlockSpec((1, lat_len, width), here),
                pl.BlockSpec(vectors.shape, lambda i, info: (0, 0)),
            ],
            out_specs=[
                pl.BlockSpec((1, pad_keys, width), out),
                pl.BlockSpec((1, width, pad_keys), out),
                pl.BlockSpec((1, pad_keys, width), out),
                pl.BlockSpec((1, lat_len, width), out),
                pl.BlockSpec((1, width, lat_len), out),
            ],
            scratch_shapes=[pltpu.VMEM((keys + 40, width), F32)],
        ),
        out_shape=[
            jax.ShapeDtypeStruct((items, pad_keys, width), BF),
            jax.ShapeDtypeStruct((items, width, pad_keys), BF),
            jax.ShapeDtypeStruct((items, pad_keys, width), BF),
            jax.ShapeDtypeStruct((items, lat_len, width), BF),
            jax.ShapeDtypeStruct((items, width, lat_len), BF),
        ],
        compiler_params=params(),
        cost_estimate=cost(items * keys * width * 20, items * keys * width * 8),
        name="norms",
    )(info, byte_array, latents, vectors)


SPLITS = (((0, 0, 384, 0), (1, 384, 768, 0)), ((0, 0, 384, 384), (1, 384, 768, 384)))


def attn_fwd_kernel(first_item, info, count_ref, text_ref, norm_ref, lat_ref, *refs):
    if first_item == 0:
        pieces, (mixed_ref, pt_ref, kv_ref, q_ref, wkv_ref, wqo_ref) = refs[:11], refs[11:]

        @pl.when(pl.program_id(0) == 0)
        def _():
            assemble(info, pieces, (wkv_ref, wqo_ref), SPLITS)

    else:
        wkv_ref, wqo_ref, mixed_ref, pt_ref, kv_ref, q_ref = refs
    wkv = wkv_ref[...].reshape(-1, 768)
    columns = lambda start, stop: wqo_ref[:, :, start:stop].reshape(-1, stop - start)
    item = info[0] * info[3] + first_item + pl.program_id(0)
    patches, texts = count_ref[item], text_ref[item]
    keys = norm_ref.shape[1]
    pad_rows = keys // 4
    true_rows = info[2]
    row = lax.broadcasted_iota(jnp.int32, (keys, 128), 0)
    group = sum(((row >= pad_rows * g).astype(jnp.int32) for g in range(1, 4)))
    inner = row - group * pad_rows
    slot = inner + group * true_rows
    valid = ((slot < PATCHES) & (slot < patches)) | ((slot >= PATCHES) & (slot - PATCHES < texts))
    valid = valid & (inner < true_rows)
    lane_lo = lax.broadcasted_iota(jnp.int32, (128, 128), 1) < HEAD_DIM
    row_lo = lax.broadcasted_iota(jnp.int32, (128, 128), 0) < HEAD_DIM
    kv_all = dot(norm_ref[0], wkv).astype(BF)
    kv_ref[0] = kv_all
    lat_norm = lat_ref[0]
    for p in range(2):
        kv = kv_all[:, p * 384 : (p + 1) * 384]
        base = p * 384
        q = dot(lat_norm, columns(base, base + 256)) * SCALE
        q01, q2 = q[:, :128], jnp.where(lane_lo, q[:, 128:], 0.0).astype(BF)
        q_ref[0, p, :, 0:128] = q01.astype(BF)
        q_ref[0, p, :, 128:256] = q2
        stacked = jnp.concatenate([jnp.where(lane_lo, q01, 0.0), jnp.where(lane_lo, 0.0, q01)], 0).astype(BF)
        first = dot_t(kv[:, 0:128], stacked)
        second = dot_t(kv[:, 256:384], q2)
        pieces = []
        for piece in (first[:, 0:128], first[:, 128:256], second):
            piece = jnp.where(valid, piece, NEG_FILL)
            top = jnp.max(piece, 0, keepdims=True)
            expo = jnp.exp(piece - top)
            pieces.append(expo * (1.0 / jnp.sum(expo, 0, keepdims=True)))
        for h in range(3):
            pt_ref[0, p, :, h * 128 : (h + 1) * 128] = pieces[h]
        low01 = jnp.concatenate([pieces[0].astype(BF), pieces[1].astype(BF)], 1)
        o01 = dot(kv[:, 128:256].T, low01)
        o2 = dot(kv[:, 256:384].T, pieces[2].astype(BF))
        mixed_ref[0, p, 0:64, :] = o2[64:128].astype(BF)
        mixed_ref[0, p, 64:192, :] = jnp.where(row_lo, o01[:, 0:128], o01[:, 128:256]).astype(BF)


def attn_fwd_call(first_item, info, counts, texts, norm, lat_norm, weights):
    items, keys, width = norm.shape
    lat_len = lat_norm.shape[1]
    out3 = lambda i, *_: (i, 0, 0)
    out4 = lambda i, *_: (i, 0, 0, 0)
    given = [pl.BlockSpec(w.shape, lambda i, *_, d=w.ndim: (0,) * d) for w in weights]
    made = [pl.BlockSpec((8, width // 8, 768), lambda i, *_: (0, 0, 0))] * (2 * (first_item == 0))
    flops = items * 2 * (keys * width * 768 + lat_len * width * 768 + 4 * keys * lat_len * 384)
    return pl.pallas_call(
        functools.partial(attn_fwd_kernel, first_item),
        grid_spec=pltpu.PrefetchScalarGridSpec(
            num_scalar_prefetch=3,
            grid=(items,),
            in_specs=[
                pl.BlockSpec((1, keys, width), out3),
                pl.BlockSpec((1, lat_len, width), out3),
                *given,
            ],
            out_specs=[
                pl.BlockSpec((1, 2, 192, lat_len), out4),
                pl.BlockSpec((1, 2, keys, 384), out4),
                pl.BlockSpec((1, keys, 768), out3),
                pl.BlockSpec((1, 2, lat_len, 256), out4),
                *made,
            ],
        ),
        out_shape=[
            jax.ShapeDtypeStruct((items, 2, 192, lat_len), BF),
            jax.ShapeDtypeStruct((items, 2, keys, 384), F32),
            jax.ShapeDtypeStruct((items, keys, 768), BF),
            jax.ShapeDtypeStruct((items, 2, lat_len, 256), BF),
        ]
        + [jax.ShapeDtypeStruct((8, width // 8, 768), BF)] * len(made),
        compiler_params=params(),
        cost_estimate=cost(flops, 8 * 1024 * 1024, items * keys * 768),
        name="attn_fwd",
    )(info, counts, texts, norm, lat_norm, *weights)


def spread(mixed_ref, w_ref, queries):
    zeros = jnp.zeros((64, mixed_ref.shape[3]), BF)
    total = []
    for item in range(mixed_ref.shape[0]):
        rows = None
        for p in range(2):
            mixed = mixed_ref[item, p]
            parts = (mixed[0:128], mixed[128:192], zeros) if queries else (zeros, mixed[0:64], mixed[64:192])
            first = p * 384 + 128 * (not queries)
            columns = w_ref[:, :, first : first + 256].reshape(-1, 256)
            add = dot_t(jnp.concatenate(parts, 0).T, columns)
            rows = add if rows is None else rows + add
        total.append(rows)
    return jnp.concatenate(total, 0)


def ff_core_kernel(chunk, info, lat_ref, cot_ref, own_ref, got_ref, vec_ref, bias_ref, wqo_ref, *refs):
    if chunk == 0:
        pieces, crossed = refs[:11], refs[11:13]
        res_ref, normt_ref, cott_ref, hidden_ref, pre_ref, part_ref, cot_sum_ref, *weights, wqx_ref = refs[13:]
        assemble(info, pieces, weights, (((0, 0, 1536, 0),), ((1, 0, 1536, 0),)))
        rows = wqx_ref.shape[1]
        for k in range(8):
            for c in range(2):
                wqx_ref[info[4] ^ k, :, 384 * c : 384 * (c + 1)] = crossed[c][k * rows : (k + 1) * rows, :]
    else:
        weights, wqx_ref = refs[:2], refs[2]
        res_ref, normt_ref, cott_ref, hidden_ref, pre_ref, part_ref, cot_sum_ref = refs[3:]
    width = vec_ref.shape[1]
    flat = lambda ref: ref[...].reshape(-1, width).astype(F32)
    residual = flat(lat_ref) + (spread(own_ref, wqo_ref, False) + spread(got_ref, wqx_ref, False))
    res_ref[...] = residual
    xhat, _ = norm_parts(residual)
    normed = (xhat * vec_ref[4:5, :] + vec_ref[5:6, :]).astype(BF)
    cot = cot_ref[...].reshape(-1, width)
    total = None
    step = 256
    for p, w_ref in enumerate(weights):
        columns = lambda start: w_ref[:, :, start : start + step].reshape(-1, step)
        for j in range(768 // step):
            cols = slice(j * step, (j + 1) * step)
            w1 = columns(j * step)
            pre = dot(normed, w1) + bias_ref[p : p + 1, cols]
            back = dot(cot, columns(768 + j * step))
            cdf = 0.5 + 0.5 * lax.erf(pre * math.sqrt(0.5))
            pdf = jnp.exp(pre * pre * -0.5) * (1.0 / math.sqrt(2.0 * math.pi))
            hidden_ref[p, :, cols] = (pre * cdf).astype(BF)
            grad = (back * (cdf + pre * pdf)).astype(BF)
            pre_ref[p, :, cols] = grad
            add = dot_t(grad, w1)
            total = add if total is None else total + add
    part_ref[...] = total.astype(BF)
    normt_ref[...] = normed.T
    cott_ref[...] = cot.T
    cot_sum_ref[...] = jnp.sum(cot.astype(F32), 0, keepdims=True)


def ff_core_call(chunk, info, latents, cotangent, own, got, vectors, bias, wqo, weights):
    items = own.shape[0]
    _, lat_len, width = latents.shape
    rows = items * lat_len
    half = lambda i, info: (2 * info[0] + chunk, 0, 0)
    z3 = lambda i, info: (0, 0, 0)
    z4 = lambda i, info: (0, 0, 0, 0)
    z2 = lambda i, info: (0, 0)
    given = [pl.BlockSpec(w.shape, lambda i, info, d=w.ndim: (0,) * d) for w in weights]
    lanes = (1536, 1536, 768) if chunk == 0 else ()
    made = [pl.BlockSpec((8, width // 8, cols), z3) for cols in lanes]
    return pl.pallas_call(
        functools.partial(ff_core_kernel, chunk),
        grid_spec=pltpu.PrefetchScalarGridSpec(
            num_scalar_prefetch=1,
            grid=(1,),
            in_specs=[
                pl.BlockSpec((items, lat_len, width), half),
                pl.BlockSpec((items, lat_len, width), half),
                pl.BlockSpec(own.shape, z4),
                pl.BlockSpec(got.shape, z4),
                pl.BlockSpec(vectors.shape, z2),
                pl.BlockSpec(bias.shape, z2),
                pl.BlockSpec(wqo.shape, z3),
                *given,
            ],
            out_specs=[
                pl.BlockSpec((rows, width), z2),
                pl.BlockSpec((width, rows), z2),
                pl.BlockSpec((width, rows), z2),
                pl.BlockSpec((2, rows, 768), z3),
                pl.BlockSpec((2, rows, 768), z3),
                pl.BlockSpec((rows, width), z2),
                pl.BlockSpec((1, width), z2),
                *made,
            ],
        ),
        out_shape=[
            jax.ShapeDtypeStruct((rows, width), F32),
            jax.ShapeDtypeStruct((width, rows), BF),
            jax.ShapeDtypeStruct((width, rows), BF),
            jax.ShapeDtypeStruct((2, rows, 768), BF),
            jax.ShapeDtypeStruct((2, rows, 768), BF),
            jax.ShapeDtypeStruct((rows, width), BF),
            jax.ShapeDtypeStruct((1, width), F32),
        ]
        + [jax.ShapeDtypeStruct((8, width // 8, cols), BF) for cols in lanes],
        compiler_params=params(),
        cost_estimate=cost(6 * rows * width * 1536, 8 * 1024 * 1024, 2 * rows * 1536),
        name="ff_core",
    )(info, latents, cotangent, own, got, vectors, bias, wqo, *weights)


def relative_rows(info, ref, order):
    block = ref.shape[0] // 8
    return jnp.concatenate([ref[pl.ds(pl.multiple_of((info[4] ^ k) * block, 16), block), :] for k in order], 0)


def ff_grad_kernel(p, info, *refs):
    chunks, refs = (refs[:4], refs[4:8]), refs[8:]
    grad_ref, bias_ref = refs[-4:-2] if p == 0 else refs
    expand, reduce, bias = 0.0, 0.0, 0.0
    for normt_ref, cott_ref, hidden_ref, pre_ref in chunks:
        hidden, pre = hidden_ref[p], pre_ref[p]
        expand += dot(relative_rows(info, normt_ref, FF_ORDERS[0]), pre)
        reduce += dot(relative_rows(info, cott_ref, FF_ORDERS[1]), hidden)
        bias += jnp.sum(pre.astype(F32), 0, keepdims=True)
    grad_ref[0] = expand.astype(BF).reshape(8, -1, expand.shape[1])
    grad_ref[1] = reduce.astype(BF).reshape(8, -1, reduce.shape[1])
    bias_ref[...] = bias
    if p == 0:
        w_refs, (part_ref, acc) = refs[:2], refs[-2:]
        j = pl.program_id(0)
        rows = chunks[0][0].shape[1]
        for c, chunk in enumerate(chunks):
            here = pl.ds(c * rows, rows)
            add = sum(dot_t(chunk[2][q], w_ref[...].reshape(-1, w_ref.shape[2])) for q, w_ref in enumerate(w_refs))
            acc[here, :] = jnp.where(j == 0, 0.0, acc[here, :]) + add

        @pl.when(j == pl.num_programs(0) - 1)
        def _():
            part_ref[...] = acc[...].astype(BF)


def ff_grad_call(p, info, chunks, weights=()):
    width, rows = chunks[0][0].shape
    step = 256
    n = 768 // step
    z2 = lambda j, info: (0, 0)
    per_chunk = [
        pl.BlockSpec((width, rows), z2),
        pl.BlockSpec((width, rows), z2),
        pl.BlockSpec((2, rows, step), lambda j, info: (0, 0, j)),
        pl.BlockSpec((2, rows, step), lambda j, info: (0, 0, j)),
    ]
    specs = [
        pl.BlockSpec((2, 8, width // 8, step), lambda j, info: (0, 0, 0, j)),
        pl.BlockSpec((1, step), lambda j, info: (0, j)),
        pl.BlockSpec((2 * rows, width), z2),
    ]
    shapes = [
        jax.ShapeDtypeStruct((2, 8, width // 8, 768), BF),
        jax.ShapeDtypeStruct((1, 768), F32),
        jax.ShapeDtypeStruct((2 * rows, width), BF),
    ]
    count = 3 if p == 0 else 2
    return pl.pallas_call(
        functools.partial(ff_grad_kernel, p),
        grid_spec=pltpu.PrefetchScalarGridSpec(
            num_scalar_prefetch=1,
            grid=(n,),
            in_specs=per_chunk * 2
            + [pl.BlockSpec((8, width // 8, step), lambda j, info: (0, 0, n + j))] * len(weights),
            out_specs=specs[:count],
            scratch_shapes=[pltpu.VMEM((2 * rows, width), F32)] * (p == 0),
        ),
        out_shape=shapes[:count],
        compiler_params=params(),
        cost_estimate=cost((2 + 2 * (p == 0)) * 2 * rows * width * 1536, (8 + 6 * (p == 0)) * 1024 * 1024),
        name="ff_grad",
    )(info, *chunks[0], *chunks[1], *weights)


def attn_bwd_kernel(last, info, cot_ref, lat_ref, res_ref, own_ref, got_ref, vec_ref,
                    mixed_ref, pt_ref, kv_ref, q_ref, normt_ref, lat_normt_ref, wqo_ref, *refs):
    if last:
        gkv_in, gqo_in, res_grad_ref, dq_ref, dkv_ref, sums_ref, g_own_ref, g_oth_ref, gkv, gqo = refs
    else:
        res_grad_ref, dq_ref, dkv_ref, sums_ref, gkv, gqo = refs
    i = pl.program_id(0)

    @pl.when(i == 0)
    def _():
        gkv[...] = gkv_in[...] if last else jnp.zeros_like(gkv)
        gqo[...] = gqo_in[...] if last else jnp.zeros_like(gqo)
        sums_ref[...] = jnp.zeros_like(sums_ref)

    xhat, rstd = norm_parts(res_ref[...])
    dy = own_ref[...].astype(F32) + got_ref[...].astype(F32)
    dx, dgain, dbias = norm_back(dy, xhat, rstd, vec_ref[4:5, :])
    grad = cot_ref[0].astype(F32) + dx
    res_grad_ref[...] = grad
    sums_ref[0:1, :] += dgain
    sums_ref[1:2, :] += dbias
    low = grad.astype(BF)
    columns = lambda start, stop: wqo_ref[:, :, start:stop].reshape(-1, stop - start)
    lane_lo = lax.broadcasted_iota(jnp.int32, (128, 128), 1) < HEAD_DIM
    row_lo = lax.broadcasted_iota(jnp.int32, (128, 128), 0) < HEAD_DIM
    both = jnp.concatenate([lat_normt_ref[0], low.T], 1)
    none = jnp.zeros((128, 128), BF)
    zeros = jnp.zeros((64, 128), BF)
    total = None
    for p in range(2):
        base = p * 384
        kv = kv_ref[0, :, base : base + 384]
        mixed_grad = dot(low, columns(base + 128, base + 384))
        mg2 = jnp.where(lane_lo, 0.0, mixed_grad[:, 0:128]).astype(BF)
        mg01 = mixed_grad[:, 128:256]
        mg01 = jnp.concatenate([jnp.where(lane_lo, mg01, 0.0), jnp.where(lane_lo, 0.0, mg01)], 0).astype(BF)
        first = dot_t(kv[:, 128:256], mg01)
        second = dot_t(kv[:, 256:384], mg2)
        probs, scores = [], []
        for h, piece in enumerate((first[:, 0:128], first[:, 128:256], second)):
            prob = pt_ref[0, p, :, h * 128 : (h + 1) * 128]
            inner = jnp.sum(piece * prob, 0, keepdims=True)
            scores.append((prob * (piece - inner)).astype(BF))
            probs.append(prob.astype(BF))
        q01 = q_ref[0, p, :, 0:128].astype(F32)
        q01 = jnp.concatenate([jnp.where(lane_lo, q01, 0.0), jnp.where(lane_lo, 0.0, q01)], 0).astype(BF)
        q2 = q_ref[0, p, :, 128:256]
        ds01 = jnp.concatenate(scores[:2], 1)
        dkv_ref[0, :, base : base + 128] = dot(ds01, q01).astype(BF)
        dkv_ref[0, :, base + 128 : base + 256] = dot(jnp.concatenate(probs[:2], 1), mg01).astype(BF)
        dkv_ref[0, :, base + 256 : base + 384] = dot(
            jnp.concatenate([scores[2], probs[2]], 1), jnp.concatenate([q2, mg2], 0)
        ).astype(BF)
        dq01 = dot(kv[:, 0:128].T, ds01)
        dq2 = dot(kv[:, 256:384].T, scores[2])
        dq01 = (jnp.where(row_lo, dq01[:, 0:128], dq01[:, 128:256]) * SCALE).astype(BF)
        dq2 = (jnp.where(row_lo, dq2, 0.0) * SCALE).astype(BF)
        dq_ref[0, p, 0:128, :] = dq01
        dq_ref[0, p, 128:192, :] = dq2[0:64]
        add = dot_t(jnp.concatenate([dq01.T, dq2.T], 1), columns(base, base + 256))
        total = add if total is None else total + add
        right = jnp.concatenate(
            [
                jnp.concatenate([dq01, none], 1),
                jnp.concatenate([dq2, jnp.concatenate([zeros, mixed_ref[0, p, 0:64, :]], 0)], 1),
                jnp.concatenate([none, mixed_ref[0, p, 64:192, :]], 1),
            ],
            0,
        )
        gqo[:, base : base + 384] += dot_t(both, right)
    lat_hat, _ = norm_parts(lat_ref[0].astype(F32))
    sums_ref[2:3, :] += jnp.sum(total * lat_hat, 0, keepdims=True)
    sums_ref[3:4, :] += jnp.sum(total, 0, keepdims=True)
    gkv[...] += dot(normt_ref[0], dkv_ref[0])

    if last:

        @pl.when(i == pl.num_programs(0) - 1)
        def _():
            block = gkv.shape[0] // 8
            for j, k in enumerate(ORDER):
                source = pl.ds(pl.multiple_of((info[4] ^ k) * block, 8), block)
                rows = slice(j * block, (j + 1) * block)
                g_own_ref[rows, 0:384] = gkv[source, 0:384].astype(BF)
                g_own_ref[rows, 384:768] = gqo[source, 0:384].astype(BF)
                g_oth_ref[rows, 0:384] = gkv[source, 384:768].astype(BF)
                g_oth_ref[rows, 384:768] = gqo[source, 384:768].astype(BF)


def attn_bwd_call(first_item, all_items, info, cotangent, latents, residual, own, got, vectors,
                  mixed, pt, kv, q, normt, lat_normt, wqo, grads=None):
    items, keys, _ = kv.shape
    width = normt.shape[1]
    lat_len = q.shape[2]
    last = grads is not None
    one = lambda i, *_: (i, 0)
    three = lambda i, *_: (i, 0, 0)
    mine = lambda i, info: (info[0] * all_items + first_item + i, 0, 0)
    four = lambda i, *_: (i, 0, 0, 0)
    z2 = lambda i, *_: (0, 0)
    flops = items * 2 * (keys * width * 768 + 3 * lat_len * width * 768 + 10 * keys * lat_len * 384)
    out_specs = [
        pl.BlockSpec((lat_len, width), one),
        pl.BlockSpec((1, 2, 192, lat_len), four),
        pl.BlockSpec((1, keys, 768), three),
        pl.BlockSpec((4, width), z2),
        pl.BlockSpec((width, 768), z2),
        pl.BlockSpec((width, 768), z2),
    ]
    out_shape = [
        jax.ShapeDtypeStruct((items * lat_len, width), F32),
        jax.ShapeDtypeStruct((items, 2, 192, lat_len), BF),
        jax.ShapeDtypeStruct((items, keys, 768), BF),
        jax.ShapeDtypeStruct((4, width), F32),
        jax.ShapeDtypeStruct((width, 768), BF if last else F32),
        jax.ShapeDtypeStruct((width, 768), BF if last else F32),
    ]
    return pl.pallas_call(
        functools.partial(attn_bwd_kernel, last),
        grid_spec=pltpu.PrefetchScalarGridSpec(
            num_scalar_prefetch=1,
            grid=(items,),
            in_specs=[
                pl.BlockSpec((1, lat_len, width), mine),
                pl.BlockSpec((1, lat_len, width), mine),
                pl.BlockSpec((lat_len, width), one),
                pl.BlockSpec((lat_len, width), one),
                pl.BlockSpec((lat_len, width), one),
                pl.BlockSpec(vectors.shape, z2),
                pl.BlockSpec((1, 2, 192, lat_len), four),
                pl.BlockSpec((1, 2, keys, 384), four),
                pl.BlockSpec((1, keys, 768), three),
                pl.BlockSpec((1, 2, lat_len, 256), four),
                pl.BlockSpec((1, width, keys), three),
                pl.BlockSpec((1, width, lat_len), three),
                pl.BlockSpec(wqo.shape, lambda i, *_: (0, 0, 0)),
            ]
            + [pl.BlockSpec((width, 768), z2)] * (2 * last),
            out_specs=out_specs,
            scratch_shapes=[pltpu.VMEM((width, 768), F32), pltpu.VMEM((width, 768), F32)] * last,
        ),
        out_shape=out_shape,
        compiler_params=params(),
        cost_estimate=cost(flops, 12 * 1024 * 1024),
        name="attn_bwd",
    )(info, cotangent, latents, residual, own, got, vectors, mixed, pt, kv, q, normt, lat_normt, wqo, *(grads or ()))


def latent_kernel(info, lat_ref, *refs):
    vec_ref, wqo_ref, wqx_ref, out_ref = refs[6:]
    width = vec_ref.shape[1]
    step = out_ref.shape[1]
    per = refs[0].shape[0] // step
    for c in range(2):
        grad_ref, own_ref, got_ref = refs[c], refs[2 + c], refs[4 + c]
        xhat, rstd = norm_parts(lat_ref[c * per : (c + 1) * per].reshape(-1, width).astype(F32))
        dy = spread(own_ref, wqo_ref, True) + spread(got_ref, wqx_ref, True)
        dx, _, _ = norm_back(dy, xhat, rstd, vec_ref[0:1, :])
        out_ref[c * per : (c + 1) * per] = (grad_ref[...] + dx).astype(BF).reshape(per, step, width)


def latent_call(info, latents, grads, own, got, vectors, wqo, wqx):
    half, width = grads[0].shape
    lat_len = latents.shape[1]
    items = 2 * half // lat_len
    z2 = lambda i, info: (0, 0)
    z3 = lambda i, info: (0, 0, 0)
    return pl.pallas_call(
        latent_kernel,
        grid_spec=pltpu.PrefetchScalarGridSpec(
            num_scalar_prefetch=1,
            grid=(1,),
            in_specs=[pl.BlockSpec((items, lat_len, width), lambda i, info: (info[0], 0, 0))]
            + [pl.BlockSpec((half, width), z2)] * 2
            + [pl.BlockSpec(own[0].shape, lambda i, info: (0, 0, 0, 0))] * 4
            + [pl.BlockSpec(vectors.shape, z2), pl.BlockSpec(wqo.shape, z3), pl.BlockSpec(wqx.shape, z3)],
            out_specs=pl.BlockSpec((items, lat_len, width), z3),
        ),
        out_shape=jax.ShapeDtypeStruct((items, lat_len, width), BF),
        compiler_params=params(),
        cost_estimate=cost(4 * items * lat_len * width * 768, 6 * 1024 * 1024),
        name="latent_back",
    )(info, latents, *grads, *own, *got, vectors, wqo, wqx)


def byte_part_kernel(info, dkv_ref, raw_ref, wkv_ref, own_ref, sums_ref, *send_refs):
    part = dot_t(dkv_ref[0], wkv_ref[...].reshape(-1, 768))
    xhat, _ = norm_parts(raw_ref[0].astype(F32))
    half = part.shape[0] // 2
    item = pl.program_id(0)

    @pl.when(item == 0)
    def _():
        sums_ref[...] = jnp.zeros_like(sums_ref)

    sums_ref[0:1, :] += jnp.sum(part * xhat, 0, keepdims=True)
    sums_ref[1:2, :] += jnp.sum(part, 0, keepdims=True)
    low = part.astype(BF)
    for side in range(2):
        for k, send_ref in enumerate(send_refs):

            @pl.when((info[1] == side) & (item == k))
            def _():
                own_ref[0] = low[half * side : half * (side + 1)]
                send_ref[0] = low[half * (1 - side) : half * (2 - side)]


def byte_part_call(info, dkv, raw, wkv):
    items, keys, _ = dkv.shape
    width = raw.shape[2]
    half = keys // 2
    out = lambda i, info: (i, 0, 0)
    whole = lambda i, info: (0, 0, 0)
    return pl.pallas_call(
        byte_part_kernel,
        grid_spec=pltpu.PrefetchScalarGridSpec(
            num_scalar_prefetch=1,
            grid=(items,),
            in_specs=[
                pl.BlockSpec((1, keys, 768), out),
                pl.BlockSpec((1, keys, width), out),
                pl.BlockSpec(wkv.shape, whole),
            ],
            out_specs=[
                pl.BlockSpec((1, half, width), out),
                pl.BlockSpec((2, width), lambda i, info: (0, 0)),
            ]
            + [pl.BlockSpec((1, half, width), whole)] * items,
        ),
        out_shape=[
            jax.ShapeDtypeStruct((items, half, width), BF),
            jax.ShapeDtypeStruct((2, width), F32),
        ]
        + [jax.ShapeDtypeStruct((1, half, width), BF)] * items,
        compiler_params=params(),
        cost_estimate=cost(items * keys * width * 768 * 2, 6 * 1024 * 1024),
        name="byte_part",
    )(info, dkv, raw, wkv)


def byte_back_kernel(info, part_ref, raw_ref, vec_ref, *refs):
    got_refs, (own_ref, oth_ref) = refs[:-2], refs[-2:]
    half = part_ref.shape[1]
    quarter = half // 2
    got = [ref[k] for ref in got_refs for k in range(ref.shape[0])]
    for k, piece in enumerate(got):
        dy = part_ref[k].astype(F32) + piece.astype(F32)
        xhat, rstd = norm_parts(raw_ref[k].astype(F32))
        dx, _, _ = norm_back(dy, xhat, rstd, vec_ref[2:3, :])
        dx = dx.astype(BF)

        @pl.when(info[0] == 0)
        def _():
            own_ref[k] = dx[:quarter]
            oth_ref[k] = dx[quarter:]

        @pl.when(info[0] != 0)
        def _():
            own_ref[k] = dx[quarter:]
            oth_ref[k] = dx[:quarter]


def byte_back_call(info, part, got, raw, vectors):
    items, half, width = part.shape
    z3 = lambda i, info: (0, 0, 0)
    return pl.pallas_call(
        byte_back_kernel,
        grid_spec=pltpu.PrefetchScalarGridSpec(
            num_scalar_prefetch=1,
            grid=(1,),
            in_specs=[
                pl.BlockSpec((items, half, width), z3),
                pl.BlockSpec((items, half, width), lambda i, info: (0, info[1], 0)),
                pl.BlockSpec(vectors.shape, lambda i, info: (0, 0)),
                *(pl.BlockSpec(piece.shape, z3) for piece in got),
            ],
            out_specs=[pl.BlockSpec((items, half // 2, width), z3)] * 2,
        ),
        out_shape=[jax.ShapeDtypeStruct((items, half // 2, width), BF)] * 2,
        compiler_params=params(),
        cost_estimate=cost(items * half * width * 20, 4 * 1024 * 1024),
        name="byte_back",
    )(info, part, raw, vectors, *got)


def body(
    latents, byte_array, cotangent, patch_count, text_len,
    inner_weight, inner_moment, inner_square,
    output_weight, output_moment, output_square,
    expand_weight, expand_moment, expand_square,
    reduce_weight, reduce_moment, reduce_square,
    expand_bias, bias_moment, bias_square,
    norm_vectors, vector_moment, vector_square,
):
    item_count, lat_len, width = latents.shape
    keys = byte_array.shape[1]
    items = item_count // 2
    n = lax.axis_size("dp")
    head = lax.axis_index("head")
    core, xside = head & 1, head >> 1
    true_rows = keys // lax.axis_size("head")
    pad_rows = -(-true_rows // 32) * 32
    pad_keys = 4 * pad_rows
    quick = n == 8
    place = lax.axis_index("dp") if quick else jnp.int32(0)
    info = jnp.stack([core, xside, jnp.int32(true_rows), jnp.int32(items), place]).astype(jnp.int32)
    half_items = items // 2

    low_inner = inner_weight.astype(BF)
    wq, wk, wv = low_inner[0], low_inner[1], low_inner[2]
    wo = output_weight.T.astype(BF)
    pack = jnp.concatenate(
        [wk[:, :128], wv[:, :128], wk[:, 128:], wv[:, 128:], wq[:, :128], wq[:, 128:], wo[:, 128:], wo[:, :128]], 1
    )
    ff_pack = jnp.concatenate([expand_weight.astype(BF), reduce_weight.T.astype(BF)], 1)
    normalise = lambda c, byte_array: norm_call(
        c * half_items, items, info, byte_array, latents, norm_vectors, half_items, pad_keys
    )
    flip = lambda value: swap(value, "head", 1)
    over = lambda value, mask: swap(value, "dp", mask)
    grouped = lambda p: [flip(jnp.concatenate([p[k] for k in group], 0)) for group in GROUPS]
    if quick:
        g = {0: pack, 4: over(pack, 4), 2: over(pack, 2), 1: over(pack, 1)}
        norm0 = normalise(0, byte_array)
        g[4], g[2], g[1], *norm0 = tie(g[4], g[2], g[1], *norm0)
        g[6], g[5], g[3] = over(g[4], 2), over(g[4], 1), over(g[2], 1)
        g[6], g[5], g[3], byte_later, ff_pack = tie(g[6], g[5], g[3], byte_array, ff_pack)
        f = {0: ff_pack, 4: over(ff_pack, 4), 2: over(ff_pack, 2), 1: over(ff_pack, 1)}
        g[7] = over(g[6], 1)
        norm1 = normalise(1, byte_later)
        g[7], f[4], f[2], f[1], *norm1 = tie(g[7], f[4], f[2], f[1], *norm1)
        f[6], f[5], f[3] = over(f[4], 2), over(f[4], 1), over(f[2], 1)
        pieces = [g[k] for k in range(8)] + grouped(g)
    else:
        norm0, norm1 = normalise(0, byte_array), normalise(1, byte_array)
        blocks = lax.all_gather(pack, "dp", axis=0, tiled=True).reshape(8, width // 8, 768)
        g = [blocks[k] for k in range(8)]
        pieces = g + grouped(g)
        blocks = lax.all_gather(ff_pack, "dp", axis=0, tiled=True).reshape(8, width // 8, 1536)
        f = [blocks[k] for k in range(8)]
    norm, normt, raw, lat_norm, lat_normt = zip(norm0, norm1)
    bias_other = flip(expand_bias)

    crossed = swap(jnp.concatenate([g[k][:, 384:] for k in range(8)], 0), "head", 2)

    attend = lambda c, weights: attn_fwd_call(
        c * half_items, info, patch_count, text_len, norm[c], lat_norm[c], weights
    )
    mixed0, *kept0, wkv, wqo = attend(0, pieces)
    got0 = swap(mixed0, "head", 2)
    if quick:
        first_flip = flip(jnp.concatenate([f[k] for k in GROUPS[0]], 0))
        wkv, f[6], f[5], f[3], first_flip, bias_other, crossed = tie(
            wkv, f[6], f[5], f[3], first_flip, bias_other, crossed
        )
        f[7] = over(f[6], 1)
        second_flip = flip(jnp.concatenate([f[k] for k in GROUPS[1]], 0))
    crossed = [crossed, flip(crossed)]
    mixed1, *kept1 = attend(1, [wkv, wqo])
    mixed1, got0, crossed[1] = tie(mixed1, got0, crossed[1])
    got1 = swap(mixed1, "head", 2)
    if quick:
        mixed1, second_flip, f[7] = tie(mixed1, second_flip, f[7])
        ff_pieces = [f[k] for k in range(8)] + [first_flip, second_flip, flip(f[7])]
    else:
        ff_pieces = f + grouped(f)

    bias_both = jnp.stack([expand_bias, bias_other])
    feed = lambda c, mixed, got, weights: ff_core_call(
        c, info, latents, cotangent, mixed, got, norm_vectors, bias_both, wqo, weights
    )
    res0, *ff0, npart0, cot_sum0, ff_own, ff_oth, wqx = feed(0, mixed0, got0, [*ff_pieces, *crossed])
    npart0, got1 = tie(npart0, got1)
    ngot0 = swap(npart0, "head", 2)
    res1, *ff1, npart1, cot_sum1 = feed(1, mixed1, got1, [ff_own, ff_oth, wqx])
    npart1, ngot0 = tie(npart1, ngot0)
    ngot1 = swap(npart1, "head", 2)
    g_oth, bias_oth = ff_grad_call(1, info, [ff0, ff1])
    g_oth, ngot0, ff1[3] = tie(g_oth, ngot0, ff1[3])
    g_got = flip(g_oth)
    g_own, bias_own, mlp_part = ff_grad_call(0, info, [ff0, ff1], [ff_own, ff_oth])
    g_own, ngot0, ngot1, g_got = tie(g_own, ngot0, ngot1, g_got)
    bias_own = bias_own + flip(bias_oth)
    pair_of = lambda kind, part: (g_own[kind, part], g_got[kind, part])
    first_steps = [plus(*pair_of(kind, slice(0, 4))) for kind in range(2)]

    attend_back = lambda c, res, npart, ngot, mixed, kept, grads: attn_bwd_call(
        c * half_items, items, info, cotangent, latents, res, npart, ngot,
        norm_vectors, mixed, *kept, normt[c], lat_normt[c], wqo, grads
    )
    res0, ngot0, bias_own, mlp_part, *first_steps = tie(res0, ngot0, bias_own, mlp_part, *first_steps)
    mlp_got = swap(mlp_part, "head", 2)
    if quick:
        ff_got = [over(first_steps[0], 1), over(first_steps[1], 2)]
    rgrad0, dq0, dkv0, sums0, *grads = attend_back(0, res0, npart0, ngot0, mixed0, kept0, None)
    bown0, bsums0, *bsend0 = byte_part_call(info, dkv0, raw[0], wkv)
    res1, bsend0[0], mlp_got = tie(res1, bsend0[0], mlp_got)
    bgot00 = swap(bsend0[0], "head", 2)
    if quick:
        res1, *ff_got = tie(res1, *ff_got)
        second_steps = [plus(*pair_of(kind, slice(4, 6)), ff_got[kind][0:2]) for kind in range(2)]
        ff_more = [over(second_steps[0], 2), over(second_steps[1], 1)]
    rgrad1, dq1, dkv1, sums1, g_attn, g_attn_oth = attend_back(1, res1, npart1, ngot1, mixed1, kept1, grads)
    g_attn_oth, bgot00, bsend0[1] = tie(g_attn_oth, bgot00, bsend0[1])
    bgot01 = swap(bsend0[1], "head", 2)
    if quick:
        g_attn_oth, *ff_more = tie(g_attn_oth, *ff_more)
        rest = [(*pair_of(kind, part), ff_got[kind][part - 4], ff_more[kind][part - 6]) for part in (6, 7) for kind in range(2)]
        third_step = jnp.concatenate([plus(*rest[0]), plus(*rest[1])], 0)
    else:
        g_ff = g_own.astype(F32) + g_got.astype(F32)
        g_ff = jnp.stack([g_ff[kind, order.index(k)] for kind, order in enumerate(FF_ORDERS) for k in range(8)])
        g_ff = g_ff.reshape(2, width, 768)
        g_ff = lax.psum_scatter(g_ff, "dp", scatter_dimension=1, tiled=True).reshape(-1, 768)
    u = g_attn.reshape(8, width // 8, 768)
    v = flip(g_attn_oth).reshape(8, width // 8, 768)
    u75 = plus(u[0:2], v[0:2])

    if quick:
        u31 = plus(u[2:4], v[2:4])
        dkv1, u75, u31, third_step = tie(dkv1, u75, u31, third_step)
        third = third_step.shape[0] // 3
        last_got = [over(third_step[:third], 4)]
        y75 = over(u75, 1)
        y31 = over(u31, 1)
    bown1, bsums1, *bsend1 = byte_part_call(info, dkv1, raw[1], wkv)
    if quick:
        bsend1[0], y75, bgot01, dq0, dq1, last_got[0] = tie(bsend1[0], y75, bgot01, dq0, dq1, last_got[0])
        u64 = plus(u[4:6], v[4:6], y75)
        last_got.append(over(third_step[third : 2 * third], 4))
        z6 = over(u64[0], 2)
    lgot0, lgot1 = swap(dq0, "head", 2), swap(dq1, "head", 2)
    side0 = list(byte_back_call(info, bown0, [bgot00, bgot01], raw[0], norm_vectors))

    residual = jnp.concatenate([res0, res1], 0)
    block_mine = residual + (mlp_part.astype(F32) + mlp_got.astype(F32)) + norm_vectors[6]
    block_mine = block_mine.astype(BF).reshape(items, lat_len, width)

    byte_side = lambda c, own, got: byte_back_call(info, own, got, raw[c], norm_vectors)
    if quick:
        block_mine, z6, y31, bsend1[0], lgot0, lgot1, last_got[1], side0[0] = tie(
            block_mine, z6, y31, bsend1[0], lgot0, lgot1, last_got[1], side0[0]
        )
        last_got.append(over(third_step[2 * third :], 4))
        z4 = over(plus(u64[1], z6), 4)
        z2 = over(plus(u[6], v[6], y31[0]), 2)
    bgot10 = swap(bsend1[0], "head", 2)
    lat_mine = latent_call(
        info, latents, [rgrad0, rgrad1], [dq0, dq1], [lgot0, lgot1], norm_vectors, wqo, wqx
    )
    block_output = pair_call(info, [block_mine], [flip(block_mine)], lat_len)
    if quick:
        block_output, lat_mine, last_got[2], z4, z2 = tie(block_output, lat_mine, last_got[2], z4, z2)
        g_ff = jnp.concatenate([sum(x.astype(F32) for x in rest[2 + kind]) for kind in range(2)], 0)
        g_ff = g_ff + jnp.concatenate(last_got, 0).astype(F32)
        ff_squares = jnp.sum(g_ff * g_ff)
        bgot10, bsend1[1] = tie(bgot10, bsend1[1])
        terms = [u[7], v[7], y31[1], z2, z4]
    else:
        g_attn = u.astype(F32) + v.astype(F32)
        g_attn = jnp.concatenate([g_attn[ORDER.index(k)] for k in range(8)], 0)
        terms = [lax.psum_scatter(g_attn, "dp", scatter_dimension=0, tiled=True)]
        ff_squares = jnp.sum(g_ff * g_ff)
    bgot11 = swap(bsend1[1], "head", 2)
    side1 = byte_side(1, bown1, [bgot10, bgot11])
    g_attn, load = collect_call(
        info, terms, [sums0, sums1, bsums0, bsums1, cot_sum0, cot_sum1, bias_own, ff_squares.reshape(1, 1)]
    )
    latent_gradient = pair_call(info, [lat_mine], [flip(lat_mine)], lat_len)
    beside = [lambda: latent_gradient, None, lambda: side1]
    outs = []
    mask = n // 2
    while mask:
        hop = over(load, mask)
        make = beside.pop(0) if beside else None
        if make:
            hop, out = lax.optimization_barrier((hop, make()))
            outs.append(out)
        load = load + hop
        mask //= 2
    latent_gradient = outs[0]
    byte_gradient = pair_call(info, [side0[0], outs[1][0]], [flip(side0[1]), flip(outs[1][1])], true_rows)
    bias_sum = load[7:8]
    squares = load[8:9] + jnp.sum(bias_sum * bias_sum)
    load = jnp.concatenate([load[:7], squares], 0)
    load = load + swap(load, "head", 1)
    load = load + swap(load, "head", 2)

    *news, grad_norm = adam_call(
        load,
        g_attn,
        g_ff,
        [
            inner_weight, inner_moment, inner_square, output_weight, output_moment, output_square,
            expand_weight, expand_moment, expand_square, reduce_weight.T, reduce_moment.T, reduce_square.T,
            norm_vectors, vector_moment, vector_square,
        ],
    )
    factor = CLIP_RATE * math.sqrt(4 * D * D + 2 * D * FF + FF + 7 * D) / grad_norm[0, 0]
    bias_new = adamw(expand_bias, bias_moment, bias_square, factor * bias_sum[0], 0.3, 0.0)
    news[9:12] = [new.T for new in news[9:12]]
    return (
        block_output, latent_gradient, byte_gradient, *news[:12], *bias_new, *news[12:], grad_norm[0, 0]
    )


def solution(mesh):
    rows, cols = P("dp", "head"), P("head", "dp")
    inner, items = P(None, "dp", "head"), P("dp", None, None)
    weights = (inner,) * 3 + (cols,) * 3 + (rows,) * 3 + (cols,) * 3 + (P("head"),) * 3 + (P(),) * 3
    return jax.shard_map(
        body,
        mesh=mesh,
        in_specs=(items, items, items, P("dp"), P("dp")) + weights,
        out_specs=(items, items, P("dp", "head", None)) + weights + (P(),),
        check_vma=False,
    )
```

```python
import functools
import math

import jax
import jax.numpy as jnp
from jax import lax
from jax.experimental import pallas as pl
from jax.experimental.pallas import tpu as pltpu
from jax.sharding import PartitionSpec as P

D = 768
HEAD_DIM = 64
FF = 3072
PATCHES = 576
STEP = 5

NEG_FILL = -1000000000.0
BETA = 0.5
ADAM_EPS = 1e-08
DECAY = 0.01
CLIP_RATE = 0.01
LN_EPS = 1e-05
SCALE = 1.0 / math.sqrt(HEAD_DIM)
BF = jnp.bfloat16
F32 = jnp.float32
VMEM_LIMIT = 20 * 1024 * 1024


def dot(a, b):
    return lax.dot_general(a, b, (((1,), (0,)), ((), ())), preferred_element_type=F32)


def dot_t(a, b):
    return lax.dot_general(a, b, (((1,), (1,)), ((), ())), preferred_element_type=F32)


def norm_parts(rows):
    centred = rows - jnp.mean(rows, -1, keepdims=True)
    rstd = lax.rsqrt(jnp.mean(centred * centred, -1, keepdims=True) + LN_EPS)
    return centred * rstd, rstd


def norm_back(dy, xhat, rstd, gain):
    scaled = dy * gain
    first = jnp.mean(scaled, -1, keepdims=True)
    second = jnp.mean(scaled * xhat, -1, keepdims=True)
    dx = rstd * (scaled - first - xhat * second)
    return dx, jnp.sum(dy * xhat, 0, keepdims=True), jnp.sum(dy, 0, keepdims=True)


def swap(value, axis, mask):
    size = lax.axis_size(axis)
    return lax.ppermute(value, axis, [(i, i ^ mask) for i in range(size)])


def tie(*values):
    return lax.optimization_barrier(tuple(values))


def plus(*values):
    return sum(value.astype(F32) for value in values).astype(BF)


def adamw(weight, moment, square, gradient, rate, decay_rate):
    moment_new = BETA * moment + (1.0 - BETA) * gradient
    square_new = BETA * square + (1.0 - BETA) * gradient * gradient
    correction = 1.0 - BETA**STEP
    step_dir = moment_new * (1.0 / correction) / (jnp.sqrt(square_new * (1.0 / correction)) + ADAM_EPS)
    return (weight - rate * (step_dir + decay_rate * weight), moment_new, square_new)


def params(**kw):
    return pltpu.CompilerParams(vmem_limit_bytes=VMEM_LIMIT, **kw)


def cost(flops, nbytes, trans=0):
    return pl.CostEstimate(flops=flops, bytes_accessed=nbytes, transcendentals=trans)


GROUPS = ((0, 4, 2, 1), (6, 5, 3), (7,))


def assemble(info, parts, outs, splits):
    rows = parts[0].shape[0]
    blocks = [(k, 0, parts[k], 0) for k in range(8)]
    for part, group in zip(parts[8:], GROUPS):
        blocks += [(k, 1, part, i * rows) for i, k in enumerate(group)]
    for k, c, part, first in blocks:
        for out, start, stop, offset in splits[c]:
            outs[out][info[4] ^ k, :, offset : offset + stop - start] = part[first : first + rows, start:stop]


ORDER = (7, 5, 3, 1, 6, 4, 2, 0)
FF_ORDERS = ((7, 3, 5, 1, 6, 2, 4, 0), (7, 3, 6, 2, 5, 1, 4, 0))


def pair_kernel(chunks, info, *refs):
    out = refs[-1]
    rows = out.shape[1]
    per = refs[0].shape[0]
    for side in range(2):
        first = (info[0] ^ side) * (chunks * per)
        for c in range(chunks):
            ref = refs[side * chunks + c]
            for k in range(per):
                out[first + c * per + k] = ref[k, :rows, :]


def pair_call(info, own, other, rows):
    per, _, width = own[0].shape
    chunks = len(own)
    return pl.pallas_call(
        functools.partial(pair_kernel, chunks),
        grid_spec=pltpu.PrefetchScalarGridSpec(
            num_scalar_prefetch=1,
            grid=(1,),
            in_specs=[pl.BlockSpec(own[0].shape, lambda i, info: (0, 0, 0))] * (2 * chunks),
            out_specs=pl.BlockSpec((2 * chunks * per, rows, width), lambda i, info: (0, 0, 0)),
        ),
        out_shape=jax.ShapeDtypeStruct((2 * chunks * per, rows, width), BF),
        compiler_params=params(),
        cost_estimate=cost(1, 4 * chunks * per * rows * width * 2),
        name="pair",
    )(info, *own, *other)


def rows_kernel(info, *refs):
    blocks, out = refs[:4], refs[4]
    true_rows, step = out.shape[0], 32
    for core in range(2):

        @pl.when(info[0] == core)
        def _():
            order = blocks if core == 0 else (*blocks[2:], *blocks[:2])
            for first in range(0, true_rows, step):
                count = min(step, true_rows - first)
                items = [ref[k, first : first + step, :].astype(F32) for ref in order for k in range(ref.shape[0])]
                by_row = pltpu.einshape("abc->bac", jnp.stack(items, 0))
                out[first : first + count] = by_row[:count].astype(BF)


def rows_call(info, own, other, rows):
    per, _, width = own[0].shape
    return pl.pallas_call(
        rows_kernel,
        grid_spec=pltpu.PrefetchScalarGridSpec(
            num_scalar_prefetch=1,
            grid=(1,),
            in_specs=[pl.BlockSpec(own[0].shape, lambda i, info: (0, 0, 0))] * 4,
            out_specs=pl.BlockSpec((rows, 4 * per, width), lambda i, info: (0, 0, 0)),
        ),
        out_shape=jax.ShapeDtypeStruct((rows, 4 * per, width), BF),
        compiler_params=params(),
        cost_estimate=cost(1, 16 * per * rows * width),
        name="rows",
    )(info, *own, *other)


def collect_kernel(count, info, *refs):
    terms, (sums0, sums1, bytes0, bytes1, cot0, cot1, bias, squares, grad_ref, load_ref) = refs[:count], refs[count:]
    grad = sum(ref[...].astype(F32) for ref in terms)
    grad_ref[...] = grad
    once = jnp.where(info[1] == 0, 1.0, 0.0)
    sums = sums0[...] + sums1[...]
    load_ref[0:2, :] = sums[2:4]
    load_ref[2:4, :] = bytes0[...] + bytes1[...]
    load_ref[4:6, :] = sums[0:2] * once
    load_ref[6:7, :] = (cot0[...] + cot1[...]) * once
    load_ref[7:8, :] = bias[...]
    total = jnp.sum(jnp.sum(grad * grad, 0, keepdims=True), 1, keepdims=True) + squares[...]
    load_ref[8:9, :] = jnp.broadcast_to(total, (1, load_ref.shape[1]))


def collect_call(info, terms, small):
    rows, width = terms[0].shape
    whole = lambda i, info: (0, 0)
    return pl.pallas_call(
        functools.partial(collect_kernel, len(terms)),
        grid_spec=pltpu.PrefetchScalarGridSpec(
            num_scalar_prefetch=1,
            grid=(1,),
            in_specs=[pl.BlockSpec(x.shape, whole) for x in (*terms, *small)],
            out_specs=[pl.BlockSpec((rows, width), whole), pl.BlockSpec((9, width), whole)],
        ),
        out_shape=[jax.ShapeDtypeStruct((rows, width), F32), jax.ShapeDtypeStruct((9, width), F32)],
        compiler_params=params(),
        cost_estimate=cost(1, 16 * rows * width),
        name="collect",
    )(info, *terms, *small)


def adam_kernel(load_ref, attn_ref, ff_ref, *refs):
    inner, output, expand, reduce, vector = (refs[3 * k : 3 * k + 3] for k in range(5))
    outs = refs[15:]
    load = load_ref[...]
    vectors = load[0:7]
    total = load[7:8, 0:1] + jnp.sum(jnp.sum(vectors * vectors, 0, keepdims=True), 1, keepdims=True)
    norm = jnp.sqrt(total)
    outs[15][...] = norm
    factor = CLIP_RATE * math.sqrt(4 * D * D + 2 * D * FF + FF + 7 * D) / norm

    def update(which, at, grad, rate, decay_rate):
        state = refs[3 * which : 3 * which + 3]
        for ref, new in zip(
            outs[3 * which : 3 * which + 3],
            adamw(*(ref[at] for ref in state), factor * grad, rate, decay_rate),
        ):
            ref[at] = new

    low, high = slice(0, 128), slice(128, 192)
    every = slice(None)
    for matrix, first, second in ((0, 384, 512), (1, 0, 256), (2, 128, 320)):
        update(0, (matrix, every, low), attn_ref[:, first : first + 128], 0.03, DECAY)
        update(0, (matrix, every, high), attn_ref[:, second : second + 64], 0.03, DECAY)
    update(1, (low, every), attn_ref[:, 640:768].T, 0.3, DECAY)
    update(1, (high, every), attn_ref[:, 512:640].T[64:128], 0.3, DECAY)
    rows = expand[0].shape[0]
    update(2, Ellipsis, ff_ref[0:rows, :], 0.03, DECAY)
    update(3, Ellipsis, ff_ref[rows : 2 * rows, :], 0.015, DECAY)
    update(4, Ellipsis, vectors, 0.3, 0.0)


def adam_call(load, attn, ff, state):
    shapes = [jax.ShapeDtypeStruct(x.shape, F32) for x in state] + [jax.ShapeDtypeStruct((1, 1), F32)]
    return pl.pallas_call(
        adam_kernel,
        out_shape=shapes,
        compiler_params=params(),
        cost_estimate=cost(1, sum(x.size for x in state) * 4 * 2),
        name="adam",
    )(load, attn, ff, *state)


def norm_kernel(info, byte_ref, lat_ref, vec_ref, norm_ref, normt_ref, raw_ref, lat_norm_ref, lat_normt_ref, scr):
    groups, true_rows, pad_rows = 4, byte_ref.shape[1] // 4, norm_ref.shape[1] // 4
    keys = byte_ref.shape[1]
    scr[pl.ds(0, keys), :] = byte_ref[0].astype(F32)
    gain, bias = vec_ref[2:3, :], vec_ref[3:4, :]
    keep = lax.broadcasted_iota(jnp.int32, (pad_rows, 1), 0) < true_rows
    for g in range(groups):
        rows = jnp.where(keep, scr[pl.ds(g * true_rows, pad_rows), :], 0.0)
        xhat, _ = norm_parts(rows)
        normed = jnp.where(keep, xhat * gain + bias, 0.0)
        here = pl.ds(g * pad_rows, pad_rows)
        raw_ref[0, here, :] = rows.astype(BF)
        norm_ref[0, here, :] = normed.astype(BF)
    normt_ref[0] = norm_ref[0].T
    xhat, _ = norm_parts(lat_ref[0].astype(F32))
    lat_norm = (xhat * vec_ref[0:1, :] + vec_ref[1:2, :]).astype(BF)
    lat_norm_ref[0] = lat_norm
    lat_normt_ref[0] = lat_norm.T


def norm_call(first_item, all_items, info, byte_array, latents, vectors, items, pad_keys):
    _, keys, width = byte_array.shape
    lat_len = latents.shape[1]
    here = lambda i, info: (info[0] * all_items + first_item + i, 0, 0)
    out = lambda i, info: (i, 0, 0)
    return pl.pallas_call(
        norm_kernel,
        grid_spec=pltpu.PrefetchScalarGridSpec(
            num_scalar_prefetch=1,
            grid=(items,),
            in_specs=[
                pl.BlockSpec((1, keys, width), here),
                pl.BlockSpec((1, lat_len, width), here),
                pl.BlockSpec(vectors.shape, lambda i, info: (0, 0)),
            ],
            out_specs=[
                pl.BlockSpec((1, pad_keys, width), out),
                pl.BlockSpec((1, width, pad_keys), out),
                pl.BlockSpec((1, pad_keys, width), out),
                pl.BlockSpec((1, lat_len, width), out),
                pl.BlockSpec((1, width, lat_len), out),
            ],
            scratch_shapes=[pltpu.VMEM((keys + 40, width), F32)],
        ),
        out_shape=[
            jax.ShapeDtypeStruct((items, pad_keys, width), BF),
            jax.ShapeDtypeStruct((items, width, pad_keys), BF),
            jax.ShapeDtypeStruct((items, pad_keys, width), BF),
            jax.ShapeDtypeStruct((items, lat_len, width), BF),
            jax.ShapeDtypeStruct((items, width, lat_len), BF),
        ],
        compiler_params=params(),
        cost_estimate=cost(items * keys * width * 20, items * keys * width * 8),
        name="norms",
    )(info, byte_array, latents, vectors)


SPLITS = (((0, 0, 384, 0), (1, 384, 768, 0)), ((0, 0, 384, 384), (1, 384, 768, 384)))


def attn_fwd_kernel(first_item, info, count_ref, text_ref, norm_ref, lat_ref, *refs):
    if first_item == 0:
        pieces, (mixed_ref, pt_ref, kv_ref, q_ref, wkv_ref, wqo_ref) = refs[:11], refs[11:]

        @pl.when(pl.program_id(0) == 0)
        def _():
            assemble(info, pieces, (wkv_ref, wqo_ref), SPLITS)

    else:
        wkv_ref, wqo_ref, mixed_ref, pt_ref, kv_ref, q_ref = refs
    wkv = wkv_ref[...].reshape(-1, 768)
    columns = lambda start, stop: wqo_ref[:, :, start:stop].reshape(-1, stop - start)
    item = info[0] * info[3] + first_item + pl.program_id(0)
    patches, texts = count_ref[item], text_ref[item]
    keys = norm_ref.shape[1]
    pad_rows = keys // 4
    true_rows = info[2]
    row = lax.broadcasted_iota(jnp.int32, (keys, 128), 0)
    group = sum(((row >= pad_rows * g).astype(jnp.int32) for g in range(1, 4)))
    inner = row - group * pad_rows
    slot = inner + group * true_rows
    valid = ((slot < PATCHES) & (slot < patches)) | ((slot >= PATCHES) & (slot - PATCHES < texts))
    valid = valid & (inner < true_rows)
    lane_lo = lax.broadcasted_iota(jnp.int32, (128, 128), 1) < HEAD_DIM
    row_lo = lax.broadcasted_iota(jnp.int32, (128, 128), 0) < HEAD_DIM
    kv_all = dot(norm_ref[0], wkv).astype(BF)
    kv_ref[0] = kv_all
    lat_norm = lat_ref[0]
    for p in range(2):
        kv = kv_all[:, p * 384 : (p + 1) * 384]
        base = p * 384
        q = dot(lat_norm, columns(base, base + 256)) * SCALE
        q01, q2 = q[:, :128], jnp.where(lane_lo, q[:, 128:], 0.0).astype(BF)
        q_ref[0, p, :, 0:128] = q01.astype(BF)
        q_ref[0, p, :, 128:256] = q2
        stacked = jnp.concatenate([jnp.where(lane_lo, q01, 0.0), jnp.where(lane_lo, 0.0, q01)], 0).astype(BF)
        first = dot_t(kv[:, 0:128], stacked)
        second = dot_t(kv[:, 256:384], q2)
        pieces = []
        for piece in (first[:, 0:128], first[:, 128:256], second):
            piece = jnp.where(valid, piece, NEG_FILL)
            top = jnp.max(piece, 0, keepdims=True)
            expo = jnp.exp(piece - top)
            pieces.append(expo * (1.0 / jnp.sum(expo, 0, keepdims=True)))
        for h in range(3):
            pt_ref[0, p, :, h * 128 : (h + 1) * 128] = pieces[h]
        low01 = jnp.concatenate([pieces[0].astype(BF), pieces[1].astype(BF)], 1)
        o01 = dot(kv[:, 128:256].T, low01)
        o2 = dot(kv[:, 256:384].T, pieces[2].astype(BF))
        mixed_ref[0, p, 0:64, :] = o2[64:128].astype(BF)
        mixed_ref[0, p, 64:192, :] = jnp.where(row_lo, o01[:, 0:128], o01[:, 128:256]).astype(BF)


def attn_fwd_call(first_item, info, counts, texts, norm, lat_norm, weights):
    items, keys, width = norm.shape
    lat_len = lat_norm.shape[1]
    out3 = lambda i, *_: (i, 0, 0)
    out4 = lambda i, *_: (i, 0, 0, 0)
    given = [pl.BlockSpec(w.shape, lambda i, *_, d=w.ndim: (0,) * d) for w in weights]
    made = [pl.BlockSpec((8, width // 8, 768), lambda i, *_: (0, 0, 0))] * (2 * (first_item == 0))
    flops = items * 2 * (keys * width * 768 + lat_len * width * 768 + 4 * keys * lat_len * 384)
    return pl.pallas_call(
        functools.partial(attn_fwd_kernel, first_item),
        grid_spec=pltpu.PrefetchScalarGridSpec(
            num_scalar_prefetch=3,
            grid=(items,),
            in_specs=[
                pl.BlockSpec((1, keys, width), out3),
                pl.BlockSpec((1, lat_len, width), out3),
                *given,
            ],
            out_specs=[
                pl.BlockSpec((1, 2, 192, lat_len), out4),
                pl.BlockSpec((1, 2, keys, 384), out4),
                pl.BlockSpec((1, keys, 768), out3),
                pl.BlockSpec((1, 2, lat_len, 256), out4),
                *made,
            ],
        ),
        out_shape=[
            jax.ShapeDtypeStruct((items, 2, 192, lat_len), BF),
            jax.ShapeDtypeStruct((items, 2, keys, 384), F32),
            jax.ShapeDtypeStruct((items, keys, 768), BF),
            jax.ShapeDtypeStruct((items, 2, lat_len, 256), BF),
        ]
        + [jax.ShapeDtypeStruct((8, width // 8, 768), BF)] * len(made),
        compiler_params=params(),
        cost_estimate=cost(flops, 8 * 1024 * 1024, items * keys * 768),
        name="attn_fwd",
    )(info, counts, texts, norm, lat_norm, *weights)


def spread(mixed_ref, w_ref, queries):
    zeros = jnp.zeros((64, mixed_ref.shape[3]), BF)
    total = []
    for item in range(mixed_ref.shape[0]):
        rows = None
        for p in range(2):
            mixed = mixed_ref[item, p]
            parts = (mixed[0:128], mixed[128:192], zeros) if queries else (zeros, mixed[0:64], mixed[64:192])
            first = p * 384 + 128 * (not queries)
            columns = w_ref[:, :, first : first + 256].reshape(-1, 256)
            add = dot_t(jnp.concatenate(parts, 0).T, columns)
            rows = add if rows is None else rows + add
        total.append(rows)
    return jnp.concatenate(total, 0)


def ff_core_kernel(chunk, info, lat_ref, cot_ref, own_ref, got_ref, vec_ref, bias_ref, wqo_ref, *refs):
    if chunk == 0:
        pieces, crossed = refs[:11], refs[11:13]
        res_ref, normt_ref, cott_ref, hidden_ref, pre_ref, part_ref, cot_sum_ref, *weights, wqx_ref = refs[13:]
        assemble(info, pieces, weights, (((0, 0, 1536, 0),), ((1, 0, 1536, 0),)))
        rows = wqx_ref.shape[1]
        for k in range(8):
            for c in range(2):
                wqx_ref[info[4] ^ k, :, 384 * c : 384 * (c + 1)] = crossed[c][k * rows : (k + 1) * rows, :]
    else:
        weights, wqx_ref = refs[:2], refs[2]
        res_ref, normt_ref, cott_ref, hidden_ref, pre_ref, part_ref, cot_sum_ref = refs[3:]
    width = vec_ref.shape[1]
    flat = lambda ref: ref[...].reshape(-1, width).astype(F32)
    residual = flat(lat_ref) + (spread(own_ref, wqo_ref, False) + spread(got_ref, wqx_ref, False))
    res_ref[...] = residual
    xhat, _ = norm_parts(residual)
    normed = (xhat * vec_ref[4:5, :] + vec_ref[5:6, :]).astype(BF)
    cot = cot_ref[...].reshape(-1, width)
    total = None
    step = 256
    for p, w_ref in enumerate(weights):
        columns = lambda start: w_ref[:, :, start : start + step].reshape(-1, step)
        for j in range(768 // step):
            cols = slice(j * step, (j + 1) * step)
            w1 = columns(j * step)
            pre = dot(normed, w1) + bias_ref[p : p + 1, cols]
            back = dot(cot, columns(768 + j * step))
            cdf = 0.5 + 0.5 * lax.erf(pre * math.sqrt(0.5))
            pdf = jnp.exp(pre * pre * -0.5) * (1.0 / math.sqrt(2.0 * math.pi))
            hidden_ref[p, :, cols] = (pre * cdf).astype(BF)
            grad = (back * (cdf + pre * pdf)).astype(BF)
            pre_ref[p, :, cols] = grad
            add = dot_t(grad, w1)
            total = add if total is None else total + add
    part_ref[...] = total.astype(BF)
    normt_ref[...] = normed.T
    cott_ref[...] = cot.T
    cot_sum_ref[...] = jnp.sum(cot.astype(F32), 0, keepdims=True)


def ff_core_call(chunk, info, latents, cotangent, own, got, vectors, bias, wqo, weights):
    items = own.shape[0]
    _, lat_len, width = latents.shape
    rows = items * lat_len
    half = lambda i, info: (2 * info[0] + chunk, 0, 0)
    z3 = lambda i, info: (0, 0, 0)
    z4 = lambda i, info: (0, 0, 0, 0)
    z2 = lambda i, info: (0, 0)
    given = [pl.BlockSpec(w.shape, lambda i, info, d=w.ndim: (0,) * d) for w in weights]
    lanes = (1536, 1536, 768) if chunk == 0 else ()
    made = [pl.BlockSpec((8, width // 8, cols), z3) for cols in lanes]
    return pl.pallas_call(
        functools.partial(ff_core_kernel, chunk),
        grid_spec=pltpu.PrefetchScalarGridSpec(
            num_scalar_prefetch=1,
            grid=(1,),
            in_specs=[
                pl.BlockSpec((items, lat_len, width), half),
                pl.BlockSpec((items, lat_len, width), half),
                pl.BlockSpec(own.shape, z4),
                pl.BlockSpec(got.shape, z4),
                pl.BlockSpec(vectors.shape, z2),
                pl.BlockSpec(bias.shape, z2),
                pl.BlockSpec(wqo.shape, z3),
                *given,
            ],
            out_specs=[
                pl.BlockSpec((rows, width), z2),
                pl.BlockSpec((width, rows), z2),
                pl.BlockSpec((width, rows), z2),
                pl.BlockSpec((2, rows, 768), z3),
                pl.BlockSpec((2, rows, 768), z3),
                pl.BlockSpec((rows, width), z2),
                pl.BlockSpec((1, width), z2),
                *made,
            ],
        ),
        out_shape=[
            jax.ShapeDtypeStruct((rows, width), F32),
            jax.ShapeDtypeStruct((width, rows), BF),
            jax.ShapeDtypeStruct((width, rows), BF),
            jax.ShapeDtypeStruct((2, rows, 768), BF),
            jax.ShapeDtypeStruct((2, rows, 768), BF),
            jax.ShapeDtypeStruct((rows, width), BF),
            jax.ShapeDtypeStruct((1, width), F32),
        ]
        + [jax.ShapeDtypeStruct((8, width // 8, cols), BF) for cols in lanes],
        compiler_params=params(),
        cost_estimate=cost(6 * rows * width * 1536, 8 * 1024 * 1024, 2 * rows * 1536),
        name="ff_core",
    )(info, latents, cotangent, own, got, vectors, bias, wqo, *weights)


def relative_rows(info, ref, order):
    block = ref.shape[0] // 8
    return jnp.concatenate([ref[pl.ds(pl.multiple_of((info[4] ^ k) * block, 16), block), :] for k in order], 0)


def ff_grad_kernel(p, info, *refs):
    chunks, refs = (refs[:4], refs[4:8]), refs[8:]
    grad_ref, bias_ref = refs[-4:-2] if p == 0 else refs
    expand, reduce, bias = 0.0, 0.0, 0.0
    for normt_ref, cott_ref, hidden_ref, pre_ref in chunks:
        hidden, pre = hidden_ref[p], pre_ref[p]
        expand += dot(relative_rows(info, normt_ref, FF_ORDERS[0]), pre)
        reduce += dot(relative_rows(info, cott_ref, FF_ORDERS[1]), hidden)
        bias += jnp.sum(pre.astype(F32), 0, keepdims=True)
    grad_ref[0] = expand.astype(BF).reshape(8, -1, expand.shape[1])
    grad_ref[1] = reduce.astype(BF).reshape(8, -1, reduce.shape[1])
    bias_ref[...] = bias
    if p == 0:
        w_refs, (part_ref, acc) = refs[:2], refs[-2:]
        j = pl.program_id(0)
        rows = chunks[0][0].shape[1]
        for c, chunk in enumerate(chunks):
            here = pl.ds(c * rows, rows)
            add = sum(dot_t(chunk[2][q], w_ref[...].reshape(-1, w_ref.shape[2])) for q, w_ref in enumerate(w_refs))
            acc[here, :] = jnp.where(j == 0, 0.0, acc[here, :]) + add

        @pl.when(j == pl.num_programs(0) - 1)
        def _():
            part_ref[...] = acc[...].astype(BF)


def ff_grad_call(p, info, chunks, weights=()):
    width, rows = chunks[0][0].shape
    step = 256
    n = 768 // step
    z2 = lambda j, info: (0, 0)
    per_chunk = [
        pl.BlockSpec((width, rows), z2),
        pl.BlockSpec((width, rows), z2),
        pl.BlockSpec((2, rows, step), lambda j, info: (0, 0, j)),
        pl.BlockSpec((2, rows, step), lambda j, info: (0, 0, j)),
    ]
    specs = [
        pl.BlockSpec((2, 8, width // 8, step), lambda j, info: (0, 0, 0, j)),
        pl.BlockSpec((1, step), lambda j, info: (0, j)),
        pl.BlockSpec((2 * rows, width), z2),
    ]
    shapes = [
        jax.ShapeDtypeStruct((2, 8, width // 8, 768), BF),
        jax.ShapeDtypeStruct((1, 768), F32),
        jax.ShapeDtypeStruct((2 * rows, width), BF),
    ]
    count = 3 if p == 0 else 2
    return pl.pallas_call(
        functools.partial(ff_grad_kernel, p),
        grid_spec=pltpu.PrefetchScalarGridSpec(
            num_scalar_prefetch=1,
            grid=(n,),
            in_specs=per_chunk * 2
            + [pl.BlockSpec((8, width // 8, step), lambda j, info: (0, 0, n + j))] * len(weights),
            out_specs=specs[:count],
            scratch_shapes=[pltpu.VMEM((2 * rows, width), F32)] * (p == 0),
        ),
        out_shape=shapes[:count],
        compiler_params=params(),
        cost_estimate=cost((2 + 2 * (p == 0)) * 2 * rows * width * 1536, (8 + 6 * (p == 0)) * 1024 * 1024),
        name="ff_grad",
    )(info, *chunks[0], *chunks[1], *weights)


def attn_bwd_kernel(last, info, cot_ref, lat_ref, res_ref, own_ref, got_ref, vec_ref,
                    mixed_ref, pt_ref, kv_ref, q_ref, normt_ref, lat_normt_ref, wqo_ref, *refs):
    if last:
        gkv_in, gqo_in, res_grad_ref, dq_ref, dkv_ref, sums_ref, g_own_ref, g_oth_ref, gkv, gqo = refs
    else:
        res_grad_ref, dq_ref, dkv_ref, sums_ref, gkv, gqo = refs
    i = pl.program_id(0)

    @pl.when(i == 0)
    def _():
        gkv[...] = gkv_in[...] if last else jnp.zeros_like(gkv)
        gqo[...] = gqo_in[...] if last else jnp.zeros_like(gqo)
        sums_ref[...] = jnp.zeros_like(sums_ref)

    xhat, rstd = norm_parts(res_ref[...])
    dy = own_ref[...].astype(F32) + got_ref[...].astype(F32)
    dx, dgain, dbias = norm_back(dy, xhat, rstd, vec_ref[4:5, :])
    grad = cot_ref[0].astype(F32) + dx
    res_grad_ref[...] = grad
    sums_ref[0:1, :] += dgain
    sums_ref[1:2, :] += dbias
    low = grad.astype(BF)
    columns = lambda start, stop: wqo_ref[:, :, start:stop].reshape(-1, stop - start)
    lane_lo = lax.broadcasted_iota(jnp.int32, (128, 128), 1) < HEAD_DIM
    row_lo = lax.broadcasted_iota(jnp.int32, (128, 128), 0) < HEAD_DIM
    both = jnp.concatenate([lat_normt_ref[0], low.T], 1)
    none = jnp.zeros((128, 128), BF)
    zeros = jnp.zeros((64, 128), BF)
    total = None
    for p in range(2):
        base = p * 384
        kv = kv_ref[0, :, base : base + 384]
        mixed_grad = dot(low, columns(base + 128, base + 384))
        mg2 = jnp.where(lane_lo, 0.0, mixed_grad[:, 0:128]).astype(BF)
        mg01 = mixed_grad[:, 128:256]
        mg01 = jnp.concatenate([jnp.where(lane_lo, mg01, 0.0), jnp.where(lane_lo, 0.0, mg01)], 0).astype(BF)
        first = dot_t(kv[:, 128:256], mg01)
        second = dot_t(kv[:, 256:384], mg2)
        probs, scores = [], []
        for h, piece in enumerate((first[:, 0:128], first[:, 128:256], second)):
            prob = pt_ref[0, p, :, h * 128 : (h + 1) * 128]
            inner = jnp.sum(piece * prob, 0, keepdims=True)
            scores.append((prob * (piece - inner)).astype(BF))
            probs.append(prob.astype(BF))
        q01 = q_ref[0, p, :, 0:128].astype(F32)
        q01 = jnp.concatenate([jnp.where(lane_lo, q01, 0.0), jnp.where(lane_lo, 0.0, q01)], 0).astype(BF)
        q2 = q_ref[0, p, :, 128:256]
        ds01 = jnp.concatenate(scores[:2], 1)
        dkv_ref[0, :, base : base + 128] = dot(ds01, q01).astype(BF)
        dkv_ref[0, :, base + 128 : base + 256] = dot(jnp.concatenate(probs[:2], 1), mg01).astype(BF)
        dkv_ref[0, :, base + 256 : base + 384] = dot(
            jnp.concatenate([scores[2], probs[2]], 1), jnp.concatenate([q2, mg2], 0)
        ).astype(BF)
        dq01 = dot(kv[:, 0:128].T, ds01)
        dq2 = dot(kv[:, 256:384].T, scores[2])
        dq01 = (jnp.where(row_lo, dq01[:, 0:128], dq01[:, 128:256]) * SCALE).astype(BF)
        dq2 = (jnp.where(row_lo, dq2, 0.0) * SCALE).astype(BF)
        dq_ref[0, p, 0:128, :] = dq01
        dq_ref[0, p, 128:192, :] = dq2[0:64]
        add = dot_t(jnp.concatenate([dq01.T, dq2.T], 1), columns(base, base + 256))
        total = add if total is None else total + add
        right = jnp.concatenate(
            [
                jnp.concatenate([dq01, none], 1),
                jnp.concatenate([dq2, jnp.concatenate([zeros, mixed_ref[0, p, 0:64, :]], 0)], 1),
                jnp.concatenate([none, mixed_ref[0, p, 64:192, :]], 1),
            ],
            0,
        )
        gqo[:, base : base + 384] += dot_t(both, right)
    lat_hat, _ = norm_parts(lat_ref[0].astype(F32))
    sums_ref[2:3, :] += jnp.sum(total * lat_hat, 0, keepdims=True)
    sums_ref[3:4, :] += jnp.sum(total, 0, keepdims=True)
    gkv[...] += dot(normt_ref[0], dkv_ref[0])

    if last:

        @pl.when(i == pl.num_programs(0) - 1)
        def _():
            block = gkv.shape[0] // 8
            for j, k in enumerate(ORDER):
                source = pl.ds(pl.multiple_of((info[4] ^ k) * block, 8), block)
                rows = slice(j * block, (j + 1) * block)
                g_own_ref[rows, 0:384] = gkv[source, 0:384].astype(BF)
                g_own_ref[rows, 384:768] = gqo[source, 0:384].astype(BF)
                g_oth_ref[rows, 0:384] = gkv[source, 384:768].astype(BF)
                g_oth_ref[rows, 384:768] = gqo[source, 384:768].astype(BF)


def attn_bwd_call(first_item, all_items, info, cotangent, latents, residual, own, got, vectors,
                  mixed, pt, kv, q, normt, lat_normt, wqo, grads=None):
    items, keys, _ = kv.shape
    width = normt.shape[1]
    lat_len = q.shape[2]
    last = grads is not None
    one = lambda i, *_: (i, 0)
    three = lambda i, *_: (i, 0, 0)
    mine = lambda i, info: (info[0] * all_items + first_item + i, 0, 0)
    four = lambda i, *_: (i, 0, 0, 0)
    z2 = lambda i, *_: (0, 0)
    flops = items * 2 * (keys * width * 768 + 3 * lat_len * width * 768 + 10 * keys * lat_len * 384)
    out_specs = [
        pl.BlockSpec((lat_len, width), one),
        pl.BlockSpec((1, 2, 192, lat_len), four),
        pl.BlockSpec((1, keys, 768), three),
        pl.BlockSpec((4, width), z2),
        pl.BlockSpec((width, 768), z2),
        pl.BlockSpec((width, 768), z2),
    ]
    out_shape = [
        jax.ShapeDtypeStruct((items * lat_len, width), F32),
        jax.ShapeDtypeStruct((items, 2, 192, lat_len), BF),
        jax.ShapeDtypeStruct((items, keys, 768), BF),
        jax.ShapeDtypeStruct((4, width), F32),
        jax.ShapeDtypeStruct((width, 768), BF if last else F32),
        jax.ShapeDtypeStruct((width, 768), BF if last else F32),
    ]
    return pl.pallas_call(
        functools.partial(attn_bwd_kernel, last),
        grid_spec=pltpu.PrefetchScalarGridSpec(
            num_scalar_prefetch=1,
            grid=(items,),
            in_specs=[
                pl.BlockSpec((1, lat_len, width), mine),
                pl.BlockSpec((1, lat_len, width), mine),
                pl.BlockSpec((lat_len, width), one),
                pl.BlockSpec((lat_len, width), one),
                pl.BlockSpec((lat_len, width), one),
                pl.BlockSpec(vectors.shape, z2),
                pl.BlockSpec((1, 2, 192, lat_len), four),
                pl.BlockSpec((1, 2, keys, 384), four),
                pl.BlockSpec((1, keys, 768), three),
                pl.BlockSpec((1, 2, lat_len, 256), four),
                pl.BlockSpec((1, width, keys), three),
                pl.BlockSpec((1, width, lat_len), three),
                pl.BlockSpec(wqo.shape, lambda i, *_: (0, 0, 0)),
            ]
            + [pl.BlockSpec((width, 768), z2)] * (2 * last),
            out_specs=out_specs,
            scratch_shapes=[pltpu.VMEM((width, 768), F32), pltpu.VMEM((width, 768), F32)] * last,
        ),
        out_shape=out_shape,
        compiler_params=params(),
        cost_estimate=cost(flops, 12 * 1024 * 1024),
        name="attn_bwd",
    )(info, cotangent, latents, residual, own, got, vectors, mixed, pt, kv, q, normt, lat_normt, wqo, *(grads or ()))


def latent_kernel(info, lat_ref, *refs):
    vec_ref, wqo_ref, wqx_ref, out_ref = refs[6:]
    width = vec_ref.shape[1]
    step = out_ref.shape[1]
    per = refs[0].shape[0] // step
    for c in range(2):
        grad_ref, own_ref, got_ref = refs[c], refs[2 + c], refs[4 + c]
        xhat, rstd = norm_parts(lat_ref[c * per : (c + 1) * per].reshape(-1, width).astype(F32))
        dy = spread(own_ref, wqo_ref, True) + spread(got_ref, wqx_ref, True)
        dx, _, _ = norm_back(dy, xhat, rstd, vec_ref[0:1, :])
        out_ref[c * per : (c + 1) * per] = (grad_ref[...] + dx).astype(BF).reshape(per, step, width)


def latent_call(info, latents, grads, own, got, vectors, wqo, wqx):
    half, width = grads[0].shape
    lat_len = latents.shape[1]
    items = 2 * half // lat_len
    z2 = lambda i, info: (0, 0)
    z3 = lambda i, info: (0, 0, 0)
    return pl.pallas_call(
        latent_kernel,
        grid_spec=pltpu.PrefetchScalarGridSpec(
            num_scalar_prefetch=1,
            grid=(1,),
            in_specs=[pl.BlockSpec((items, lat_len, width), lambda i, info: (info[0], 0, 0))]
            + [pl.BlockSpec((half, width), z2)] * 2
            + [pl.BlockSpec(own[0].shape, lambda i, info: (0, 0, 0, 0))] * 4
            + [pl.BlockSpec(vectors.shape, z2), pl.BlockSpec(wqo.shape, z3), pl.BlockSpec(wqx.shape, z3)],
            out_specs=pl.BlockSpec((items, lat_len, width), z3),
        ),
        out_shape=jax.ShapeDtypeStruct((items, lat_len, width), BF),
        compiler_params=params(),
        cost_estimate=cost(4 * items * lat_len * width * 768, 6 * 1024 * 1024),
        name="latent_back",
    )(info, latents, *grads, *own, *got, vectors, wqo, wqx)


def byte_part_kernel(info, dkv_ref, raw_ref, wkv_ref, own_ref, sums_ref, *send_refs):
    part = dot_t(dkv_ref[0], wkv_ref[...].reshape(-1, 768))
    xhat, _ = norm_parts(raw_ref[0].astype(F32))
    half = part.shape[0] // 2
    item = pl.program_id(0)

    @pl.when(item == 0)
    def _():
        sums_ref[...] = jnp.zeros_like(sums_ref)

    sums_ref[0:1, :] += jnp.sum(part * xhat, 0, keepdims=True)
    sums_ref[1:2, :] += jnp.sum(part, 0, keepdims=True)
    low = part.astype(BF)
    for side in range(2):
        for k, send_ref in enumerate(send_refs):

            @pl.when((info[1] == side) & (item == k))
            def _():
                own_ref[0] = low[half * side : half * (side + 1)]
                send_ref[0] = low[half * (1 - side) : half * (2 - side)]


def byte_part_call(info, dkv, raw, wkv):
    items, keys, _ = dkv.shape
    width = raw.shape[2]
    half = keys // 2
    out = lambda i, info: (i, 0, 0)
    whole = lambda i, info: (0, 0, 0)
    return pl.pallas_call(
        byte_part_kernel,
        grid_spec=pltpu.PrefetchScalarGridSpec(
            num_scalar_prefetch=1,
            grid=(items,),
            in_specs=[
                pl.BlockSpec((1, keys, 768), out),
                pl.BlockSpec((1, keys, width), out),
                pl.BlockSpec(wkv.shape, whole),
            ],
            out_specs=[
                pl.BlockSpec((1, half, width), out),
                pl.BlockSpec((2, width), lambda i, info: (0, 0)),
            ]
            + [pl.BlockSpec((1, half, width), whole)] * items,
        ),
        out_shape=[
            jax.ShapeDtypeStruct((items, half, width), BF),
            jax.ShapeDtypeStruct((2, width), F32),
        ]
        + [jax.ShapeDtypeStruct((1, half, width), BF)] * items,
        compiler_params=params(),
        cost_estimate=cost(items * keys * width * 768 * 2, 6 * 1024 * 1024),
        name="byte_part",
    )(info, dkv, raw, wkv)


def byte_back_kernel(info, part_ref, raw_ref, vec_ref, *refs):
    got_refs, (own_ref, oth_ref) = refs[:-2], refs[-2:]
    half = part_ref.shape[1]
    quarter = half // 2
    got = [ref[k] for ref in got_refs for k in range(ref.shape[0])]
    for k, piece in enumerate(got):
        dy = part_ref[k].astype(F32) + piece.astype(F32)
        xhat, rstd = norm_parts(raw_ref[k].astype(F32))
        dx, _, _ = norm_back(dy, xhat, rstd, vec_ref[2:3, :])
        dx = dx.astype(BF)

        @pl.when(info[0] == 0)
        def _():
            own_ref[k] = dx[:quarter]
            oth_ref[k] = dx[quarter:]

        @pl.when(info[0] != 0)
        def _():
            own_ref[k] = dx[quarter:]
            oth_ref[k] = dx[:quarter]


def byte_back_call(info, part, got, raw, vectors):
    items, half, width = part.shape
    z3 = lambda i, info: (0, 0, 0)
    return pl.pallas_call(
        byte_back_kernel,
        grid_spec=pltpu.PrefetchScalarGridSpec(
            num_scalar_prefetch=1,
            grid=(1,),
            in_specs=[
                pl.BlockSpec((items, half, width), z3),
                pl.BlockSpec((items, half, width), lambda i, info: (0, info[1], 0)),
                pl.BlockSpec(vectors.shape, lambda i, info: (0, 0)),
                *(pl.BlockSpec(piece.shape, z3) for piece in got),
            ],
            out_specs=[pl.BlockSpec((items, half // 2, width), z3)] * 2,
        ),
        out_shape=[jax.ShapeDtypeStruct((items, half // 2, width), BF)] * 2,
        compiler_params=params(),
        cost_estimate=cost(items * half * width * 20, 4 * 1024 * 1024),
        name="byte_back",
    )(info, part, raw, vectors, *got)


def body(
    latents, byte_array, cotangent, patch_count, text_len,
    inner_weight, inner_moment, inner_square,
    output_weight, output_moment, output_square,
    expand_weight, expand_moment, expand_square,
    reduce_weight, reduce_moment, reduce_square,
    expand_bias, bias_moment, bias_square,
    norm_vectors, vector_moment, vector_square,
):
    item_count, lat_len, width = latents.shape
    keys = byte_array.shape[1]
    items = item_count // 2
    n = lax.axis_size("dp")
    head = lax.axis_index("head")
    core, xside = head & 1, head >> 1
    true_rows = keys // lax.axis_size("head")
    pad_rows = -(-true_rows // 32) * 32
    pad_keys = 4 * pad_rows
    quick = n == 8
    place = lax.axis_index("dp") if quick else jnp.int32(0)
    info = jnp.stack([core, xside, jnp.int32(true_rows), jnp.int32(items), place]).astype(jnp.int32)
    half_items = items // 2

    low_inner = inner_weight.astype(BF)
    wq, wk, wv = low_inner[0], low_inner[1], low_inner[2]
    wo = output_weight.T.astype(BF)
    pack = jnp.concatenate(
        [wk[:, :128], wv[:, :128], wk[:, 128:], wv[:, 128:], wq[:, :128], wq[:, 128:], wo[:, 128:], wo[:, :128]], 1
    )
    ff_pack = jnp.concatenate([expand_weight.astype(BF), reduce_weight.T.astype(BF)], 1)
    normalise = lambda c, byte_array: norm_call(
        c * half_items, items, info, byte_array, latents, norm_vectors, half_items, pad_keys
    )
    flip = lambda value: swap(value, "head", 1)
    over = lambda value, mask: swap(value, "dp", mask)
    grouped = lambda p: [flip(jnp.concatenate([p[k] for k in group], 0)) for group in GROUPS]
    if quick:
        g = {0: pack, 4: over(pack, 4), 2: over(pack, 2), 1: over(pack, 1)}
        norm0 = normalise(0, byte_array)
        g[4], g[2], g[1], *norm0 = tie(g[4], g[2], g[1], *norm0)
        g[6], g[5], g[3] = over(g[4], 2), over(g[4], 1), over(g[2], 1)
        g[6], g[5], g[3], byte_later, ff_pack = tie(g[6], g[5], g[3], byte_array, ff_pack)
        f = {0: ff_pack, 4: over(ff_pack, 4), 2: over(ff_pack, 2), 1: over(ff_pack, 1)}
        g[7] = over(g[6], 1)
        norm1 = normalise(1, byte_later)
        g[7], f[4], f[2], f[1], *norm1 = tie(g[7], f[4], f[2], f[1], *norm1)
        f[6], f[5], f[3] = over(f[4], 2), over(f[4], 1), over(f[2], 1)
        pieces = [g[k] for k in range(8)] + grouped(g)
    else:
        norm0, norm1 = normalise(0, byte_array), normalise(1, byte_array)
        blocks = lax.all_gather(pack, "dp", axis=0, tiled=True).reshape(8, width // 8, 768)
        g = [blocks[k] for k in range(8)]
        pieces = g + grouped(g)
        blocks = lax.all_gather(ff_pack, "dp", axis=0, tiled=True).reshape(8, width // 8, 1536)
        f = [blocks[k] for k in range(8)]
    norm, normt, raw, lat_norm, lat_normt = zip(norm0, norm1)
    bias_other = flip(expand_bias)

    crossed = swap(jnp.concatenate([g[k][:, 384:] for k in range(8)], 0), "head", 2)

    attend = lambda c, weights: attn_fwd_call(
        c * half_items, info, patch_count, text_len, norm[c], lat_norm[c], weights
    )
    mixed0, *kept0, wkv, wqo = attend(0, pieces)
    got0 = swap(mixed0, "head", 2)
    if quick:
        first_flip = flip(jnp.concatenate([f[k] for k in GROUPS[0]], 0))
        wkv, f[6], f[5], f[3], first_flip, bias_other, crossed = tie(
            wkv, f[6], f[5], f[3], first_flip, bias_other, crossed
        )
        f[7] = over(f[6], 1)
        second_flip = flip(jnp.concatenate([f[k] for k in GROUPS[1]], 0))
    crossed = [crossed, flip(crossed)]
    mixed1, *kept1 = attend(1, [wkv, wqo])
    mixed1, got0, crossed[1] = tie(mixed1, got0, crossed[1])
    got1 = swap(mixed1, "head", 2)
    if quick:
        mixed1, second_flip, f[7] = tie(mixed1, second_flip, f[7])
        ff_pieces = [f[k] for k in range(8)] + [first_flip, second_flip, flip(f[7])]
    else:
        ff_pieces = f + grouped(f)

    bias_both = jnp.stack([expand_bias, bias_other])
    feed = lambda c, mixed, got, weights: ff_core_call(
        c, info, latents, cotangent, mixed, got, norm_vectors, bias_both, wqo, weights
    )
    res0, *ff0, npart0, cot_sum0, ff_own, ff_oth, wqx = feed(0, mixed0, got0, [*ff_pieces, *crossed])
    npart0, got1 = tie(npart0, got1)
    ngot0 = swap(npart0, "head", 2)
    res1, *ff1, npart1, cot_sum1 = feed(1, mixed1, got1, [ff_own, ff_oth, wqx])
    npart1, ngot0 = tie(npart1, ngot0)
    ngot1 = swap(npart1, "head", 2)
    g_oth, bias_oth = ff_grad_call(1, info, [ff0, ff1])
    g_oth, ngot0, ff1[3] = tie(g_oth, ngot0, ff1[3])
    g_got = flip(g_oth)
    g_own, bias_own, mlp_part = ff_grad_call(0, info, [ff0, ff1], [ff_own, ff_oth])
    g_own, ngot0, ngot1, g_got = tie(g_own, ngot0, ngot1, g_got)
    bias_own = bias_own + flip(bias_oth)
    pair_of = lambda kind, part: (g_own[kind, part], g_got[kind, part])
    first_steps = [plus(*pair_of(kind, slice(0, 4))) for kind in range(2)]

    attend_back = lambda c, res, npart, ngot, mixed, kept, grads: attn_bwd_call(
        c * half_items, items, info, cotangent, latents, res, npart, ngot,
        norm_vectors, mixed, *kept, normt[c], lat_normt[c], wqo, grads
    )
    res0, ngot0, bias_own, mlp_part, *first_steps = tie(res0, ngot0, bias_own, mlp_part, *first_steps)
    mlp_got = swap(mlp_part, "head", 2)
    if quick:
        ff_got = [over(first_steps[0], 1), over(first_steps[1], 2)]
    rgrad0, dq0, dkv0, sums0, *grads = attend_back(0, res0, npart0, ngot0, mixed0, kept0, None)
    bown0, bsums0, *bsend0 = byte_part_call(info, dkv0, raw[0], wkv)
    res1, bsend0[0], mlp_got = tie(res1, bsend0[0], mlp_got)
    bgot00 = swap(bsend0[0], "head", 2)
    if quick:
        res1, *ff_got = tie(res1, *ff_got)
        second_steps = [plus(*pair_of(kind, slice(4, 6)), ff_got[kind][0:2]) for kind in range(2)]
        ff_more = [over(second_steps[0], 2), over(second_steps[1], 1)]
    rgrad1, dq1, dkv1, sums1, g_attn, g_attn_oth = attend_back(1, res1, npart1, ngot1, mixed1, kept1, grads)
    g_attn_oth, bgot00, bsend0[1] = tie(g_attn_oth, bgot00, bsend0[1])
    bgot01 = swap(bsend0[1], "head", 2)
    if quick:
        g_attn_oth, *ff_more = tie(g_attn_oth, *ff_more)
        rest = [(*pair_of(kind, part), ff_got[kind][part - 4], ff_more[kind][part - 6]) for part in (6, 7) for kind in range(2)]
        third_step = jnp.concatenate([plus(*rest[0]), plus(*rest[1])], 0)
    else:
        g_ff = g_own.astype(F32) + g_got.astype(F32)
        g_ff = jnp.stack([g_ff[kind, order.index(k)] for kind, order in enumerate(FF_ORDERS) for k in range(8)])
        g_ff = g_ff.reshape(2, width, 768)
        g_ff = lax.psum_scatter(g_ff, "dp", scatter_dimension=1, tiled=True).reshape(-1, 768)
    u = g_attn.reshape(8, width // 8, 768)
    v = flip(g_attn_oth).reshape(8, width // 8, 768)
    u75 = plus(u[0:2], v[0:2])

    if quick:
        u31 = plus(u[2:4], v[2:4])
        dkv1, u75, u31, third_step = tie(dkv1, u75, u31, third_step)
        third = 5 * third_step.shape[0] // 12
        last_got = [over(third_step[:third], 4)]
        y75 = over(u75, 1)
        y31 = over(u31, 1)
    bown1, bsums1, *bsend1 = byte_part_call(info, dkv1, raw[1], wkv)
    if quick:
        bsend1[0], y75, bgot01, dq0, dq1, last_got[0] = tie(bsend1[0], y75, bgot01, dq0, dq1, last_got[0])
        u64 = plus(u[4:6], v[4:6], y75)
        last_got.append(over(third_step[third : 2 * third], 4))
        z6 = over(u64[0], 2)
    lgot0, lgot1 = swap(dq0, "head", 2), swap(dq1, "head", 2)
    side0 = list(byte_back_call(info, bown0, [bgot00, bgot01], raw[0], norm_vectors))

    residual = jnp.concatenate([res0, res1], 0)
    block_mine = residual + (mlp_part.astype(F32) + mlp_got.astype(F32)) + norm_vectors[6]
    block_mine = block_mine.astype(BF).reshape(items, lat_len, width)

    byte_side = lambda c, own, got: byte_back_call(info, own, got, raw[c], norm_vectors)
    if quick:
        block_mine, z6, y31, bsend1[0], lgot0, lgot1, last_got[1], side0[0] = tie(
            block_mine, z6, y31, bsend1[0], lgot0, lgot1, last_got[1], side0[0]
        )
        last_got.append(over(third_step[2 * third :], 4))
        z4 = over(plus(u64[1], z6), 4)
        z2 = over(plus(u[6], v[6], y31[0]), 2)
    bgot10 = swap(bsend1[0], "head", 2)
    lat_mine = latent_call(
        info, latents, [rgrad0, rgrad1], [dq0, dq1], [lgot0, lgot1], norm_vectors, wqo, wqx
    )
    block_output = pair_call(info, [block_mine], [flip(block_mine)], lat_len)
    if quick:
        block_output, lat_mine, last_got[2], z4, z2 = tie(block_output, lat_mine, last_got[2], z4, z2)
        g_ff = jnp.concatenate([sum(x.astype(F32) for x in rest[2 + kind]) for kind in range(2)], 0)
        g_ff = g_ff + jnp.concatenate(last_got, 0).astype(F32)
        ff_squares = jnp.sum(g_ff * g_ff)
        bgot10, bsend1[1] = tie(bgot10, bsend1[1])
        terms = [u[7], v[7], y31[1], z2, z4]
    else:
        g_attn = u.astype(F32) + v.astype(F32)
        g_attn = jnp.concatenate([g_attn[ORDER.index(k)] for k in range(8)], 0)
        terms = [lax.psum_scatter(g_attn, "dp", scatter_dimension=0, tiled=True)]
        ff_squares = jnp.sum(g_ff * g_ff)
    bgot11 = swap(bsend1[1], "head", 2)
    side1 = byte_side(1, bown1, [bgot10, bgot11])
    g_attn, load = collect_call(
        info, terms, [sums0, sums1, bsums0, bsums1, cot_sum0, cot_sum1, bias_own, ff_squares.reshape(1, 1)]
    )
    latent_gradient = pair_call(info, [lat_mine], [flip(lat_mine)], lat_len)
    beside = [lambda: latent_gradient, None, lambda: side1]
    outs = []
    mask = n // 2
    while mask:
        hop = over(load, mask)
        make = beside.pop(0) if beside else None
        if make:
            hop, out = lax.optimization_barrier((hop, make()))
            outs.append(out)
        load = load + hop
        mask //= 2
    latent_gradient = outs[0]
    bias_sum = load[7:8]
    squares = load[8:9] + jnp.sum(bias_sum * bias_sum)
    load = jnp.concatenate([load[:7], squares], 0)
    load = load + swap(load, "head", 1)
    by_row = rows_call(info, [side0[0], outs[1][0]], [flip(side0[1]), flip(outs[1][1])], true_rows)
    hop, by_row = tie(swap(load, "head", 2), by_row)
    byte_gradient = by_row.transpose(1, 0, 2)
    load = load + hop

    *news, grad_norm = adam_call(
        load,
        g_attn,
        g_ff,
        [
            inner_weight, inner_moment, inner_square, output_weight, output_moment, output_square,
            expand_weight, expand_moment, expand_square, reduce_weight.T, reduce_moment.T, reduce_square.T,
            norm_vectors, vector_moment, vector_square,
        ],
    )
    factor = CLIP_RATE * math.sqrt(4 * D * D + 2 * D * FF + FF + 7 * D) / grad_norm[0, 0]
    bias_new = adamw(expand_bias, bias_moment, bias_square, factor * bias_sum[0], 0.3, 0.0)
    news[9:12] = [new.T for new in news[9:12]]
    return (
        block_output, latent_gradient, byte_gradient, *news[:12], *bias_new, *news[12:], grad_norm[0, 0]
    )


def solution(mesh):
    rows, cols = P("dp", "head"), P("head", "dp")
    inner, items = P(None, "dp", "head"), P("dp", None, None)
    weights = (inner,) * 3 + (cols,) * 3 + (rows,) * 3 + (cols,) * 3 + (P("head"),) * 3 + (P(),) * 3
    return jax.shard_map(
        body,
        mesh=mesh,
        in_specs=(items, items, items, P("dp"), P("dp")) + weights,
        out_specs=(items, items, P("dp", "head", None)) + weights + (P(),),
        check_vma=False,
    )
```

```python
import functools
import math

import jax
import jax.numpy as jnp
from jax import lax
from jax.experimental import pallas as pl
from jax.experimental.pallas import tpu as pltpu
from jax.sharding import PartitionSpec as P

D = 768
HEAD_DIM = 64
FF = 3072
PATCHES = 576
STEP = 5

NEG_FILL = -1000000000.0
BETA = 0.5
ADAM_EPS = 1e-08
DECAY = 0.01
CLIP_RATE = 0.01
LN_EPS = 1e-05
SCALE = 1.0 / math.sqrt(HEAD_DIM)
BF = jnp.bfloat16
F32 = jnp.float32
VMEM_LIMIT = 20 * 1024 * 1024


def dot(a, b):
    return lax.dot_general(a, b, (((1,), (0,)), ((), ())), preferred_element_type=F32)


def dot_t(a, b):
    return lax.dot_general(a, b, (((1,), (1,)), ((), ())), preferred_element_type=F32)


def norm_parts(rows):
    centred = rows - jnp.mean(rows, -1, keepdims=True)
    rstd = lax.rsqrt(jnp.mean(centred * centred, -1, keepdims=True) + LN_EPS)
    return centred * rstd, rstd


def norm_back(dy, xhat, rstd, gain):
    scaled = dy * gain
    first = jnp.mean(scaled, -1, keepdims=True)
    second = jnp.mean(scaled * xhat, -1, keepdims=True)
    dx = rstd * (scaled - first - xhat * second)
    return dx, jnp.sum(dy * xhat, 0, keepdims=True), jnp.sum(dy, 0, keepdims=True)


def swap(value, axis, mask):
    size = lax.axis_size(axis)
    return lax.ppermute(value, axis, [(i, i ^ mask) for i in range(size)])


def tie(*values):
    return lax.optimization_barrier(tuple(values))


def plus(*values):
    return sum(value.astype(F32) for value in values).astype(BF)


def adamw(weight, moment, square, gradient, rate, decay_rate):
    moment_new = BETA * moment + (1.0 - BETA) * gradient
    square_new = BETA * square + (1.0 - BETA) * gradient * gradient
    correction = 1.0 - BETA**STEP
    step_dir = moment_new * (1.0 / correction) / (jnp.sqrt(square_new * (1.0 / correction)) + ADAM_EPS)
    return (weight - rate * (step_dir + decay_rate * weight), moment_new, square_new)


def params(**kw):
    return pltpu.CompilerParams(vmem_limit_bytes=VMEM_LIMIT, **kw)


def cost(flops, nbytes, trans=0):
    return pl.CostEstimate(flops=flops, bytes_accessed=nbytes, transcendentals=trans)


GROUPS = ((0, 4, 2, 1), (6, 5, 3), (7,))


def assemble(info, parts, outs, splits):
    rows = parts[0].shape[0]
    blocks = [(k, 0, parts[k], 0) for k in range(8)]
    for part, group in zip(parts[8:], GROUPS):
        blocks += [(k, 1, part, i * rows) for i, k in enumerate(group)]
    for k, c, part, first in blocks:
        for out, start, stop, offset in splits[c]:
            outs[out][info[4] ^ k, :, offset : offset + stop - start] = part[first : first + rows, start:stop]


ORDER = (7, 5, 3, 1, 6, 4, 2, 0)
FF_ORDERS = ((7, 3, 5, 1, 6, 2, 4, 0), (7, 3, 6, 2, 5, 1, 4, 0))


def pair_kernel(chunks, info, *refs):
    out = refs[-1]
    rows = out.shape[1]
    per = refs[0].shape[0]
    for side in range(2):
        first = (info[0] ^ side) * (chunks * per)
        for c in range(chunks):
            ref = refs[side * chunks + c]
            for k in range(per):
                out[first + c * per + k] = ref[k, :rows, :]


def pair_call(info, own, other, rows):
    per, _, width = own[0].shape
    chunks = len(own)
    return pl.pallas_call(
        functools.partial(pair_kernel, chunks),
        grid_spec=pltpu.PrefetchScalarGridSpec(
            num_scalar_prefetch=1,
            grid=(1,),
            in_specs=[pl.BlockSpec(own[0].shape, lambda i, info: (0, 0, 0))] * (2 * chunks),
            out_specs=pl.BlockSpec((2 * chunks * per, rows, width), lambda i, info: (0, 0, 0)),
        ),
        out_shape=jax.ShapeDtypeStruct((2 * chunks * per, rows, width), BF),
        compiler_params=params(),
        cost_estimate=cost(1, 4 * chunks * per * rows * width * 2),
        name="pair",
    )(info, *own, *other)


def rows_kernel(info, *refs):
    blocks, out = refs[:4], refs[4]
    true_rows, step = out.shape[0], 32
    for core in range(2):

        @pl.when(info[0] == core)
        def _():
            order = blocks if core == 0 else (*blocks[2:], *blocks[:2])
            for first in range(0, true_rows, step):
                count = min(step, true_rows - first)
                items = [ref[k, first : first + step, :].astype(F32) for ref in order for k in range(ref.shape[0])]
                by_row = pltpu.einshape("abc->bac", jnp.stack(items, 0))
                out[first : first + count] = by_row[:count].astype(BF)


def rows_call(info, own, other, rows):
    per, _, width = own[0].shape
    return pl.pallas_call(
        rows_kernel,
        grid_spec=pltpu.PrefetchScalarGridSpec(
            num_scalar_prefetch=1,
            grid=(1,),
            in_specs=[pl.BlockSpec(own[0].shape, lambda i, info: (0, 0, 0))] * 4,
            out_specs=pl.BlockSpec((rows, 4 * per, width), lambda i, info: (0, 0, 0)),
        ),
        out_shape=jax.ShapeDtypeStruct((rows, 4 * per, width), BF),
        compiler_params=params(),
        cost_estimate=cost(1, 16 * per * rows * width),
        name="rows",
    )(info, *own, *other)


def collect_kernel(count, info, *refs):
    terms, (sums0, sums1, bytes0, bytes1, cot0, cot1, bias, squares, grad_ref, load_ref) = refs[:count], refs[count:]
    grad = sum(ref[...].astype(F32) for ref in terms)
    grad_ref[...] = grad
    once = jnp.where(info[1] == 0, 1.0, 0.0)
    sums = sums0[...] + sums1[...]
    load_ref[0:2, :] = sums[2:4]
    load_ref[2:4, :] = bytes0[...] + bytes1[...]
    load_ref[4:6, :] = sums[0:2] * once
    load_ref[6:7, :] = (cot0[...] + cot1[...]) * once
    load_ref[7:8, :] = bias[...]
    total = jnp.sum(jnp.sum(grad * grad, 0, keepdims=True), 1, keepdims=True) + squares[...]
    load_ref[8:9, :] = jnp.broadcast_to(total, (1, load_ref.shape[1]))


def collect_call(info, terms, small):
    rows, width = terms[0].shape
    whole = lambda i, info: (0, 0)
    return pl.pallas_call(
        functools.partial(collect_kernel, len(terms)),
        grid_spec=pltpu.PrefetchScalarGridSpec(
            num_scalar_prefetch=1,
            grid=(1,),
            in_specs=[pl.BlockSpec(x.shape, whole) for x in (*terms, *small)],
            out_specs=[pl.BlockSpec((rows, width), whole), pl.BlockSpec((9, width), whole)],
        ),
        out_shape=[jax.ShapeDtypeStruct((rows, width), F32), jax.ShapeDtypeStruct((9, width), F32)],
        compiler_params=params(),
        cost_estimate=cost(1, 16 * rows * width),
        name="collect",
    )(info, *terms, *small)


def adam_kernel(load_ref, attn_ref, ff_ref, *refs):
    inner, output, expand, reduce, vector = (refs[3 * k : 3 * k + 3] for k in range(5))
    outs = refs[15:]
    load = load_ref[...]
    vectors = load[0:7]
    total = load[7:8, 0:1] + jnp.sum(jnp.sum(vectors * vectors, 0, keepdims=True), 1, keepdims=True)
    norm = jnp.sqrt(total)
    outs[15][...] = norm
    factor = CLIP_RATE * math.sqrt(4 * D * D + 2 * D * FF + FF + 7 * D) / norm

    def update(which, at, grad, rate, decay_rate):
        state = refs[3 * which : 3 * which + 3]
        for ref, new in zip(
            outs[3 * which : 3 * which + 3],
            adamw(*(ref[at] for ref in state), factor * grad, rate, decay_rate),
        ):
            ref[at] = new

    low, high = slice(0, 128), slice(128, 192)
    every = slice(None)
    for matrix, first, second in ((0, 384, 512), (1, 0, 256), (2, 128, 320)):
        update(0, (matrix, every, low), attn_ref[:, first : first + 128], 0.03, DECAY)
        update(0, (matrix, every, high), attn_ref[:, second : second + 64], 0.03, DECAY)
    update(1, (low, every), attn_ref[:, 640:768].T, 0.3, DECAY)
    update(1, (high, every), attn_ref[:, 512:640].T[64:128], 0.3, DECAY)
    rows = expand[0].shape[0]
    update(2, Ellipsis, ff_ref[0:rows, :], 0.03, DECAY)
    update(3, Ellipsis, ff_ref[rows : 2 * rows, :], 0.015, DECAY)
    update(4, Ellipsis, vectors, 0.3, 0.0)


def adam_call(load, attn, ff, state):
    shapes = [jax.ShapeDtypeStruct(x.shape, F32) for x in state] + [jax.ShapeDtypeStruct((1, 1), F32)]
    return pl.pallas_call(
        adam_kernel,
        out_shape=shapes,
        compiler_params=params(),
        cost_estimate=cost(1, sum(x.size for x in state) * 4 * 2),
        name="adam",
    )(load, attn, ff, *state)


def norm_kernel(info, byte_ref, lat_ref, vec_ref, norm_ref, normt_ref, raw_ref, lat_norm_ref, lat_normt_ref, scr):
    groups, true_rows, pad_rows = 4, byte_ref.shape[1] // 4, norm_ref.shape[1] // 4
    keys = byte_ref.shape[1]
    scr[pl.ds(0, keys), :] = byte_ref[0].astype(F32)
    gain, bias = vec_ref[2:3, :], vec_ref[3:4, :]
    keep = lax.broadcasted_iota(jnp.int32, (pad_rows, 1), 0) < true_rows
    for g in range(groups):
        rows = jnp.where(keep, scr[pl.ds(g * true_rows, pad_rows), :], 0.0)
        xhat, _ = norm_parts(rows)
        normed = jnp.where(keep, xhat * gain + bias, 0.0)
        here = pl.ds(g * pad_rows, pad_rows)
        raw_ref[0, here, :] = rows.astype(BF)
        norm_ref[0, here, :] = normed.astype(BF)
    normt_ref[0] = norm_ref[0].T
    xhat, _ = norm_parts(lat_ref[0].astype(F32))
    lat_norm = (xhat * vec_ref[0:1, :] + vec_ref[1:2, :]).astype(BF)
    lat_norm_ref[0] = lat_norm
    lat_normt_ref[0] = lat_norm.T


def norm_call(first_item, all_items, info, byte_array, latents, vectors, items, pad_keys):
    _, keys, width = byte_array.shape
    lat_len = latents.shape[1]
    here = lambda i, info: (info[0] * all_items + first_item + i, 0, 0)
    out = lambda i, info: (i, 0, 0)
    return pl.pallas_call(
        norm_kernel,
        grid_spec=pltpu.PrefetchScalarGridSpec(
            num_scalar_prefetch=1,
            grid=(items,),
            in_specs=[
                pl.BlockSpec((1, keys, width), here),
                pl.BlockSpec((1, lat_len, width), here),
                pl.BlockSpec(vectors.shape, lambda i, info: (0, 0)),
            ],
            out_specs=[
                pl.BlockSpec((1, pad_keys, width), out),
                pl.BlockSpec((1, width, pad_keys), out),
                pl.BlockSpec((1, pad_keys, width), out),
                pl.BlockSpec((1, lat_len, width), out),
                pl.BlockSpec((1, width, lat_len), out),
            ],
            scratch_shapes=[pltpu.VMEM((keys + 40, width), F32)],
        ),
        out_shape=[
            jax.ShapeDtypeStruct((items, pad_keys, width), BF),
            jax.ShapeDtypeStruct((items, width, pad_keys), BF),
            jax.ShapeDtypeStruct((items, pad_keys, width), BF),
            jax.ShapeDtypeStruct((items, lat_len, width), BF),
            jax.ShapeDtypeStruct((items, width, lat_len), BF),
        ],
        compiler_params=params(),
        cost_estimate=cost(items * keys * width * 20, items * keys * width * 8),
        name="norms",
    )(info, byte_array, latents, vectors)


SPLITS = (((0, 0, 384, 0), (1, 384, 768, 0)), ((0, 0, 384, 384), (1, 384, 768, 384)))


def attn_fwd_kernel(first_item, info, count_ref, text_ref, norm_ref, lat_ref, *refs):
    if first_item == 0:
        pieces, (mixed_ref, pt_ref, kv_ref, q_ref, wkv_ref, wqo_ref) = refs[:11], refs[11:]

        @pl.when(pl.program_id(0) == 0)
        def _():
            assemble(info, pieces, (wkv_ref, wqo_ref), SPLITS)

    else:
        wkv_ref, wqo_ref, mixed_ref, pt_ref, kv_ref, q_ref = refs
    wkv = wkv_ref[...].reshape(-1, 768)
    columns = lambda start, stop: wqo_ref[:, :, start:stop].reshape(-1, stop - start)
    item = info[0] * info[3] + first_item + pl.program_id(0)
    patches, texts = count_ref[item], text_ref[item]
    keys = norm_ref.shape[1]
    pad_rows = keys // 4
    true_rows = info[2]
    row = lax.broadcasted_iota(jnp.int32, (keys, 128), 0)
    group = sum(((row >= pad_rows * g).astype(jnp.int32) for g in range(1, 4)))
    inner = row - group * pad_rows
    slot = inner + group * true_rows
    valid = ((slot < PATCHES) & (slot < patches)) | ((slot >= PATCHES) & (slot - PATCHES < texts))
    valid = valid & (inner < true_rows)
    lane_lo = lax.broadcasted_iota(jnp.int32, (128, 128), 1) < HEAD_DIM
    row_lo = lax.broadcasted_iota(jnp.int32, (128, 128), 0) < HEAD_DIM
    kv_all = dot(norm_ref[0], wkv).astype(BF)
    kv_ref[0] = kv_all
    lat_norm = lat_ref[0]
    for p in range(2):
        kv = kv_all[:, p * 384 : (p + 1) * 384]
        base = p * 384
        q = dot(lat_norm, columns(base, base + 256)) * SCALE
        q01, q2 = q[:, :128], jnp.where(lane_lo, q[:, 128:], 0.0).astype(BF)
        q_ref[0, p, :, 0:128] = q01.astype(BF)
        q_ref[0, p, :, 128:256] = q2
        stacked = jnp.concatenate([jnp.where(lane_lo, q01, 0.0), jnp.where(lane_lo, 0.0, q01)], 0).astype(BF)
        first = dot_t(kv[:, 0:128], stacked)
        second = dot_t(kv[:, 256:384], q2)
        pieces = []
        for piece in (first[:, 0:128], first[:, 128:256], second):
            piece = jnp.where(valid, piece, NEG_FILL)
            top = jnp.max(piece, 0, keepdims=True)
            expo = jnp.exp(piece - top)
            pieces.append(expo * (1.0 / jnp.sum(expo, 0, keepdims=True)))
        for h in range(3):
            pt_ref[0, p, :, h * 128 : (h + 1) * 128] = pieces[h]
        low01 = jnp.concatenate([pieces[0].astype(BF), pieces[1].astype(BF)], 1)
        o01 = dot(kv[:, 128:256].T, low01)
        o2 = dot(kv[:, 256:384].T, pieces[2].astype(BF))
        mixed_ref[0, p, 0:64, :] = o2[64:128].astype(BF)
        mixed_ref[0, p, 64:192, :] = jnp.where(row_lo, o01[:, 0:128], o01[:, 128:256]).astype(BF)


def attn_fwd_call(first_item, info, counts, texts, norm, lat_norm, weights):
    items, keys, width = norm.shape
    lat_len = lat_norm.shape[1]
    out3 = lambda i, *_: (i, 0, 0)
    out4 = lambda i, *_: (i, 0, 0, 0)
    given = [pl.BlockSpec(w.shape, lambda i, *_, d=w.ndim: (0,) * d) for w in weights]
    made = [pl.BlockSpec((8, width // 8, 768), lambda i, *_: (0, 0, 0))] * (2 * (first_item == 0))
    flops = items * 2 * (keys * width * 768 + lat_len * width * 768 + 4 * keys * lat_len * 384)
    return pl.pallas_call(
        functools.partial(attn_fwd_kernel, first_item),
        grid_spec=pltpu.PrefetchScalarGridSpec(
            num_scalar_prefetch=3,
            grid=(items,),
            in_specs=[
                pl.BlockSpec((1, keys, width), out3),
                pl.BlockSpec((1, lat_len, width), out3),
                *given,
            ],
            out_specs=[
                pl.BlockSpec((1, 2, 192, lat_len), out4),
                pl.BlockSpec((1, 2, keys, 384), out4),
                pl.BlockSpec((1, keys, 768), out3),
                pl.BlockSpec((1, 2, lat_len, 256), out4),
                *made,
            ],
        ),
        out_shape=[
            jax.ShapeDtypeStruct((items, 2, 192, lat_len), BF),
            jax.ShapeDtypeStruct((items, 2, keys, 384), F32),
            jax.ShapeDtypeStruct((items, keys, 768), BF),
            jax.ShapeDtypeStruct((items, 2, lat_len, 256), BF),
        ]
        + [jax.ShapeDtypeStruct((8, width // 8, 768), BF)] * len(made),
        compiler_params=params(),
        cost_estimate=cost(flops, 8 * 1024 * 1024, items * keys * 768),
        name="attn_fwd",
    )(info, counts, texts, norm, lat_norm, *weights)


def spread(mixed_ref, w_ref, queries):
    zeros = jnp.zeros((64, mixed_ref.shape[3]), BF)
    total = []
    for item in range(mixed_ref.shape[0]):
        rows = None
        for p in range(2):
            mixed = mixed_ref[item, p]
            parts = (mixed[0:128], mixed[128:192], zeros) if queries else (zeros, mixed[0:64], mixed[64:192])
            first = p * 384 + 128 * (not queries)
            columns = w_ref[:, :, first : first + 256].reshape(-1, 256)
            add = dot_t(jnp.concatenate(parts, 0).T, columns)
            rows = add if rows is None else rows + add
        total.append(rows)
    return jnp.concatenate(total, 0)


def ff_core_kernel(chunk, info, lat_ref, cot_ref, own_ref, got_ref, vec_ref, bias_ref, wqo_ref, *refs):
    if chunk == 0:
        pieces, crossed = refs[:11], refs[11:13]
        res_ref, normt_ref, cott_ref, hidden_ref, pre_ref, part_ref, cot_sum_ref, *weights, wqx_ref = refs[13:]
        assemble(info, pieces, weights, (((0, 0, 1536, 0),), ((1, 0, 1536, 0),)))
        rows = wqx_ref.shape[1]
        for k in range(8):
            for c in range(2):
                wqx_ref[info[4] ^ k, :, 384 * c : 384 * (c + 1)] = crossed[c][k * rows : (k + 1) * rows, :]
    else:
        weights, wqx_ref = refs[:2], refs[2]
        res_ref, normt_ref, cott_ref, hidden_ref, pre_ref, part_ref, cot_sum_ref = refs[3:]
    width = vec_ref.shape[1]
    flat = lambda ref: ref[...].reshape(-1, width).astype(F32)
    residual = flat(lat_ref) + (spread(own_ref, wqo_ref, False) + spread(got_ref, wqx_ref, False))
    res_ref[...] = residual
    xhat, _ = norm_parts(residual)
    normed = (xhat * vec_ref[4:5, :] + vec_ref[5:6, :]).astype(BF)
    cot = cot_ref[...].reshape(-1, width)
    total = None
    step = 256
    for p, w_ref in enumerate(weights):
        columns = lambda start: w_ref[:, :, start : start + step].reshape(-1, step)
        for j in range(768 // step):
            cols = slice(j * step, (j + 1) * step)
            w1 = columns(j * step)
            pre = dot(normed, w1) + bias_ref[p : p + 1, cols]
            back = dot(cot, columns(768 + j * step))
            cdf = 0.5 + 0.5 * lax.erf(pre * math.sqrt(0.5))
            pdf = jnp.exp(pre * pre * -0.5) * (1.0 / math.sqrt(2.0 * math.pi))
            hidden_ref[p, :, cols] = (pre * cdf).astype(BF)
            grad = (back * (cdf + pre * pdf)).astype(BF)
            pre_ref[p, :, cols] = grad
            add = dot_t(grad, w1)
            total = add if total is None else total + add
    part_ref[...] = total.astype(BF)
    normt_ref[...] = normed.T
    cott_ref[...] = cot.T
    cot_sum_ref[...] = jnp.sum(cot.astype(F32), 0, keepdims=True)


def ff_core_call(chunk, info, latents, cotangent, own, got, vectors, bias, wqo, weights):
    items = own.shape[0]
    _, lat_len, width = latents.shape
    rows = items * lat_len
    half = lambda i, info: (2 * info[0] + chunk, 0, 0)
    z3 = lambda i, info: (0, 0, 0)
    z4 = lambda i, info: (0, 0, 0, 0)
    z2 = lambda i, info: (0, 0)
    given = [pl.BlockSpec(w.shape, lambda i, info, d=w.ndim: (0,) * d) for w in weights]
    lanes = (1536, 1536, 768) if chunk == 0 else ()
    made = [pl.BlockSpec((8, width // 8, cols), z3) for cols in lanes]
    return pl.pallas_call(
        functools.partial(ff_core_kernel, chunk),
        grid_spec=pltpu.PrefetchScalarGridSpec(
            num_scalar_prefetch=1,
            grid=(1,),
            in_specs=[
                pl.BlockSpec((items, lat_len, width), half),
                pl.BlockSpec((items, lat_len, width), half),
                pl.BlockSpec(own.shape, z4),
                pl.BlockSpec(got.shape, z4),
                pl.BlockSpec(vectors.shape, z2),
                pl.BlockSpec(bias.shape, z2),
                pl.BlockSpec(wqo.shape, z3),
                *given,
            ],
            out_specs=[
                pl.BlockSpec((rows, width), z2),
                pl.BlockSpec((width, rows), z2),
                pl.BlockSpec((width, rows), z2),
                pl.BlockSpec((2, rows, 768), z3),
                pl.BlockSpec((2, rows, 768), z3),
                pl.BlockSpec((rows, width), z2),
                pl.BlockSpec((1, width), z2),
                *made,
            ],
        ),
        out_shape=[
            jax.ShapeDtypeStruct((rows, width), F32),
            jax.ShapeDtypeStruct((width, rows), BF),
            jax.ShapeDtypeStruct((width, rows), BF),
            jax.ShapeDtypeStruct((2, rows, 768), BF),
            jax.ShapeDtypeStruct((2, rows, 768), BF),
            jax.ShapeDtypeStruct((rows, width), BF),
            jax.ShapeDtypeStruct((1, width), F32),
        ]
        + [jax.ShapeDtypeStruct((8, width // 8, cols), BF) for cols in lanes],
        compiler_params=params(),
        cost_estimate=cost(6 * rows * width * 1536, 8 * 1024 * 1024, 2 * rows * 1536),
        name="ff_core",
    )(info, latents, cotangent, own, got, vectors, bias, wqo, *weights)


def relative_rows(info, ref, order):
    block = ref.shape[0] // 8
    return jnp.concatenate([ref[pl.ds(pl.multiple_of((info[4] ^ k) * block, 16), block), :] for k in order], 0)


def ff_grad_kernel(p, info, *refs):
    chunks, refs = (refs[:4], refs[4:8]), refs[8:]
    grad_ref, bias_ref = refs[-4:-2] if p == 0 else refs
    expand, reduce, bias = 0.0, 0.0, 0.0
    for normt_ref, cott_ref, hidden_ref, pre_ref in chunks:
        hidden, pre = hidden_ref[p], pre_ref[p]
        expand += dot(relative_rows(info, normt_ref, FF_ORDERS[0]), pre)
        reduce += dot(relative_rows(info, cott_ref, FF_ORDERS[1]), hidden)
        bias += jnp.sum(pre.astype(F32), 0, keepdims=True)
    grad_ref[0] = expand.astype(BF).reshape(8, -1, expand.shape[1])
    grad_ref[1] = reduce.astype(BF).reshape(8, -1, reduce.shape[1])
    bias_ref[...] = bias
    if p == 0:
        w_refs, (part_ref, acc) = refs[:2], refs[-2:]
        j = pl.program_id(0)
        rows = chunks[0][0].shape[1]
        for c, chunk in enumerate(chunks):
            here = pl.ds(c * rows, rows)
            add = sum(dot_t(chunk[2][q], w_ref[...].reshape(-1, w_ref.shape[2])) for q, w_ref in enumerate(w_refs))
            acc[here, :] = jnp.where(j == 0, 0.0, acc[here, :]) + add

        @pl.when(j == pl.num_programs(0) - 1)
        def _():
            part_ref[...] = acc[...].astype(BF)


def ff_grad_call(p, info, chunks, weights=()):
    width, rows = chunks[0][0].shape
    step = 256
    n = 768 // step
    z2 = lambda j, info: (0, 0)
    per_chunk = [
        pl.BlockSpec((width, rows), z2),
        pl.BlockSpec((width, rows), z2),
        pl.BlockSpec((2, rows, step), lambda j, info: (0, 0, j)),
        pl.BlockSpec((2, rows, step), lambda j, info: (0, 0, j)),
    ]
    specs = [
        pl.BlockSpec((2, 8, width // 8, step), lambda j, info: (0, 0, 0, j)),
        pl.BlockSpec((1, step), lambda j, info: (0, j)),
        pl.BlockSpec((2 * rows, width), z2),
    ]
    shapes = [
        jax.ShapeDtypeStruct((2, 8, width // 8, 768), BF),
        jax.ShapeDtypeStruct((1, 768), F32),
        jax.ShapeDtypeStruct((2 * rows, width), BF),
    ]
    count = 3 if p == 0 else 2
    return pl.pallas_call(
        functools.partial(ff_grad_kernel, p),
        grid_spec=pltpu.PrefetchScalarGridSpec(
            num_scalar_prefetch=1,
            grid=(n,),
            in_specs=per_chunk * 2
            + [pl.BlockSpec((8, width // 8, step), lambda j, info: (0, 0, n + j))] * len(weights),
            out_specs=specs[:count],
            scratch_shapes=[pltpu.VMEM((2 * rows, width), F32)] * (p == 0),
        ),
        out_shape=shapes[:count],
        compiler_params=params(),
        cost_estimate=cost((2 + 2 * (p == 0)) * 2 * rows * width * 1536, (8 + 6 * (p == 0)) * 1024 * 1024),
        name="ff_grad",
    )(info, *chunks[0], *chunks[1], *weights)


def attn_bwd_kernel(last, info, cot_ref, lat_ref, res_ref, own_ref, got_ref, vec_ref,
                    mixed_ref, pt_ref, kv_ref, q_ref, normt_ref, lat_normt_ref, wqo_ref, *refs):
    if last:
        gkv_in, gqo_in, res_grad_ref, dq_ref, dkv_ref, sums_ref, g_own_ref, g_oth_ref, gkv, gqo = refs
    else:
        res_grad_ref, dq_ref, dkv_ref, sums_ref, gkv, gqo = refs
    i = pl.program_id(0)

    @pl.when(i == 0)
    def _():
        gkv[...] = gkv_in[...] if last else jnp.zeros_like(gkv)
        gqo[...] = gqo_in[...] if last else jnp.zeros_like(gqo)
        sums_ref[...] = jnp.zeros_like(sums_ref)

    xhat, rstd = norm_parts(res_ref[...])
    dy = own_ref[...].astype(F32) + got_ref[...].astype(F32)
    dx, dgain, dbias = norm_back(dy, xhat, rstd, vec_ref[4:5, :])
    grad = cot_ref[0].astype(F32) + dx
    res_grad_ref[...] = grad
    sums_ref[0:1, :] += dgain
    sums_ref[1:2, :] += dbias
    low = grad.astype(BF)
    columns = lambda start, stop: wqo_ref[:, :, start:stop].reshape(-1, stop - start)
    lane_lo = lax.broadcasted_iota(jnp.int32, (128, 128), 1) < HEAD_DIM
    row_lo = lax.broadcasted_iota(jnp.int32, (128, 128), 0) < HEAD_DIM
    both = jnp.concatenate([lat_normt_ref[0], low.T], 1)
    none = jnp.zeros((128, 128), BF)
    zeros = jnp.zeros((64, 128), BF)
    total = None
    for p in range(2):
        base = p * 384
        kv = kv_ref[0, :, base : base + 384]
        mixed_grad = dot(low, columns(base + 128, base + 384))
        mg2 = jnp.where(lane_lo, 0.0, mixed_grad[:, 0:128]).astype(BF)
        mg01 = mixed_grad[:, 128:256]
        mg01 = jnp.concatenate([jnp.where(lane_lo, mg01, 0.0), jnp.where(lane_lo, 0.0, mg01)], 0).astype(BF)
        first = dot_t(kv[:, 128:256], mg01)
        second = dot_t(kv[:, 256:384], mg2)
        probs, scores = [], []
        for h, piece in enumerate((first[:, 0:128], first[:, 128:256], second)):
            prob = pt_ref[0, p, :, h * 128 : (h + 1) * 128]
            inner = jnp.sum(piece * prob, 0, keepdims=True)
            scores.append((prob * (piece - inner)).astype(BF))
            probs.append(prob.astype(BF))
        q01 = q_ref[0, p, :, 0:128].astype(F32)
        q01 = jnp.concatenate([jnp.where(lane_lo, q01, 0.0), jnp.where(lane_lo, 0.0, q01)], 0).astype(BF)
        q2 = q_ref[0, p, :, 128:256]
        ds01 = jnp.concatenate(scores[:2], 1)
        dkv_ref[0, :, base : base + 128] = dot(ds01, q01).astype(BF)
        dkv_ref[0, :, base + 128 : base + 256] = dot(jnp.concatenate(probs[:2], 1), mg01).astype(BF)
        dkv_ref[0, :, base + 256 : base + 384] = dot(
            jnp.concatenate([scores[2], probs[2]], 1), jnp.concatenate([q2, mg2], 0)
        ).astype(BF)
        dq01 = dot(kv[:, 0:128].T, ds01)
        dq2 = dot(kv[:, 256:384].T, scores[2])
        dq01 = (jnp.where(row_lo, dq01[:, 0:128], dq01[:, 128:256]) * SCALE).astype(BF)
        dq2 = (jnp.where(row_lo, dq2, 0.0) * SCALE).astype(BF)
        dq_ref[0, p, 0:128, :] = dq01
        dq_ref[0, p, 128:192, :] = dq2[0:64]
        add = dot_t(jnp.concatenate([dq01.T, dq2.T], 1), columns(base, base + 256))
        total = add if total is None else total + add
        right = jnp.concatenate(
            [
                jnp.concatenate([dq01, none], 1),
                jnp.concatenate([dq2, jnp.concatenate([zeros, mixed_ref[0, p, 0:64, :]], 0)], 1),
                jnp.concatenate([none, mixed_ref[0, p, 64:192, :]], 1),
            ],
            0,
        )
        gqo[:, base : base + 384] += dot_t(both, right)
    lat_hat, _ = norm_parts(lat_ref[0].astype(F32))
    sums_ref[2:3, :] += jnp.sum(total * lat_hat, 0, keepdims=True)
    sums_ref[3:4, :] += jnp.sum(total, 0, keepdims=True)
    gkv[...] += dot(normt_ref[0], dkv_ref[0])

    if last:

        @pl.when(i == pl.num_programs(0) - 1)
        def _():
            block = gkv.shape[0] // 8
            for j, k in enumerate(ORDER):
                source = pl.ds(pl.multiple_of((info[4] ^ k) * block, 8), block)
                rows = slice(j * block, (j + 1) * block)
                g_own_ref[rows, 0:384] = gkv[source, 0:384].astype(BF)
                g_own_ref[rows, 384:768] = gqo[source, 0:384].astype(BF)
                g_oth_ref[rows, 0:384] = gkv[source, 384:768].astype(BF)
                g_oth_ref[rows, 384:768] = gqo[source, 384:768].astype(BF)


def attn_bwd_call(first_item, all_items, info, cotangent, latents, residual, own, got, vectors,
                  mixed, pt, kv, q, normt, lat_normt, wqo, grads=None):
    items, keys, _ = kv.shape
    width = normt.shape[1]
    lat_len = q.shape[2]
    last = grads is not None
    one = lambda i, *_: (i, 0)
    three = lambda i, *_: (i, 0, 0)
    mine = lambda i, info: (info[0] * all_items + first_item + i, 0, 0)
    four = lambda i, *_: (i, 0, 0, 0)
    z2 = lambda i, *_: (0, 0)
    flops = items * 2 * (keys * width * 768 + 3 * lat_len * width * 768 + 10 * keys * lat_len * 384)
    out_specs = [
        pl.BlockSpec((lat_len, width), one),
        pl.BlockSpec((1, 2, 192, lat_len), four),
        pl.BlockSpec((1, keys, 768), three),
        pl.BlockSpec((4, width), z2),
        pl.BlockSpec((width, 768), z2),
        pl.BlockSpec((width, 768), z2),
    ]
    out_shape = [
        jax.ShapeDtypeStruct((items * lat_len, width), F32),
        jax.ShapeDtypeStruct((items, 2, 192, lat_len), BF),
        jax.ShapeDtypeStruct((items, keys, 768), BF),
        jax.ShapeDtypeStruct((4, width), F32),
        jax.ShapeDtypeStruct((width, 768), BF if last else F32),
        jax.ShapeDtypeStruct((width, 768), BF if last else F32),
    ]
    return pl.pallas_call(
        functools.partial(attn_bwd_kernel, last),
        grid_spec=pltpu.PrefetchScalarGridSpec(
            num_scalar_prefetch=1,
            grid=(items,),
            in_specs=[
                pl.BlockSpec((1, lat_len, width), mine),
                pl.BlockSpec((1, lat_len, width), mine),
                pl.BlockSpec((lat_len, width), one),
                pl.BlockSpec((lat_len, width), one),
                pl.BlockSpec((lat_len, width), one),
                pl.BlockSpec(vectors.shape, z2),
                pl.BlockSpec((1, 2, 192, lat_len), four),
                pl.BlockSpec((1, 2, keys, 384), four),
                pl.BlockSpec((1, keys, 768), three),
                pl.BlockSpec((1, 2, lat_len, 256), four),
                pl.BlockSpec((1, width, keys), three),
                pl.BlockSpec((1, width, lat_len), three),
                pl.BlockSpec(wqo.shape, lambda i, *_: (0, 0, 0)),
            ]
            + [pl.BlockSpec((width, 768), z2)] * (2 * last),
            out_specs=out_specs,
            scratch_shapes=[pltpu.VMEM((width, 768), F32), pltpu.VMEM((width, 768), F32)] * last,
        ),
        out_shape=out_shape,
        compiler_params=params(),
        cost_estimate=cost(flops, 12 * 1024 * 1024),
        name="attn_bwd",
    )(info, cotangent, latents, residual, own, got, vectors, mixed, pt, kv, q, normt, lat_normt, wqo, *(grads or ()))


def latent_kernel(info, lat_ref, *refs):
    vec_ref, wqo_ref, wqx_ref, out_ref = refs[6:]
    width = vec_ref.shape[1]
    step = out_ref.shape[1]
    per = refs[0].shape[0] // step
    for c in range(2):
        grad_ref, own_ref, got_ref = refs[c], refs[2 + c], refs[4 + c]
        xhat, rstd = norm_parts(lat_ref[c * per : (c + 1) * per].reshape(-1, width).astype(F32))
        dy = spread(own_ref, wqo_ref, True) + spread(got_ref, wqx_ref, True)
        dx, _, _ = norm_back(dy, xhat, rstd, vec_ref[0:1, :])
        out_ref[c * per : (c + 1) * per] = (grad_ref[...] + dx).astype(BF).reshape(per, step, width)


def latent_call(info, latents, grads, own, got, vectors, wqo, wqx):
    half, width = grads[0].shape
    lat_len = latents.shape[1]
    items = 2 * half // lat_len
    z2 = lambda i, info: (0, 0)
    z3 = lambda i, info: (0, 0, 0)
    return pl.pallas_call(
        latent_kernel,
        grid_spec=pltpu.PrefetchScalarGridSpec(
            num_scalar_prefetch=1,
            grid=(1,),
            in_specs=[pl.BlockSpec((items, lat_len, width), lambda i, info: (info[0], 0, 0))]
            + [pl.BlockSpec((half, width), z2)] * 2
            + [pl.BlockSpec(own[0].shape, lambda i, info: (0, 0, 0, 0))] * 4
            + [pl.BlockSpec(vectors.shape, z2), pl.BlockSpec(wqo.shape, z3), pl.BlockSpec(wqx.shape, z3)],
            out_specs=pl.BlockSpec((items, lat_len, width), z3),
        ),
        out_shape=jax.ShapeDtypeStruct((items, lat_len, width), BF),
        compiler_params=params(),
        cost_estimate=cost(4 * items * lat_len * width * 768, 6 * 1024 * 1024),
        name="latent_back",
    )(info, latents, *grads, *own, *got, vectors, wqo, wqx)


def byte_part_kernel(info, dkv_ref, raw_ref, wkv_ref, own_ref, sums_ref, *send_refs):
    part = dot_t(dkv_ref[0], wkv_ref[...].reshape(-1, 768))
    xhat, _ = norm_parts(raw_ref[0].astype(F32))
    half = part.shape[0] // 2
    item = pl.program_id(0)

    @pl.when(item == 0)
    def _():
        sums_ref[...] = jnp.zeros_like(sums_ref)

    sums_ref[0:1, :] += jnp.sum(part * xhat, 0, keepdims=True)
    sums_ref[1:2, :] += jnp.sum(part, 0, keepdims=True)
    low = part.astype(BF)
    for side in range(2):
        for k, send_ref in enumerate(send_refs):

            @pl.when((info[1] == side) & (item == k))
            def _():
                own_ref[0] = low[half * side : half * (side + 1)]
                send_ref[0] = low[half * (1 - side) : half * (2 - side)]


def byte_part_call(info, dkv, raw, wkv):
    items, keys, _ = dkv.shape
    width = raw.shape[2]
    half = keys // 2
    out = lambda i, info: (i, 0, 0)
    whole = lambda i, info: (0, 0, 0)
    return pl.pallas_call(
        byte_part_kernel,
        grid_spec=pltpu.PrefetchScalarGridSpec(
            num_scalar_prefetch=1,
            grid=(items,),
            in_specs=[
                pl.BlockSpec((1, keys, 768), out),
                pl.BlockSpec((1, keys, width), out),
                pl.BlockSpec(wkv.shape, whole),
            ],
            out_specs=[
                pl.BlockSpec((1, half, width), out),
                pl.BlockSpec((2, width), lambda i, info: (0, 0)),
            ]
            + [pl.BlockSpec((1, half, width), whole)] * items,
        ),
        out_shape=[
            jax.ShapeDtypeStruct((items, half, width), BF),
            jax.ShapeDtypeStruct((2, width), F32),
        ]
        + [jax.ShapeDtypeStruct((1, half, width), BF)] * items,
        compiler_params=params(),
        cost_estimate=cost(items * keys * width * 768 * 2, 6 * 1024 * 1024),
        name="byte_part",
    )(info, dkv, raw, wkv)


def byte_back_kernel(info, part_ref, raw_ref, vec_ref, *refs):
    got_refs, (own_ref, oth_ref) = refs[:-2], refs[-2:]
    half = part_ref.shape[1]
    quarter = half // 2
    got = [ref[k] for ref in got_refs for k in range(ref.shape[0])]
    for k, piece in enumerate(got):
        dy = part_ref[k].astype(F32) + piece.astype(F32)
        xhat, rstd = norm_parts(raw_ref[k].astype(F32))
        dx, _, _ = norm_back(dy, xhat, rstd, vec_ref[2:3, :])
        dx = dx.astype(BF)

        @pl.when(info[0] == 0)
        def _():
            own_ref[k] = dx[:quarter]
            oth_ref[k] = dx[quarter:]

        @pl.when(info[0] != 0)
        def _():
            own_ref[k] = dx[quarter:]
            oth_ref[k] = dx[:quarter]


def byte_back_call(info, part, got, raw, vectors):
    items, half, width = part.shape
    z3 = lambda i, info: (0, 0, 0)
    return pl.pallas_call(
        byte_back_kernel,
        grid_spec=pltpu.PrefetchScalarGridSpec(
            num_scalar_prefetch=1,
            grid=(1,),
            in_specs=[
                pl.BlockSpec((items, half, width), z3),
                pl.BlockSpec((items, half, width), lambda i, info: (0, info[1], 0)),
                pl.BlockSpec(vectors.shape, lambda i, info: (0, 0)),
                *(pl.BlockSpec(piece.shape, z3) for piece in got),
            ],
            out_specs=[pl.BlockSpec((items, half // 2, width), z3)] * 2,
        ),
        out_shape=[jax.ShapeDtypeStruct((items, half // 2, width), BF)] * 2,
        compiler_params=params(),
        cost_estimate=cost(items * half * width * 20, 4 * 1024 * 1024),
        name="byte_back",
    )(info, part, raw, vectors, *got)


def body(
    latents, byte_array, cotangent, patch_count, text_len,
    inner_weight, inner_moment, inner_square,
    output_weight, output_moment, output_square,
    expand_weight, expand_moment, expand_square,
    reduce_weight, reduce_moment, reduce_square,
    expand_bias, bias_moment, bias_square,
    norm_vectors, vector_moment, vector_square,
):
    item_count, lat_len, width = latents.shape
    keys = byte_array.shape[1]
    items = item_count // 2
    n = lax.axis_size("dp")
    head = lax.axis_index("head")
    core, xside = head & 1, head >> 1
    true_rows = keys // lax.axis_size("head")
    pad_rows = -(-true_rows // 32) * 32
    pad_keys = 4 * pad_rows
    quick = n == 8
    place = lax.axis_index("dp") if quick else jnp.int32(0)
    info = jnp.stack([core, xside, jnp.int32(true_rows), jnp.int32(items), place]).astype(jnp.int32)
    half_items = items // 2

    low_inner = inner_weight.astype(BF)
    wq, wk, wv = low_inner[0], low_inner[1], low_inner[2]
    wo = output_weight.T.astype(BF)
    pack = jnp.concatenate(
        [wk[:, :128], wv[:, :128], wk[:, 128:], wv[:, 128:], wq[:, :128], wq[:, 128:], wo[:, 128:], wo[:, :128]], 1
    )
    ff_pack = jnp.concatenate([expand_weight.astype(BF), reduce_weight.T.astype(BF)], 1)
    normalise = lambda c, byte_array: norm_call(
        c * half_items, items, info, byte_array, latents, norm_vectors, half_items, pad_keys
    )
    flip = lambda value: swap(value, "head", 1)
    over = lambda value, mask: swap(value, "dp", mask)
    grouped = lambda p: [flip(jnp.concatenate([p[k] for k in group], 0)) for group in GROUPS]
    if quick:
        g = {0: pack, 4: over(pack, 4), 2: over(pack, 2), 1: over(pack, 1)}
        norm0 = normalise(0, byte_array)
        g[4], g[2], g[1], *norm0 = tie(g[4], g[2], g[1], *norm0)
        g[6], g[5], g[3] = over(g[4], 2), over(g[4], 1), over(g[2], 1)
        g[6], g[5], g[3], byte_later, ff_pack = tie(g[6], g[5], g[3], byte_array, ff_pack)
        f = {0: ff_pack, 4: over(ff_pack, 4), 2: over(ff_pack, 2), 1: over(ff_pack, 1)}
        g[7] = over(g[6], 1)
        norm1 = normalise(1, byte_later)
        g[7], f[4], f[2], f[1], *norm1 = tie(g[7], f[4], f[2], f[1], *norm1)
        f[6], f[5], f[3] = over(f[4], 2), over(f[4], 1), over(f[2], 1)
        pieces = [g[k] for k in range(8)] + grouped(g)
    else:
        norm0, norm1 = normalise(0, byte_array), normalise(1, byte_array)
        blocks = lax.all_gather(pack, "dp", axis=0, tiled=True).reshape(8, width // 8, 768)
        g = [blocks[k] for k in range(8)]
        pieces = g + grouped(g)
        blocks = lax.all_gather(ff_pack, "dp", axis=0, tiled=True).reshape(8, width // 8, 1536)
        f = [blocks[k] for k in range(8)]
    norm, normt, raw, lat_norm, lat_normt = zip(norm0, norm1)
    bias_other = flip(expand_bias)

    crossed = swap(jnp.concatenate([g[k][:, 384:] for k in range(8)], 0), "head", 2)

    attend = lambda c, weights: attn_fwd_call(
        c * half_items, info, patch_count, text_len, norm[c], lat_norm[c], weights
    )
    mixed0, *kept0, wkv, wqo = attend(0, pieces)
    got0 = swap(mixed0, "head", 2)
    if quick:
        first_flip = flip(jnp.concatenate([f[k] for k in GROUPS[0]], 0))
        wkv, f[6], f[5], f[3], first_flip, bias_other, crossed = tie(
            wkv, f[6], f[5], f[3], first_flip, bias_other, crossed
        )
        f[7] = over(f[6], 1)
        second_flip = flip(jnp.concatenate([f[k] for k in GROUPS[1]], 0))
    crossed = [crossed, flip(crossed)]
    mixed1, *kept1 = attend(1, [wkv, wqo])
    mixed1, got0, crossed[1] = tie(mixed1, got0, crossed[1])
    got1 = swap(mixed1, "head", 2)
    if quick:
        mixed1, second_flip, f[7] = tie(mixed1, second_flip, f[7])
        ff_pieces = [f[k] for k in range(8)] + [first_flip, second_flip, flip(f[7])]
    else:
        ff_pieces = f + grouped(f)

    bias_both = jnp.stack([expand_bias, bias_other])
    feed = lambda c, mixed, got, weights: ff_core_call(
        c, info, latents, cotangent, mixed, got, norm_vectors, bias_both, wqo, weights
    )
    res0, *ff0, npart0, cot_sum0, ff_own, ff_oth, wqx = feed(0, mixed0, got0, [*ff_pieces, *crossed])
    npart0, got1 = tie(npart0, got1)
    ngot0 = swap(npart0, "head", 2)
    res1, *ff1, npart1, cot_sum1 = feed(1, mixed1, got1, [ff_own, ff_oth, wqx])
    npart1, ngot0 = tie(npart1, ngot0)
    ngot1 = swap(npart1, "head", 2)
    g_oth, bias_oth = ff_grad_call(1, info, [ff0, ff1])
    g_oth, ngot0, ff1[3] = tie(g_oth, ngot0, ff1[3])
    g_got = flip(g_oth)
    g_own, bias_own, mlp_part = ff_grad_call(0, info, [ff0, ff1], [ff_own, ff_oth])
    g_own, ngot0, g_got = tie(g_own, ngot0, g_got)
    bias_own = bias_own + flip(bias_oth)
    pair_of = lambda kind, part: (g_own[kind, part], g_got[kind, part])
    first_steps = [plus(*pair_of(kind, slice(0, 4))) for kind in range(2)]

    attend_back = lambda c, res, npart, ngot, mixed, kept, grads: attn_bwd_call(
        c * half_items, items, info, cotangent, latents, res, npart, ngot,
        norm_vectors, mixed, *kept, normt[c], lat_normt[c], wqo, grads
    )
    res0, ngot0, bias_own, *first_steps = tie(res0, ngot0, bias_own, *first_steps)
    if quick:
        ff_got = [over(first_steps[0], 1), over(first_steps[1], 2)]
    rgrad0, dq0, dkv0, sums0, *grads = attend_back(0, res0, npart0, ngot0, mixed0, kept0, None)
    dkv0, ngot1, mlp_part = tie(dkv0, ngot1, mlp_part)
    mlp_got = swap(mlp_part, "head", 2)
    bown0, bsums0, *bsend0 = byte_part_call(info, dkv0, raw[0], wkv)
    res1, bsend0[0] = tie(res1, bsend0[0])
    bgot00 = swap(bsend0[0], "head", 2)
    if quick:
        res1, *ff_got = tie(res1, *ff_got)
        second_steps = [plus(*pair_of(kind, slice(4, 6)), ff_got[kind][0:2]) for kind in range(2)]
        ff_more = [over(second_steps[0], 2), over(second_steps[1], 1)]
    rgrad1, dq1, dkv1, sums1, g_attn, g_attn_oth = attend_back(1, res1, npart1, ngot1, mixed1, kept1, grads)
    g_attn_oth, mlp_got, bsend0[1] = tie(g_attn_oth, mlp_got, bsend0[1])
    bgot01 = swap(bsend0[1], "head", 2)
    if quick:
        g_attn_oth, *ff_more = tie(g_attn_oth, *ff_more)
        rest = [(*pair_of(kind, part), ff_got[kind][part - 4], ff_more[kind][part - 6]) for part in (6, 7) for kind in range(2)]
        third_step = jnp.concatenate([plus(*rest[0]), plus(*rest[1])], 0)
    else:
        g_ff = g_own.astype(F32) + g_got.astype(F32)
        g_ff = jnp.stack([g_ff[kind, order.index(k)] for kind, order in enumerate(FF_ORDERS) for k in range(8)])
        g_ff = g_ff.reshape(2, width, 768)
        g_ff = lax.psum_scatter(g_ff, "dp", scatter_dimension=1, tiled=True).reshape(-1, 768)
    u = g_attn.reshape(8, width // 8, 768)
    v = flip(g_attn_oth).reshape(8, width // 8, 768)
    u75 = plus(u[0:2], v[0:2])

    if quick:
        u31 = plus(u[2:4], v[2:4])
        dkv1, u75, u31, third_step = tie(dkv1, u75, u31, third_step)
        third = 5 * third_step.shape[0] // 12
        last_got = [over(third_step[:third], 4)]
        y75 = over(u75, 1)
        y31 = over(u31, 1)
    bown1, bsums1, *bsend1 = byte_part_call(info, dkv1, raw[1], wkv)
    if quick:
        bsend1[0], y75, bgot00, dq0, dq1, last_got[0] = tie(bsend1[0], y75, bgot00, dq0, dq1, last_got[0])
        u64 = plus(u[4:6], v[4:6], y75)
        last_got.append(over(third_step[third : 2 * third], 4))
        z6 = over(u64[0], 2)
    lgot0, lgot1 = swap(dq0, "head", 2), swap(dq1, "head", 2)
    side0 = list(byte_back_call(info, bown0, [bgot00, bgot01], raw[0], norm_vectors))

    residual = jnp.concatenate([res0, res1], 0)
    block_mine = residual + (mlp_part.astype(F32) + mlp_got.astype(F32)) + norm_vectors[6]
    block_mine = block_mine.astype(BF).reshape(items, lat_len, width)

    byte_side = lambda c, own, got: byte_back_call(info, own, got, raw[c], norm_vectors)
    if quick:
        block_mine, z6, y31, bsend1[0], last_got[1], side0[0] = tie(
            block_mine, z6, y31, bsend1[0], last_got[1], side0[0]
        )
        last_got.append(over(third_step[2 * third :], 4))
        z4 = over(plus(u64[1], z6), 4)
        z2 = over(plus(u[6], v[6], y31[0]), 2)
    bgot10 = swap(bsend1[0], "head", 2)
    lat_mine = latent_call(
        info, latents, [rgrad0, rgrad1], [dq0, dq1], [lgot0, lgot1], norm_vectors, wqo, wqx
    )
    block_output = pair_call(info, [block_mine], [flip(block_mine)], lat_len)
    if quick:
        block_output, lat_mine, last_got[2], z4, z2 = tie(block_output, lat_mine, last_got[2], z4, z2)
        g_ff = jnp.concatenate([sum(x.astype(F32) for x in rest[2 + kind]) for kind in range(2)], 0)
        g_ff = g_ff + jnp.concatenate(last_got, 0).astype(F32)
        ff_squares = jnp.sum(g_ff * g_ff)
        bgot10, bsend1[1] = tie(bgot10, bsend1[1])
        terms = [u[7], v[7], y31[1], z2, z4]
    else:
        g_attn = u.astype(F32) + v.astype(F32)
        g_attn = jnp.concatenate([g_attn[ORDER.index(k)] for k in range(8)], 0)
        terms = [lax.psum_scatter(g_attn, "dp", scatter_dimension=0, tiled=True)]
        ff_squares = jnp.sum(g_ff * g_ff)
    bgot11 = swap(bsend1[1], "head", 2)
    side1 = byte_side(1, bown1, [bgot10, bgot11])
    g_attn, load = collect_call(
        info, terms, [sums0, sums1, bsums0, bsums1, cot_sum0, cot_sum1, bias_own, ff_squares.reshape(1, 1)]
    )
    latent_gradient = pair_call(info, [lat_mine], [flip(lat_mine)], lat_len)
    beside = [lambda: latent_gradient, None, lambda: side1]
    outs = []
    mask = n // 2
    while mask:
        hop = over(load, mask)
        make = beside.pop(0) if beside else None
        if make:
            hop, out = lax.optimization_barrier((hop, make()))
            outs.append(out)
        load = load + hop
        mask //= 2
    latent_gradient = outs[0]
    bias_sum = load[7:8]
    squares = load[8:9] + jnp.sum(bias_sum * bias_sum)
    load = jnp.concatenate([load[:7], squares], 0)
    load = load + swap(load, "head", 1)
    by_row = rows_call(info, [side0[0], outs[1][0]], [flip(side0[1]), flip(outs[1][1])], true_rows)
    hop, by_row = tie(swap(load, "head", 2), by_row)
    byte_gradient = by_row.transpose(1, 0, 2)
    load = load + hop

    *news, grad_norm = adam_call(
        load,
        g_attn,
        g_ff,
        [
            inner_weight, inner_moment, inner_square, output_weight, output_moment, output_square,
            expand_weight, expand_moment, expand_square, reduce_weight.T, reduce_moment.T, reduce_square.T,
            norm_vectors, vector_moment, vector_square,
        ],
    )
    factor = CLIP_RATE * math.sqrt(4 * D * D + 2 * D * FF + FF + 7 * D) / grad_norm[0, 0]
    bias_new = adamw(expand_bias, bias_moment, bias_square, factor * bias_sum[0], 0.3, 0.0)
    news[9:12] = [new.T for new in news[9:12]]
    return (
        block_output, latent_gradient, byte_gradient, *news[:12], *bias_new, *news[12:], grad_norm[0, 0]
    )


def solution(mesh):
    rows, cols = P("dp", "head"), P("head", "dp")
    inner, items = P(None, "dp", "head"), P("dp", None, None)
    weights = (inner,) * 3 + (cols,) * 3 + (rows,) * 3 + (cols,) * 3 + (P("head"),) * 3 + (P(),) * 3
    return jax.shard_map(
        body,
        mesh=mesh,
        in_specs=(items, items, items, P("dp"), P("dp")) + weights,
        out_specs=(items, items, P("dp", "head", None)) + weights + (P(),),
        check_vma=False,
    )
```

```python
import functools
import math

import jax
import jax.numpy as jnp
from jax import lax
from jax.experimental import pallas as pl
from jax.experimental.pallas import tpu as pltpu
from jax.sharding import PartitionSpec as P

D = 768
HEAD_DIM = 64
FF = 3072
PATCHES = 576
STEP = 5

NEG_FILL = -1000000000.0
BETA = 0.5
ADAM_EPS = 1e-08
DECAY = 0.01
CLIP_RATE = 0.01
LN_EPS = 1e-05
SCALE = 1.0 / math.sqrt(HEAD_DIM)
BF = jnp.bfloat16
F32 = jnp.float32
VMEM_LIMIT = 20 * 1024 * 1024


def dot(a, b):
    return lax.dot_general(a, b, (((1,), (0,)), ((), ())), preferred_element_type=F32)


def dot_t(a, b):
    return lax.dot_general(a, b, (((1,), (1,)), ((), ())), preferred_element_type=F32)


def norm_parts(rows):
    centred = rows - jnp.mean(rows, -1, keepdims=True)
    rstd = lax.rsqrt(jnp.mean(centred * centred, -1, keepdims=True) + LN_EPS)
    return centred * rstd, rstd


def norm_back(dy, xhat, rstd, gain):
    scaled = dy * gain
    first = jnp.mean(scaled, -1, keepdims=True)
    second = jnp.mean(scaled * xhat, -1, keepdims=True)
    dx = rstd * (scaled - first - xhat * second)
    return dx, jnp.sum(dy * xhat, 0, keepdims=True), jnp.sum(dy, 0, keepdims=True)


def swap(value, axis, mask):
    size = lax.axis_size(axis)
    return lax.ppermute(value, axis, [(i, i ^ mask) for i in range(size)])


def tie(*values):
    return lax.optimization_barrier(tuple(values))


def plus(*values):
    return sum(value.astype(F32) for value in values).astype(BF)


def adamw(weight, moment, square, gradient, rate, decay_rate):
    moment_new = BETA * moment + (1.0 - BETA) * gradient
    square_new = BETA * square + (1.0 - BETA) * gradient * gradient
    correction = 1.0 - BETA**STEP
    step_dir = moment_new * (1.0 / correction) / (jnp.sqrt(square_new * (1.0 / correction)) + ADAM_EPS)
    return (weight - rate * (step_dir + decay_rate * weight), moment_new, square_new)


def params(**kw):
    return pltpu.CompilerParams(vmem_limit_bytes=VMEM_LIMIT, **kw)


def cost(flops, nbytes, trans=0):
    return pl.CostEstimate(flops=flops, bytes_accessed=nbytes, transcendentals=trans)


GROUPS = ((0, 4, 2, 1), (6, 5, 3), (7,))


def assemble(info, parts, outs, splits):
    rows = parts[0].shape[0]
    blocks = [(k, 0, parts[k], 0) for k in range(8)]
    for part, group in zip(parts[8:], GROUPS):
        blocks += [(k, 1, part, i * rows) for i, k in enumerate(group)]
    for k, c, part, first in blocks:
        for out, start, stop, offset in splits[c]:
            outs[out][info[4] ^ k, :, offset : offset + stop - start] = part[first : first + rows, start:stop]


ORDER = (7, 5, 3, 1, 6, 4, 2, 0)
FF_ORDERS = ((7, 3, 5, 1, 6, 2, 4, 0), (7, 3, 6, 2, 5, 1, 4, 0))


def pair_kernel(chunks, info, *refs):
    out = refs[-1]
    rows = out.shape[1]
    per = refs[0].shape[0]
    for side in range(2):
        first = (info[0] ^ side) * (chunks * per)
        for c in range(chunks):
            ref = refs[side * chunks + c]
            for k in range(per):
                out[first + c * per + k] = ref[k, :rows, :]


def pair_call(info, own, other, rows):
    per, _, width = own[0].shape
    chunks = len(own)
    return pl.pallas_call(
        functools.partial(pair_kernel, chunks),
        grid_spec=pltpu.PrefetchScalarGridSpec(
            num_scalar_prefetch=1,
            grid=(1,),
            in_specs=[pl.BlockSpec(own[0].shape, lambda i, info: (0, 0, 0))] * (2 * chunks),
            out_specs=pl.BlockSpec((2 * chunks * per, rows, width), lambda i, info: (0, 0, 0)),
        ),
        out_shape=jax.ShapeDtypeStruct((2 * chunks * per, rows, width), BF),
        compiler_params=params(),
        cost_estimate=cost(1, 4 * chunks * per * rows * width * 2),
        name="pair",
    )(info, *own, *other)


def rows_kernel(info, *refs):
    blocks, out = refs[:4], refs[4]
    true_rows, step = out.shape[0], 32
    for core in range(2):

        @pl.when(info[0] == core)
        def _():
            order = blocks if core == 0 else (*blocks[2:], *blocks[:2])
            for first in range(0, true_rows, step):
                count = min(step, true_rows - first)
                items = [ref[k, first : first + step, :].astype(F32) for ref in order for k in range(ref.shape[0])]
                by_row = pltpu.einshape("abc->bac", jnp.stack(items, 0))
                out[first : first + count] = by_row[:count].astype(BF)


def rows_call(info, own, other, rows):
    per, _, width = own[0].shape
    return pl.pallas_call(
        rows_kernel,
        grid_spec=pltpu.PrefetchScalarGridSpec(
            num_scalar_prefetch=1,
            grid=(1,),
            in_specs=[pl.BlockSpec(own[0].shape, lambda i, info: (0, 0, 0))] * 4,
            out_specs=pl.BlockSpec((rows, 4 * per, width), lambda i, info: (0, 0, 0)),
        ),
        out_shape=jax.ShapeDtypeStruct((rows, 4 * per, width), BF),
        compiler_params=params(),
        cost_estimate=cost(1, 16 * per * rows * width),
        name="rows",
    )(info, *own, *other)


def collect_kernel(count, info, *refs):
    terms, (sums0, sums1, bytes0, bytes1, cot0, cot1, bias, squares, grad_ref, load_ref) = refs[:count], refs[count:]
    grad = sum(ref[...].astype(F32) for ref in terms)
    grad_ref[...] = grad
    once = jnp.where(info[1] == 0, 1.0, 0.0)
    sums = sums0[...] + sums1[...]
    load_ref[0:2, :] = sums[2:4]
    load_ref[2:4, :] = bytes0[...] + bytes1[...]
    load_ref[4:6, :] = sums[0:2] * once
    load_ref[6:7, :] = (cot0[...] + cot1[...]) * once
    load_ref[7:8, :] = bias[...]
    total = jnp.sum(jnp.sum(grad * grad, 0, keepdims=True), 1, keepdims=True) + squares[...]
    load_ref[8:9, :] = jnp.broadcast_to(total, (1, load_ref.shape[1]))


def collect_call(info, terms, small):
    rows, width = terms[0].shape
    whole = lambda i, info: (0, 0)
    return pl.pallas_call(
        functools.partial(collect_kernel, len(terms)),
        grid_spec=pltpu.PrefetchScalarGridSpec(
            num_scalar_prefetch=1,
            grid=(1,),
            in_specs=[pl.BlockSpec(x.shape, whole) for x in (*terms, *small)],
            out_specs=[pl.BlockSpec((rows, width), whole), pl.BlockSpec((9, width), whole)],
        ),
        out_shape=[jax.ShapeDtypeStruct((rows, width), F32), jax.ShapeDtypeStruct((9, width), F32)],
        compiler_params=params(),
        cost_estimate=cost(1, 16 * rows * width),
        name="collect",
    )(info, *terms, *small)


def adam_kernel(load_ref, attn_ref, ff_ref, *refs):
    inner, output, expand, reduce, vector = (refs[3 * k : 3 * k + 3] for k in range(5))
    outs = refs[15:]
    load = load_ref[...]
    vectors = load[0:7]
    total = jnp.sum(jnp.sum(vectors * vectors, 0, keepdims=True) + load[7:8], 1, keepdims=True) + load[8:9, 0:1]
    norm = jnp.sqrt(total)
    outs[15][...] = norm
    factor = CLIP_RATE * math.sqrt(4 * D * D + 2 * D * FF + FF + 7 * D) / norm

    def update(which, at, grad, rate, decay_rate):
        state = refs[3 * which : 3 * which + 3]
        for ref, new in zip(
            outs[3 * which : 3 * which + 3],
            adamw(*(ref[at] for ref in state), factor * grad, rate, decay_rate),
        ):
            ref[at] = new

    low, high = slice(0, 128), slice(128, 192)
    every = slice(None)
    for matrix, first, second in ((0, 384, 512), (1, 0, 256), (2, 128, 320)):
        update(0, (matrix, every, low), attn_ref[:, first : first + 128], 0.03, DECAY)
        update(0, (matrix, every, high), attn_ref[:, second : second + 64], 0.03, DECAY)
    update(1, (low, every), attn_ref[:, 640:768].T, 0.3, DECAY)
    update(1, (high, every), attn_ref[:, 512:640].T[64:128], 0.3, DECAY)
    rows = expand[0].shape[0]
    update(2, Ellipsis, ff_ref[0:rows, :], 0.03, DECAY)
    update(3, Ellipsis, ff_ref[rows : 2 * rows, :], 0.015, DECAY)
    update(4, Ellipsis, vectors, 0.3, 0.0)


def adam_call(load, attn, ff, state):
    shapes = [jax.ShapeDtypeStruct(x.shape, F32) for x in state] + [jax.ShapeDtypeStruct((1, 1), F32)]
    return pl.pallas_call(
        adam_kernel,
        out_shape=shapes,
        compiler_params=params(),
        cost_estimate=cost(1, sum(x.size for x in state) * 4 * 2),
        name="adam",
    )(load, attn, ff, *state)


def norm_kernel(info, byte_ref, lat_ref, vec_ref, norm_ref, normt_ref, raw_ref, lat_norm_ref, lat_normt_ref, scr):
    groups, true_rows, pad_rows = 4, byte_ref.shape[1] // 4, norm_ref.shape[1] // 4
    keys = byte_ref.shape[1]
    scr[pl.ds(0, keys), :] = byte_ref[0].astype(F32)
    gain, bias = vec_ref[2:3, :], vec_ref[3:4, :]
    keep = lax.broadcasted_iota(jnp.int32, (pad_rows, 1), 0) < true_rows
    for g in range(groups):
        rows = jnp.where(keep, scr[pl.ds(g * true_rows, pad_rows), :], 0.0)
        xhat, _ = norm_parts(rows)
        normed = jnp.where(keep, xhat * gain + bias, 0.0)
        here = pl.ds(g * pad_rows, pad_rows)
        raw_ref[0, here, :] = rows.astype(BF)
        norm_ref[0, here, :] = normed.astype(BF)
    normt_ref[0] = norm_ref[0].T
    xhat, _ = norm_parts(lat_ref[0].astype(F32))
    lat_norm = (xhat * vec_ref[0:1, :] + vec_ref[1:2, :]).astype(BF)
    lat_norm_ref[0] = lat_norm
    lat_normt_ref[0] = lat_norm.T


def norm_call(first_item, all_items, info, byte_array, latents, vectors, items, pad_keys):
    _, keys, width = byte_array.shape
    lat_len = latents.shape[1]
    here = lambda i, info: (info[0] * all_items + first_item + i, 0, 0)
    out = lambda i, info: (i, 0, 0)
    return pl.pallas_call(
        norm_kernel,
        grid_spec=pltpu.PrefetchScalarGridSpec(
            num_scalar_prefetch=1,
            grid=(items,),
            in_specs=[
                pl.BlockSpec((1, keys, width), here),
                pl.BlockSpec((1, lat_len, width), here),
                pl.BlockSpec(vectors.shape, lambda i, info: (0, 0)),
            ],
            out_specs=[
                pl.BlockSpec((1, pad_keys, width), out),
                pl.BlockSpec((1, width, pad_keys), out),
                pl.BlockSpec((1, pad_keys, width), out),
                pl.BlockSpec((1, lat_len, width), out),
                pl.BlockSpec((1, width, lat_len), out),
            ],
            scratch_shapes=[pltpu.VMEM((keys + 40, width), F32)],
        ),
        out_shape=[
            jax.ShapeDtypeStruct((items, pad_keys, width), BF),
            jax.ShapeDtypeStruct((items, width, pad_keys), BF),
            jax.ShapeDtypeStruct((items, pad_keys, width), BF),
            jax.ShapeDtypeStruct((items, lat_len, width), BF),
            jax.ShapeDtypeStruct((items, width, lat_len), BF),
        ],
        compiler_params=params(),
        cost_estimate=cost(items * keys * width * 20, items * keys * width * 8),
        name="norms",
    )(info, byte_array, latents, vectors)


SPLITS = (((0, 0, 384, 0), (1, 384, 768, 0)), ((0, 0, 384, 384), (1, 384, 768, 384)))


def attn_fwd_kernel(first_item, info, count_ref, text_ref, norm_ref, lat_ref, *refs):
    if first_item == 0:
        pieces, (mixed_ref, pt_ref, kv_ref, q_ref, wkv_ref, wqo_ref) = refs[:11], refs[11:]

        @pl.when(pl.program_id(0) == 0)
        def _():
            assemble(info, pieces, (wkv_ref, wqo_ref), SPLITS)

    else:
        wkv_ref, wqo_ref, mixed_ref, pt_ref, kv_ref, q_ref = refs
    wkv = wkv_ref[...].reshape(-1, 768)
    columns = lambda start, stop: wqo_ref[:, :, start:stop].reshape(-1, stop - start)
    item = info[0] * info[3] + first_item + pl.program_id(0)
    patches, texts = count_ref[item], text_ref[item]
    keys = norm_ref.shape[1]
    pad_rows = keys // 4
    true_rows = info[2]
    row = lax.broadcasted_iota(jnp.int32, (keys, 128), 0)
    group = sum(((row >= pad_rows * g).astype(jnp.int32) for g in range(1, 4)))
    inner = row - group * pad_rows
    slot = inner + group * true_rows
    valid = ((slot < PATCHES) & (slot < patches)) | ((slot >= PATCHES) & (slot - PATCHES < texts))
    valid = valid & (inner < true_rows)
    lane_lo = lax.broadcasted_iota(jnp.int32, (128, 128), 1) < HEAD_DIM
    row_lo = lax.broadcasted_iota(jnp.int32, (128, 128), 0) < HEAD_DIM
    kv_all = dot(norm_ref[0], wkv).astype(BF)
    kv_ref[0] = kv_all
    lat_norm = lat_ref[0]
    for p in range(2):
        kv = kv_all[:, p * 384 : (p + 1) * 384]
        base = p * 384
        q = dot(lat_norm, columns(base, base + 256)) * SCALE
        q01, q2 = q[:, :128], jnp.where(lane_lo, q[:, 128:], 0.0).astype(BF)
        q_ref[0, p, :, 0:128] = q01.astype(BF)
        q_ref[0, p, :, 128:256] = q2
        stacked = jnp.concatenate([jnp.where(lane_lo, q01, 0.0), jnp.where(lane_lo, 0.0, q01)], 0).astype(BF)
        first = dot_t(kv[:, 0:128], stacked)
        second = dot_t(kv[:, 256:384], q2)
        pieces = []
        for piece in (first[:, 0:128], first[:, 128:256], second):
            piece = jnp.where(valid, piece, NEG_FILL)
            top = jnp.max(piece, 0, keepdims=True)
            expo = jnp.exp(piece - top)
            pieces.append(expo * (1.0 / jnp.sum(expo, 0, keepdims=True)))
        for h in range(3):
            pt_ref[0, p, :, h * 128 : (h + 1) * 128] = pieces[h]
        low01 = jnp.concatenate([pieces[0].astype(BF), pieces[1].astype(BF)], 1)
        o01 = dot(kv[:, 128:256].T, low01)
        o2 = dot(kv[:, 256:384].T, pieces[2].astype(BF))
        mixed_ref[0, p, 0:64, :] = o2[64:128].astype(BF)
        mixed_ref[0, p, 64:192, :] = jnp.where(row_lo, o01[:, 0:128], o01[:, 128:256]).astype(BF)


def attn_fwd_call(first_item, info, counts, texts, norm, lat_norm, weights):
    items, keys, width = norm.shape
    lat_len = lat_norm.shape[1]
    out3 = lambda i, *_: (i, 0, 0)
    out4 = lambda i, *_: (i, 0, 0, 0)
    given = [pl.BlockSpec(w.shape, lambda i, *_, d=w.ndim: (0,) * d) for w in weights]
    made = [pl.BlockSpec((8, width // 8, 768), lambda i, *_: (0, 0, 0))] * (2 * (first_item == 0))
    flops = items * 2 * (keys * width * 768 + lat_len * width * 768 + 4 * keys * lat_len * 384)
    return pl.pallas_call(
        functools.partial(attn_fwd_kernel, first_item),
        grid_spec=pltpu.PrefetchScalarGridSpec(
            num_scalar_prefetch=3,
            grid=(items,),
            in_specs=[
                pl.BlockSpec((1, keys, width), out3),
                pl.BlockSpec((1, lat_len, width), out3),
                *given,
            ],
            out_specs=[
                pl.BlockSpec((1, 2, 192, lat_len), out4),
                pl.BlockSpec((1, 2, keys, 384), out4),
                pl.BlockSpec((1, keys, 768), out3),
                pl.BlockSpec((1, 2, lat_len, 256), out4),
                *made,
            ],
        ),
        out_shape=[
            jax.ShapeDtypeStruct((items, 2, 192, lat_len), BF),
            jax.ShapeDtypeStruct((items, 2, keys, 384), F32),
            jax.ShapeDtypeStruct((items, keys, 768), BF),
            jax.ShapeDtypeStruct((items, 2, lat_len, 256), BF),
        ]
        + [jax.ShapeDtypeStruct((8, width // 8, 768), BF)] * len(made),
        compiler_params=params(),
        cost_estimate=cost(flops, 8 * 1024 * 1024, items * keys * 768),
        name="attn_fwd",
    )(info, counts, texts, norm, lat_norm, *weights)


def spread(mixed_ref, w_ref, queries):
    zeros = jnp.zeros((64, mixed_ref.shape[3]), BF)
    total = []
    for item in range(mixed_ref.shape[0]):
        rows = None
        for p in range(2):
            mixed = mixed_ref[item, p]
            parts = (mixed[0:128], mixed[128:192], zeros) if queries else (zeros, mixed[0:64], mixed[64:192])
            first = p * 384 + 128 * (not queries)
            columns = w_ref[:, :, first : first + 256].reshape(-1, 256)
            add = dot_t(jnp.concatenate(parts, 0).T, columns)
            rows = add if rows is None else rows + add
        total.append(rows)
    return jnp.concatenate(total, 0)


def ff_core_kernel(chunk, info, lat_ref, cot_ref, own_ref, got_ref, vec_ref, bias_ref, wqo_ref, *refs):
    if chunk == 0:
        pieces, crossed = refs[:11], refs[11:13]
        res_ref, normt_ref, cott_ref, hidden_ref, pre_ref, part_ref, cot_sum_ref, *weights, wqx_ref = refs[13:]
        assemble(info, pieces, weights, (((0, 0, 1536, 0),), ((1, 0, 1536, 0),)))
        rows = wqx_ref.shape[1]
        for k in range(8):
            for c in range(2):
                wqx_ref[info[4] ^ k, :, 384 * c : 384 * (c + 1)] = crossed[c][k * rows : (k + 1) * rows, :]
    else:
        weights, wqx_ref = refs[:2], refs[2]
        res_ref, normt_ref, cott_ref, hidden_ref, pre_ref, part_ref, cot_sum_ref = refs[3:]
    width = vec_ref.shape[1]
    flat = lambda ref: ref[...].reshape(-1, width).astype(F32)
    residual = flat(lat_ref) + (spread(own_ref, wqo_ref, False) + spread(got_ref, wqx_ref, False))
    res_ref[...] = residual
    xhat, _ = norm_parts(residual)
    normed = (xhat * vec_ref[4:5, :] + vec_ref[5:6, :]).astype(BF)
    cot = cot_ref[...].reshape(-1, width)
    total = None
    step = 256
    for p, w_ref in enumerate(weights):
        columns = lambda start: w_ref[:, :, start : start + step].reshape(-1, step)
        for j in range(768 // step):
            cols = slice(j * step, (j + 1) * step)
            w1 = columns(j * step)
            pre = dot(normed, w1) + bias_ref[p : p + 1, cols]
            back = dot(cot, columns(768 + j * step))
            cdf = 0.5 + 0.5 * lax.erf(pre * math.sqrt(0.5))
            pdf = jnp.exp(pre * pre * -0.5) * (1.0 / math.sqrt(2.0 * math.pi))
            hidden_ref[p, :, cols] = (pre * cdf).astype(BF)
            grad = (back * (cdf + pre * pdf)).astype(BF)
            pre_ref[p, :, cols] = grad
            add = dot_t(grad, w1)
            total = add if total is None else total + add
    part_ref[...] = total.astype(BF)
    normt_ref[...] = normed.T
    cott_ref[...] = cot.T
    cot_sum_ref[...] = jnp.sum(cot.astype(F32), 0, keepdims=True)


def ff_core_call(chunk, info, latents, cotangent, own, got, vectors, bias, wqo, weights):
    items = own.shape[0]
    _, lat_len, width = latents.shape
    rows = items * lat_len
    half = lambda i, info: (2 * info[0] + chunk, 0, 0)
    z3 = lambda i, info: (0, 0, 0)
    z4 = lambda i, info: (0, 0, 0, 0)
    z2 = lambda i, info: (0, 0)
    given = [pl.BlockSpec(w.shape, lambda i, info, d=w.ndim: (0,) * d) for w in weights]
    lanes = (1536, 1536, 768) if chunk == 0 else ()
    made = [pl.BlockSpec((8, width // 8, cols), z3) for cols in lanes]
    return pl.pallas_call(
        functools.partial(ff_core_kernel, chunk),
        grid_spec=pltpu.PrefetchScalarGridSpec(
            num_scalar_prefetch=1,
            grid=(1,),
            in_specs=[
                pl.BlockSpec((items, lat_len, width), half),
                pl.BlockSpec((items, lat_len, width), half),
                pl.BlockSpec(own.shape, z4),
                pl.BlockSpec(got.shape, z4),
                pl.BlockSpec(vectors.shape, z2),
                pl.BlockSpec(bias.shape, z2),
                pl.BlockSpec(wqo.shape, z3),
                *given,
            ],
            out_specs=[
                pl.BlockSpec((rows, width), z2),
                pl.BlockSpec((width, rows), z2),
                pl.BlockSpec((width, rows), z2),
                pl.BlockSpec((2, rows, 768), z3),
                pl.BlockSpec((2, rows, 768), z3),
                pl.BlockSpec((rows, width), z2),
                pl.BlockSpec((1, width), z2),
                *made,
            ],
        ),
        out_shape=[
            jax.ShapeDtypeStruct((rows, width), F32),
            jax.ShapeDtypeStruct((width, rows), BF),
            jax.ShapeDtypeStruct((width, rows), BF),
            jax.ShapeDtypeStruct((2, rows, 768), BF),
            jax.ShapeDtypeStruct((2, rows, 768), BF),
            jax.ShapeDtypeStruct((rows, width), BF),
            jax.ShapeDtypeStruct((1, width), F32),
        ]
        + [jax.ShapeDtypeStruct((8, width // 8, cols), BF) for cols in lanes],
        compiler_params=params(),
        cost_estimate=cost(6 * rows * width * 1536, 8 * 1024 * 1024, 2 * rows * 1536),
        name="ff_core",
    )(info, latents, cotangent, own, got, vectors, bias, wqo, *weights)


def relative_rows(info, ref, order):
    block = ref.shape[0] // 8
    return jnp.concatenate([ref[pl.ds(pl.multiple_of((info[4] ^ k) * block, 16), block), :] for k in order], 0)


def ff_grad_kernel(p, info, *refs):
    chunks, refs = (refs[:4], refs[4:8]), refs[8:]
    grad_ref, bias_ref = refs[-4:-2] if p == 0 else refs
    expand, reduce, bias = 0.0, 0.0, 0.0
    for normt_ref, cott_ref, hidden_ref, pre_ref in chunks:
        hidden, pre = hidden_ref[p], pre_ref[p]
        expand += dot(relative_rows(info, normt_ref, FF_ORDERS[0]), pre)
        reduce += dot(relative_rows(info, cott_ref, FF_ORDERS[1]), hidden)
        bias += jnp.sum(pre.astype(F32), 0, keepdims=True)
    grad_ref[0] = expand.astype(BF).reshape(8, -1, expand.shape[1])
    grad_ref[1] = reduce.astype(BF).reshape(8, -1, reduce.shape[1])
    bias_ref[...] = bias
    if p == 0:
        w_refs, (part_ref, acc) = refs[:2], refs[-2:]
        j = pl.program_id(0)
        rows = chunks[0][0].shape[1]
        for c, chunk in enumerate(chunks):
            here = pl.ds(c * rows, rows)
            add = sum(dot_t(chunk[2][q], w_ref[...].reshape(-1, w_ref.shape[2])) for q, w_ref in enumerate(w_refs))
            acc[here, :] = jnp.where(j == 0, 0.0, acc[here, :]) + add

        @pl.when(j == pl.num_programs(0) - 1)
        def _():
            part_ref[...] = acc[...].astype(BF)


def ff_grad_call(p, info, chunks, weights=()):
    width, rows = chunks[0][0].shape
    step = 256
    n = 768 // step
    z2 = lambda j, info: (0, 0)
    per_chunk = [
        pl.BlockSpec((width, rows), z2),
        pl.BlockSpec((width, rows), z2),
        pl.BlockSpec((2, rows, step), lambda j, info: (0, 0, j)),
        pl.BlockSpec((2, rows, step), lambda j, info: (0, 0, j)),
    ]
    specs = [
        pl.BlockSpec((2, 8, width // 8, step), lambda j, info: (0, 0, 0, j)),
        pl.BlockSpec((1, step), lambda j, info: (0, j)),
        pl.BlockSpec((2 * rows, width), z2),
    ]
    shapes = [
        jax.ShapeDtypeStruct((2, 8, width // 8, 768), BF),
        jax.ShapeDtypeStruct((1, 768), F32),
        jax.ShapeDtypeStruct((2 * rows, width), BF),
    ]
    count = 3 if p == 0 else 2
    return pl.pallas_call(
        functools.partial(ff_grad_kernel, p),
        grid_spec=pltpu.PrefetchScalarGridSpec(
            num_scalar_prefetch=1,
            grid=(n,),
            in_specs=per_chunk * 2
            + [pl.BlockSpec((8, width // 8, step), lambda j, info: (0, 0, n + j))] * len(weights),
            out_specs=specs[:count],
            scratch_shapes=[pltpu.VMEM((2 * rows, width), F32)] * (p == 0),
        ),
        out_shape=shapes[:count],
        compiler_params=params(),
        cost_estimate=cost((2 + 2 * (p == 0)) * 2 * rows * width * 1536, (8 + 6 * (p == 0)) * 1024 * 1024),
        name="ff_grad",
    )(info, *chunks[0], *chunks[1], *weights)


def attn_bwd_kernel(last, info, cot_ref, lat_ref, res_ref, own_ref, got_ref, vec_ref,
                    mixed_ref, pt_ref, kv_ref, q_ref, normt_ref, lat_normt_ref, wqo_ref, *refs):
    if last:
        gkv_in, gqo_in, res_grad_ref, dq_ref, dkv_ref, sums_ref, g_own_ref, g_oth_ref, gkv, gqo = refs
    else:
        res_grad_ref, dq_ref, dkv_ref, sums_ref, gkv, gqo = refs
    i = pl.program_id(0)

    @pl.when(i == 0)
    def _():
        gkv[...] = gkv_in[...] if last else jnp.zeros_like(gkv)
        gqo[...] = gqo_in[...] if last else jnp.zeros_like(gqo)
        sums_ref[...] = jnp.zeros_like(sums_ref)

    xhat, rstd = norm_parts(res_ref[...])
    dy = own_ref[...].astype(F32) + got_ref[...].astype(F32)
    dx, dgain, dbias = norm_back(dy, xhat, rstd, vec_ref[4:5, :])
    grad = cot_ref[0].astype(F32) + dx
    res_grad_ref[...] = grad
    sums_ref[0:1, :] += dgain
    sums_ref[1:2, :] += dbias
    low = grad.astype(BF)
    columns = lambda start, stop: wqo_ref[:, :, start:stop].reshape(-1, stop - start)
    lane_lo = lax.broadcasted_iota(jnp.int32, (128, 128), 1) < HEAD_DIM
    row_lo = lax.broadcasted_iota(jnp.int32, (128, 128), 0) < HEAD_DIM
    both = jnp.concatenate([lat_normt_ref[0], low.T], 1)
    none = jnp.zeros((128, 128), BF)
    zeros = jnp.zeros((64, 128), BF)
    total = None
    for p in range(2):
        base = p * 384
        kv = kv_ref[0, :, base : base + 384]
        mixed_grad = dot(low, columns(base + 128, base + 384))
        mg2 = jnp.where(lane_lo, 0.0, mixed_grad[:, 0:128]).astype(BF)
        mg01 = mixed_grad[:, 128:256]
        mg01 = jnp.concatenate([jnp.where(lane_lo, mg01, 0.0), jnp.where(lane_lo, 0.0, mg01)], 0).astype(BF)
        first = dot_t(kv[:, 128:256], mg01)
        second = dot_t(kv[:, 256:384], mg2)
        probs, scores = [], []
        for h, piece in enumerate((first[:, 0:128], first[:, 128:256], second)):
            prob = pt_ref[0, p, :, h * 128 : (h + 1) * 128]
            inner = jnp.sum(piece * prob, 0, keepdims=True)
            scores.append((prob * (piece - inner)).astype(BF))
            probs.append(prob.astype(BF))
        q01 = q_ref[0, p, :, 0:128].astype(F32)
        q01 = jnp.concatenate([jnp.where(lane_lo, q01, 0.0), jnp.where(lane_lo, 0.0, q01)], 0).astype(BF)
        q2 = q_ref[0, p, :, 128:256]
        ds01 = jnp.concatenate(scores[:2], 1)
        dkv_ref[0, :, base : base + 128] = dot(ds01, q01).astype(BF)
        dkv_ref[0, :, base + 128 : base + 256] = dot(jnp.concatenate(probs[:2], 1), mg01).astype(BF)
        dkv_ref[0, :, base + 256 : base + 384] = dot(
            jnp.concatenate([scores[2], probs[2]], 1), jnp.concatenate([q2, mg2], 0)
        ).astype(BF)
        dq01 = dot(kv[:, 0:128].T, ds01)
        dq2 = dot(kv[:, 256:384].T, scores[2])
        dq01 = (jnp.where(row_lo, dq01[:, 0:128], dq01[:, 128:256]) * SCALE).astype(BF)
        dq2 = (jnp.where(row_lo, dq2, 0.0) * SCALE).astype(BF)
        dq_ref[0, p, 0:128, :] = dq01
        dq_ref[0, p, 128:192, :] = dq2[0:64]
        add = dot_t(jnp.concatenate([dq01.T, dq2.T], 1), columns(base, base + 256))
        total = add if total is None else total + add
        right = jnp.concatenate(
            [
                jnp.concatenate([dq01, none], 1),
                jnp.concatenate([dq2, jnp.concatenate([zeros, mixed_ref[0, p, 0:64, :]], 0)], 1),
                jnp.concatenate([none, mixed_ref[0, p, 64:192, :]], 1),
            ],
            0,
        )
        gqo[:, base : base + 384] += dot_t(both, right)
    lat_hat, _ = norm_parts(lat_ref[0].astype(F32))
    sums_ref[2:3, :] += jnp.sum(total * lat_hat, 0, keepdims=True)
    sums_ref[3:4, :] += jnp.sum(total, 0, keepdims=True)
    gkv[...] += dot(normt_ref[0], dkv_ref[0])

    if last:

        @pl.when(i == pl.num_programs(0) - 1)
        def _():
            block = gkv.shape[0] // 8
            for j, k in enumerate(ORDER):
                source = pl.ds(pl.multiple_of((info[4] ^ k) * block, 8), block)
                rows = slice(j * block, (j + 1) * block)
                g_own_ref[rows, 0:384] = gkv[source, 0:384].astype(BF)
                g_own_ref[rows, 384:768] = gqo[source, 0:384].astype(BF)
                g_oth_ref[rows, 0:384] = gkv[source, 384:768].astype(BF)
                g_oth_ref[rows, 384:768] = gqo[source, 384:768].astype(BF)


def attn_bwd_call(first_item, all_items, info, cotangent, latents, residual, own, got, vectors,
                  mixed, pt, kv, q, normt, lat_normt, wqo, grads=None):
    items, keys, _ = kv.shape
    width = normt.shape[1]
    lat_len = q.shape[2]
    last = grads is not None
    one = lambda i, *_: (i, 0)
    three = lambda i, *_: (i, 0, 0)
    mine = lambda i, info: (info[0] * all_items + first_item + i, 0, 0)
    four = lambda i, *_: (i, 0, 0, 0)
    z2 = lambda i, *_: (0, 0)
    flops = items * 2 * (keys * width * 768 + 3 * lat_len * width * 768 + 10 * keys * lat_len * 384)
    out_specs = [
        pl.BlockSpec((lat_len, width), one),
        pl.BlockSpec((1, 2, 192, lat_len), four),
        pl.BlockSpec((1, keys, 768), three),
        pl.BlockSpec((4, width), z2),
        pl.BlockSpec((width, 768), z2),
        pl.BlockSpec((width, 768), z2),
    ]
    out_shape = [
        jax.ShapeDtypeStruct((items * lat_len, width), F32),
        jax.ShapeDtypeStruct((items, 2, 192, lat_len), BF),
        jax.ShapeDtypeStruct((items, keys, 768), BF),
        jax.ShapeDtypeStruct((4, width), F32),
        jax.ShapeDtypeStruct((width, 768), BF if last else F32),
        jax.ShapeDtypeStruct((width, 768), BF if last else F32),
    ]
    return pl.pallas_call(
        functools.partial(attn_bwd_kernel, last),
        grid_spec=pltpu.PrefetchScalarGridSpec(
            num_scalar_prefetch=1,
            grid=(items,),
            in_specs=[
                pl.BlockSpec((1, lat_len, width), mine),
                pl.BlockSpec((1, lat_len, width), mine),
                pl.BlockSpec((lat_len, width), one),
                pl.BlockSpec((lat_len, width), one),
                pl.BlockSpec((lat_len, width), one),
                pl.BlockSpec(vectors.shape, z2),
                pl.BlockSpec((1, 2, 192, lat_len), four),
                pl.BlockSpec((1, 2, keys, 384), four),
                pl.BlockSpec((1, keys, 768), three),
                pl.BlockSpec((1, 2, lat_len, 256), four),
                pl.BlockSpec((1, width, keys), three),
                pl.BlockSpec((1, width, lat_len), three),
                pl.BlockSpec(wqo.shape, lambda i, *_: (0, 0, 0)),
            ]
            + [pl.BlockSpec((width, 768), z2)] * (2 * last),
            out_specs=out_specs,
            scratch_shapes=[pltpu.VMEM((width, 768), F32), pltpu.VMEM((width, 768), F32)] * last,
        ),
        out_shape=out_shape,
        compiler_params=params(),
        cost_estimate=cost(flops, 12 * 1024 * 1024),
        name="attn_bwd",
    )(info, cotangent, latents, residual, own, got, vectors, mixed, pt, kv, q, normt, lat_normt, wqo, *(grads or ()))


def latent_kernel(info, lat_ref, *refs):
    vec_ref, wqo_ref, wqx_ref, out_ref = refs[6:]
    width = vec_ref.shape[1]
    step = out_ref.shape[1]
    per = refs[0].shape[0] // step
    for c in range(2):
        grad_ref, own_ref, got_ref = refs[c], refs[2 + c], refs[4 + c]
        xhat, rstd = norm_parts(lat_ref[c * per : (c + 1) * per].reshape(-1, width).astype(F32))
        dy = spread(own_ref, wqo_ref, True) + spread(got_ref, wqx_ref, True)
        dx, _, _ = norm_back(dy, xhat, rstd, vec_ref[0:1, :])
        out_ref[c * per : (c + 1) * per] = (grad_ref[...] + dx).astype(BF).reshape(per, step, width)


def latent_call(info, latents, grads, own, got, vectors, wqo, wqx):
    half, width = grads[0].shape
    lat_len = latents.shape[1]
    items = 2 * half // lat_len
    z2 = lambda i, info: (0, 0)
    z3 = lambda i, info: (0, 0, 0)
    return pl.pallas_call(
        latent_kernel,
        grid_spec=pltpu.PrefetchScalarGridSpec(
            num_scalar_prefetch=1,
            grid=(1,),
            in_specs=[pl.BlockSpec((items, lat_len, width), lambda i, info: (info[0], 0, 0))]
            + [pl.BlockSpec((half, width), z2)] * 2
            + [pl.BlockSpec(own[0].shape, lambda i, info: (0, 0, 0, 0))] * 4
            + [pl.BlockSpec(vectors.shape, z2), pl.BlockSpec(wqo.shape, z3), pl.BlockSpec(wqx.shape, z3)],
            out_specs=pl.BlockSpec((items, lat_len, width), z3),
        ),
        out_shape=jax.ShapeDtypeStruct((items, lat_len, width), BF),
        compiler_params=params(),
        cost_estimate=cost(4 * items * lat_len * width * 768, 6 * 1024 * 1024),
        name="latent_back",
    )(info, latents, *grads, *own, *got, vectors, wqo, wqx)


def byte_part_kernel(info, dkv_ref, raw_ref, wkv_ref, own_ref, sums_ref, *send_refs):
    part = dot_t(dkv_ref[0], wkv_ref[...].reshape(-1, 768))
    xhat, _ = norm_parts(raw_ref[0].astype(F32))
    half = part.shape[0] // 2
    item = pl.program_id(0)

    @pl.when(item == 0)
    def _():
        sums_ref[...] = jnp.zeros_like(sums_ref)

    sums_ref[0:1, :] += jnp.sum(part * xhat, 0, keepdims=True)
    sums_ref[1:2, :] += jnp.sum(part, 0, keepdims=True)
    low = part.astype(BF)
    for side in range(2):
        for k, send_ref in enumerate(send_refs):

            @pl.when((info[1] == side) & (item == k))
            def _():
                own_ref[0] = low[half * side : half * (side + 1)]
                send_ref[0] = low[half * (1 - side) : half * (2 - side)]


def byte_part_call(info, dkv, raw, wkv):
    items, keys, _ = dkv.shape
    width = raw.shape[2]
    half = keys // 2
    out = lambda i, info: (i, 0, 0)
    whole = lambda i, info: (0, 0, 0)
    return pl.pallas_call(
        byte_part_kernel,
        grid_spec=pltpu.PrefetchScalarGridSpec(
            num_scalar_prefetch=1,
            grid=(items,),
            in_specs=[
                pl.BlockSpec((1, keys, 768), out),
                pl.BlockSpec((1, keys, width), out),
                pl.BlockSpec(wkv.shape, whole),
            ],
            out_specs=[
                pl.BlockSpec((1, half, width), out),
                pl.BlockSpec((2, width), lambda i, info: (0, 0)),
            ]
            + [pl.BlockSpec((1, half, width), whole)] * items,
        ),
        out_shape=[
            jax.ShapeDtypeStruct((items, half, width), BF),
            jax.ShapeDtypeStruct((2, width), F32),
        ]
        + [jax.ShapeDtypeStruct((1, half, width), BF)] * items,
        compiler_params=params(),
        cost_estimate=cost(items * keys * width * 768 * 2, 6 * 1024 * 1024),
        name="byte_part",
    )(info, dkv, raw, wkv)


def byte_back_kernel(info, part_ref, raw_ref, vec_ref, *refs):
    got_refs, (own_ref, oth_ref) = refs[:-2], refs[-2:]
    half = part_ref.shape[1]
    quarter = half // 2
    got = [ref[k] for ref in got_refs for k in range(ref.shape[0])]
    for k, piece in enumerate(got):
        dy = part_ref[k].astype(F32) + piece.astype(F32)
        xhat, rstd = norm_parts(raw_ref[k].astype(F32))
        dx, _, _ = norm_back(dy, xhat, rstd, vec_ref[2:3, :])
        dx = dx.astype(BF)

        @pl.when(info[0] == 0)
        def _():
            own_ref[k] = dx[:quarter]
            oth_ref[k] = dx[quarter:]

        @pl.when(info[0] != 0)
        def _():
            own_ref[k] = dx[quarter:]
            oth_ref[k] = dx[:quarter]


def byte_back_call(info, part, got, raw, vectors):
    items, half, width = part.shape
    z3 = lambda i, info: (0, 0, 0)
    return pl.pallas_call(
        byte_back_kernel,
        grid_spec=pltpu.PrefetchScalarGridSpec(
            num_scalar_prefetch=1,
            grid=(1,),
            in_specs=[
                pl.BlockSpec((items, half, width), z3),
                pl.BlockSpec((items, half, width), lambda i, info: (0, info[1], 0)),
                pl.BlockSpec(vectors.shape, lambda i, info: (0, 0)),
                *(pl.BlockSpec(piece.shape, z3) for piece in got),
            ],
            out_specs=[pl.BlockSpec((items, half // 2, width), z3)] * 2,
        ),
        out_shape=[jax.ShapeDtypeStruct((items, half // 2, width), BF)] * 2,
        compiler_params=params(),
        cost_estimate=cost(items * half * width * 20, 4 * 1024 * 1024),
        name="byte_back",
    )(info, part, raw, vectors, *got)


def body(
    latents, byte_array, cotangent, patch_count, text_len,
    inner_weight, inner_moment, inner_square,
    output_weight, output_moment, output_square,
    expand_weight, expand_moment, expand_square,
    reduce_weight, reduce_moment, reduce_square,
    expand_bias, bias_moment, bias_square,
    norm_vectors, vector_moment, vector_square,
):
    item_count, lat_len, width = latents.shape
    keys = byte_array.shape[1]
    items = item_count // 2
    n = lax.axis_size("dp")
    head = lax.axis_index("head")
    core, xside = head & 1, head >> 1
    true_rows = keys // lax.axis_size("head")
    pad_rows = -(-true_rows // 32) * 32
    pad_keys = 4 * pad_rows
    quick = n == 8
    place = lax.axis_index("dp") if quick else jnp.int32(0)
    info = jnp.stack([core, xside, jnp.int32(true_rows), jnp.int32(items), place]).astype(jnp.int32)
    half_items = items // 2

    low_inner = inner_weight.astype(BF)
    wq, wk, wv = low_inner[0], low_inner[1], low_inner[2]
    wo = output_weight.T.astype(BF)
    pack = jnp.concatenate(
        [wk[:, :128], wv[:, :128], wk[:, 128:], wv[:, 128:], wq[:, :128], wq[:, 128:], wo[:, 128:], wo[:, :128]], 1
    )
    ff_pack = jnp.concatenate([expand_weight.astype(BF), reduce_weight.T.astype(BF)], 1)
    normalise = lambda c, byte_array: norm_call(
        c * half_items, items, info, byte_array, latents, norm_vectors, half_items, pad_keys
    )
    flip = lambda value: swap(value, "head", 1)
    over = lambda value, mask: swap(value, "dp", mask)
    grouped = lambda p: [flip(jnp.concatenate([p[k] for k in group], 0)) for group in GROUPS]
    if quick:
        g = {0: pack, 4: over(pack, 4), 2: over(pack, 2), 1: over(pack, 1)}
        norm0 = normalise(0, byte_array)
        g[4], g[2], g[1], *norm0 = tie(g[4], g[2], g[1], *norm0)
        g[6], g[5], g[3] = over(g[4], 2), over(g[4], 1), over(g[2], 1)
        g[6], g[5], g[3], byte_later, ff_pack = tie(g[6], g[5], g[3], byte_array, ff_pack)
        f = {0: ff_pack, 4: over(ff_pack, 4), 2: over(ff_pack, 2), 1: over(ff_pack, 1)}
        g[7] = over(g[6], 1)
        norm1 = normalise(1, byte_later)
        g[7], f[4], f[2], f[1], *norm1 = tie(g[7], f[4], f[2], f[1], *norm1)
        f[6], f[5], f[3] = over(f[4], 2), over(f[4], 1), over(f[2], 1)
        pieces = [g[k] for k in range(8)] + grouped(g)
    else:
        norm0, norm1 = normalise(0, byte_array), normalise(1, byte_array)
        blocks = lax.all_gather(pack, "dp", axis=0, tiled=True).reshape(8, width // 8, 768)
        g = [blocks[k] for k in range(8)]
        pieces = g + grouped(g)
        blocks = lax.all_gather(ff_pack, "dp", axis=0, tiled=True).reshape(8, width // 8, 1536)
        f = [blocks[k] for k in range(8)]
    norm, normt, raw, lat_norm, lat_normt = zip(norm0, norm1)
    bias_other = flip(expand_bias)

    crossed = swap(jnp.concatenate([g[k][:, 384:] for k in range(8)], 0), "head", 2)

    attend = lambda c, weights: attn_fwd_call(
        c * half_items, info, patch_count, text_len, norm[c], lat_norm[c], weights
    )
    mixed0, *kept0, wkv, wqo = attend(0, pieces)
    got0 = swap(mixed0, "head", 2)
    if quick:
        first_flip = flip(jnp.concatenate([f[k] for k in GROUPS[0]], 0))
        wkv, f[6], f[5], f[3], first_flip, bias_other, crossed = tie(
            wkv, f[6], f[5], f[3], first_flip, bias_other, crossed
        )
        f[7] = over(f[6], 1)
        second_flip = flip(jnp.concatenate([f[k] for k in GROUPS[1]], 0))
    crossed = [crossed, flip(crossed)]
    mixed1, *kept1 = attend(1, [wkv, wqo])
    mixed1, got0, crossed[1] = tie(mixed1, got0, crossed[1])
    got1 = swap(mixed1, "head", 2)
    if quick:
        mixed1, second_flip, f[7] = tie(mixed1, second_flip, f[7])
        ff_pieces = [f[k] for k in range(8)] + [first_flip, second_flip, flip(f[7])]
    else:
        ff_pieces = f + grouped(f)

    bias_both = jnp.stack([expand_bias, bias_other])
    feed = lambda c, mixed, got, weights: ff_core_call(
        c, info, latents, cotangent, mixed, got, norm_vectors, bias_both, wqo, weights
    )
    res0, *ff0, npart0, cot_sum0, ff_own, ff_oth, wqx = feed(0, mixed0, got0, [*ff_pieces, *crossed])
    npart0, got1 = tie(npart0, got1)
    ngot0 = swap(npart0, "head", 2)
    res1, *ff1, npart1, cot_sum1 = feed(1, mixed1, got1, [ff_own, ff_oth, wqx])
    npart1, ngot0 = tie(npart1, ngot0)
    ngot1 = swap(npart1, "head", 2)
    g_oth, bias_oth = ff_grad_call(1, info, [ff0, ff1])
    g_oth, ngot0, ff1[3] = tie(g_oth, ngot0, ff1[3])
    g_got = flip(g_oth)
    g_own, bias_own, mlp_part = ff_grad_call(0, info, [ff0, ff1], [ff_own, ff_oth])
    g_own, ngot0, g_got = tie(g_own, ngot0, g_got)
    bias_own = bias_own + flip(bias_oth)
    pair_of = lambda kind, part: (g_own[kind, part], g_got[kind, part])
    first_steps = [plus(*pair_of(kind, slice(0, 4))) for kind in range(2)]

    attend_back = lambda c, res, npart, ngot, mixed, kept, grads: attn_bwd_call(
        c * half_items, items, info, cotangent, latents, res, npart, ngot,
        norm_vectors, mixed, *kept, normt[c], lat_normt[c], wqo, grads
    )
    res0, ngot0, bias_own, *first_steps = tie(res0, ngot0, bias_own, *first_steps)
    if quick:
        ff_got = [over(first_steps[0], 1), over(first_steps[1], 2)]
    rgrad0, dq0, dkv0, sums0, *grads = attend_back(0, res0, npart0, ngot0, mixed0, kept0, None)
    dkv0, ngot1, mlp_part = tie(dkv0, ngot1, mlp_part)
    mlp_got = swap(mlp_part, "head", 2)
    bown0, bsums0, *bsend0 = byte_part_call(info, dkv0, raw[0], wkv)
    res1, bsend0[0] = tie(res1, bsend0[0])
    bgot00 = swap(bsend0[0], "head", 2)
    if quick:
        res1, *ff_got = tie(res1, *ff_got)
        second_steps = [plus(*pair_of(kind, slice(4, 6)), ff_got[kind][0:2]) for kind in range(2)]
        ff_more = [over(second_steps[0], 2), over(second_steps[1], 1)]
    rgrad1, dq1, dkv1, sums1, g_attn, g_attn_oth = attend_back(1, res1, npart1, ngot1, mixed1, kept1, grads)
    g_attn_oth, mlp_got, bsend0[1] = tie(g_attn_oth, mlp_got, bsend0[1])
    bgot01 = swap(bsend0[1], "head", 2)
    if quick:
        g_attn_oth, *ff_more = tie(g_attn_oth, *ff_more)
        rest = [(*pair_of(kind, part), ff_got[kind][part - 4], ff_more[kind][part - 6]) for part in (6, 7) for kind in range(2)]
        third_step = jnp.concatenate([plus(*rest[0]), plus(*rest[1])], 0)
    else:
        g_ff = g_own.astype(F32) + g_got.astype(F32)
        g_ff = jnp.stack([g_ff[kind, order.index(k)] for kind, order in enumerate(FF_ORDERS) for k in range(8)])
        g_ff = g_ff.reshape(2, width, 768)
        g_ff = lax.psum_scatter(g_ff, "dp", scatter_dimension=1, tiled=True).reshape(-1, 768)
    u = g_attn.reshape(8, width // 8, 768)
    v = flip(g_attn_oth).reshape(8, width // 8, 768)
    u75 = plus(u[0:2], v[0:2])

    if quick:
        u31 = plus(u[2:4], v[2:4])
        dkv1, u75, u31, third_step = tie(dkv1, u75, u31, third_step)
        third = 5 * third_step.shape[0] // 12
        last_got = [over(third_step[:third], 4)]
        y75 = over(u75, 1)
        y31 = over(u31, 1)
    bown1, bsums1, *bsend1 = byte_part_call(info, dkv1, raw[1], wkv)
    if quick:
        bsend1[0], y75, dq0, dq1, last_got[0] = tie(bsend1[0], y75, dq0, dq1, last_got[0])
        u64 = plus(u[4:6], v[4:6], y75)
        last_got.append(over(third_step[third : 2 * third], 4))
        z6 = over(u64[0], 2)
    lgot0, lgot1 = swap(dq0, "head", 2), swap(dq1, "head", 2)
    side0 = list(byte_back_call(info, bown0, [bgot00, bgot01], raw[0], norm_vectors))

    residual = jnp.concatenate([res0, res1], 0)
    block_mine = residual + (mlp_part.astype(F32) + mlp_got.astype(F32)) + norm_vectors[6]
    block_mine = block_mine.astype(BF).reshape(items, lat_len, width)

    byte_side = lambda c, own, got: byte_back_call(info, own, got, raw[c], norm_vectors)
    if quick:
        block_mine, z6, y31, bsend1[0], last_got[1], side0[0] = tie(
            block_mine, z6, y31, bsend1[0], last_got[1], side0[0]
        )
        last_got.append(over(third_step[2 * third :], 4))
        z4 = over(plus(u64[1], z6), 4)
        z2 = over(plus(u[6], v[6], y31[0]), 2)
    bgot10 = swap(bsend1[0], "head", 2)
    lat_mine = latent_call(
        info, latents, [rgrad0, rgrad1], [dq0, dq1], [lgot0, lgot1], norm_vectors, wqo, wqx
    )
    block_output = pair_call(info, [block_mine], [flip(block_mine)], lat_len)
    if quick:
        block_output, lat_mine, last_got[2], z4, z2 = tie(block_output, lat_mine, last_got[2], z4, z2)
        g_ff = jnp.concatenate([sum(x.astype(F32) for x in rest[2 + kind]) for kind in range(2)], 0)
        g_ff = g_ff + jnp.concatenate(last_got, 0).astype(F32)
        ff_squares = jnp.sum(g_ff * g_ff)
        bgot10, bsend1[1] = tie(bgot10, bsend1[1])
        terms = [u[7], v[7], y31[1], z2, z4]
    else:
        g_attn = u.astype(F32) + v.astype(F32)
        g_attn = jnp.concatenate([g_attn[ORDER.index(k)] for k in range(8)], 0)
        terms = [lax.psum_scatter(g_attn, "dp", scatter_dimension=0, tiled=True)]
        ff_squares = jnp.sum(g_ff * g_ff)
    bgot11 = swap(bsend1[1], "head", 2)
    side1 = byte_side(1, bown1, [bgot10, bgot11])
    g_attn, load = collect_call(
        info, terms, [sums0, sums1, bsums0, bsums1, cot_sum0, cot_sum1, bias_own, ff_squares.reshape(1, 1)]
    )
    latent_gradient = pair_call(info, [lat_mine], [flip(lat_mine)], lat_len)
    beside = [lambda: latent_gradient, None, lambda: side1]
    outs = []
    mask = n // 2
    while mask:
        hop = over(load, mask)
        make = beside.pop(0) if beside else None
        if make:
            hop, out = lax.optimization_barrier((hop, make()))
            outs.append(out)
        load = load + hop
        mask //= 2
    latent_gradient = outs[0]
    bias_sum = load[7:8]
    load = jnp.where(jnp.arange(load.shape[0])[:, None] == 7, load * load, load)
    load = load + swap(load, "head", 1)
    by_row = rows_call(info, [side0[0], outs[1][0]], [flip(side0[1]), flip(outs[1][1])], true_rows)
    hop, by_row = tie(swap(load, "head", 2), by_row)
    byte_gradient = by_row.transpose(1, 0, 2)
    load = load + hop

    *news, grad_norm = adam_call(
        load,
        g_attn,
        g_ff,
        [
            inner_weight, inner_moment, inner_square, output_weight, output_moment, output_square,
            expand_weight, expand_moment, expand_square, reduce_weight.T, reduce_moment.T, reduce_square.T,
            norm_vectors, vector_moment, vector_square,
        ],
    )
    factor = CLIP_RATE * math.sqrt(4 * D * D + 2 * D * FF + FF + 7 * D) / grad_norm[0, 0]
    bias_new = adamw(expand_bias, bias_moment, bias_square, factor * bias_sum[0], 0.3, 0.0)
    news[9:12] = [new.T for new in news[9:12]]
    return (
        block_output, latent_gradient, byte_gradient, *news[:12], *bias_new, *news[12:], grad_norm[0, 0]
    )


def solution(mesh):
    rows, cols = P("dp", "head"), P("head", "dp")
    inner, items = P(None, "dp", "head"), P("dp", None, None)
    weights = (inner,) * 3 + (cols,) * 3 + (rows,) * 3 + (cols,) * 3 + (P("head"),) * 3 + (P(),) * 3
    return jax.shard_map(
        body,
        mesh=mesh,
        in_specs=(items, items, items, P("dp"), P("dp")) + weights,
        out_specs=(items, items, P("dp", "head", None)) + weights + (P(),),
        check_vma=False,
    )
```
